256 devices in a mesh: dp: 8 (over x_lo, y), ctx: 32 (over x_hi, z, core).
Axes of the slice: x: 4 (x_hi: 2, x_lo: 2; x = x_hi * 2 + x_lo), y: 4, z: 8, core: 2. Of those that a mesh axis runs over, the one named last changes fastest.
Arguments:
- tokens: bfloat16 [8, 16384, 1024], P('dp', 'ctx'), may hold values from -6 to 6
- starts: int32 [8, 2048], P('dp', 'ctx'), may hold values from 0 to 16383, as said below
- gain: float32 [1024], replicated, may hold values from 0.1 to 1.9
- w_query: bfloat16 [1024, 1024], P('dp')
- w_key: bfloat16 [1024, 1024], P('dp')
- w_value: bfloat16 [1024, 1024], P('dp'), may hold values from -0.1875 to 0.1875
- w_out: bfloat16 [1024, 1024], P('dp'), may hold values from -0.1875 to 0.1875
- cotangent: bfloat16 [8, 16384, 1024], P('dp', 'ctx'), may hold values from -6 to 6
Outputs:
- grad_tokens: bfloat16 [8, 16384, 1024], P('dp', 'ctx')
The draws below stay inside these ranges and needn't reach their ends.
Inputs may be any that keep to these rules, and one draw needn't show every extreme that they name: starts[b, 0] is 0 and starts[b, j] rises strictly with j; segment j lies with the device that holds starts[b, j], and every position held by one device along ctx belongs to a segment held by that device or by one of its two neighbours along ctx; in the first sequence segment 64 - 1 starts at 513 or later and the last segment starts at 16383.
All inputs are finite; a program needn't handle non-finite values.
Results may differ from the reference program's by a relative error of at most 0.013.
Values may be sent and summed in bfloat16 or wider, within the bound.
No kernel may reach another device: no remote copies, remote signals or barrier semaphores. Data moves between devices by JAX's collectives and lax.ppermute only.
A program may use at most 128 MiB of HBM per device.

```python
import math
import jax
import jax.numpy as jnp
from jax import lax

D = 1024
HEADS = 8
HEAD = 128
SHORTEN = 8
TOK_DEV = 512
BATCH = 8
LENGTH = 16384
SEG_DEV = 64
SEGS = 2048


def draw_starts(key, part):
    key = jax.random.fold_in(key, 3)
    first_key, second_key = jax.random.split(key)
    upper = 2 * SHORTEN - 1
    first_draw = jax.random.randint(first_key, (BATCH, SEGS), 0, upper)
    second_draw = jax.random.randint(second_key, (BATCH, SEGS), 0, upper)
    index = jnp.arange(SEGS, dtype=jnp.int32)[None, :]
    row = jnp.arange(BATCH, dtype=jnp.int32)[:, None]
    length = 1 + first_draw * second_draw // (2 * SHORTEN - 2)
    stride = jnp.where(index == 0, 0, length - SHORTEN)
    walk = jnp.cumsum(stride, axis=1).astype(jnp.int32)
    drift = TOK_DEV // 2
    folded = jnp.mod(walk + drift, 4 * drift)
    folded = jnp.where(folded <= 2 * drift, folded, 4 * drift - folded)
    offset = folded - drift
    raw = index * SHORTEN + offset
    ceiling = LENGTH - (SEGS - index)
    result = jnp.maximum(index, jnp.minimum(raw, ceiling))
    pivot = SEG_DEV - 1
    below = (row == 0) & (index < pivot)
    above = (row == 0) & (index >= pivot)
    result = jnp.where(below, jnp.minimum(result, TOK_DEV + 1 - (pivot - index)), result)
    result = jnp.where(above, jnp.maximum(result, TOK_DEV + 1 + (index - pivot)), result)
    result = jnp.where((index == SEGS - 1) & (row == 0), LENGTH - 1, result)
    return result.astype(jnp.int32)


def draw_w_query(key, part):
    key = jax.random.fold_in(key, 5)
    own = jax.random.normal(key, (D, HEADS * HEAD), jnp.float32)
    result = own / math.sqrt(D)
    return result.astype(jnp.bfloat16)


def draw_w_key(key, part):
    key = jax.random.fold_in(key, 7)
    own = jax.random.normal(key, (D, HEADS * HEAD), jnp.float32)
    result = own / math.sqrt(D)
    return result.astype(jnp.bfloat16)


def block_scale(key, shape, pieces, low, largest):
    loudness, own = 1.0, jax.random.fold_in(key, 6)
    for axis_at, parts in pieces:
        steps = jnp.exp(jax.random.uniform(jax.random.fold_in(own, axis_at), (parts,), jnp.float32, low / len(pieces), largest / len(pieces)))
        loudness = loudness * jnp.repeat(steps, shape[axis_at] // parts).reshape([-1 if axis == axis_at else 1 for axis in range(len(shape))])
    return loudness


def normal_values(stream_key, shape, scale, reach, pieces=(), kind=jnp.bfloat16):
    loudness = block_scale(stream_key, shape, pieces, -0.22, 0.18) if pieces else 1.0
    values = jax.random.normal(stream_key, shape, jnp.float32) * scale * loudness
    return jnp.minimum(jnp.maximum(values, -reach), reach).astype(kind)


def setup_inputs(seed: int = 0) -> dict:
    streams_of = jax.random.split(jax.random.key(seed), 9)
    return {
        "tokens": normal_values(streams_of[0], (BATCH, LENGTH, D), 1.0, 6.0, ((0, 8), (1, 32))),
        "starts": draw_starts(jax.random.fold_in(streams_of[8], 71), 0),
        "gain": jnp.clip(1.0 + 0.18 * jax.random.normal(streams_of[2], (D,), jnp.float32), 0.1, 1.9),
        "w_query": draw_w_query(jax.random.fold_in(streams_of[8], 71), 0),
        "w_key": draw_w_key(jax.random.fold_in(streams_of[8], 71), 0),
        "w_value": normal_values(streams_of[5], (D, HEADS * HEAD), D ** -0.5, 0.1875, ((0, 8),)),
        "w_out": normal_values(streams_of[6], (HEADS * HEAD, D), (HEADS * HEAD) ** -0.5, 0.1875, ((0, 8),)),
        "cotangent": normal_values(streams_of[7], (BATCH, LENGTH, D), 1.0, 6.0, ((0, 8), (1, 32))),
    }


def reference(tokens, starts, gain, w_query, w_key, w_value, w_out, cotangent):
    inner = HEADS * HEAD
    scale = 1.0 / math.sqrt(HEAD)

    def one_sequence(items):
        xrow, first_pos, grad_out = items
        positions = jnp.arange(LENGTH, dtype=jnp.int32)
        seg = (jnp.searchsorted(first_pos, positions, side='right') - 1).astype(jnp.int32)
        count = jax.ops.segment_sum(jnp.ones((LENGTH,), jnp.float32), seg, num_segments=SEGS)
        pooled = jax.ops.segment_sum(xrow.astype(jnp.float32), seg, num_segments=SEGS) / count[:, None]
        rms = jnp.sqrt(lax.optimization_barrier(jnp.mean(pooled * pooled, axis=-1, keepdims=True)) + 1e-06)
        normed = pooled / rms
        normin = (normed * gain).astype(jnp.bfloat16)
        query = jnp.dot(normin, w_query, preferred_element_type=jnp.float32).astype(jnp.bfloat16).reshape(SEGS, HEADS, HEAD)
        keys = jnp.dot(normin, w_key, preferred_element_type=jnp.float32).astype(jnp.bfloat16).reshape(SEGS, HEADS, HEAD)
        values = jnp.dot(normin, w_value, preferred_element_type=jnp.float32).astype(jnp.bfloat16).reshape(SEGS, HEADS, HEAD)
        allowed = jnp.arange(SEGS)[None, :] <= jnp.arange(SEGS)[:, None]
        score = jnp.einsum('qhd,khd->hqk', query.astype(jnp.float32), keys.astype(jnp.float32)) * scale
        score = jnp.where(allowed[None], score, -1e+30)
        peak = lax.optimization_barrier(jnp.max(score, axis=-1, keepdims=True))
        expo = jnp.where(allowed[None], jnp.exp(score - peak), 0.0)
        probs = expo / lax.optimization_barrier(jnp.sum(expo, axis=-1, keepdims=True))
        probs_b = probs.astype(jnp.bfloat16)
        attended = jnp.einsum('hqk,khd->qhd', probs_b.astype(jnp.float32), values.astype(jnp.float32)).astype(jnp.bfloat16)
        earlier = jnp.where(seg > 0, seg - 1, SEGS).astype(jnp.int32)
        dout = jax.ops.segment_sum(grad_out.astype(jnp.float32), earlier, num_segments=SEGS + 1)[:SEGS]
        dout_b = dout.astype(jnp.bfloat16)
        dattended = jnp.dot(dout_b, w_out.T, preferred_element_type=jnp.float32).astype(jnp.bfloat16).reshape(SEGS, HEADS, HEAD)
        delta = jnp.einsum('qhd,qhd->hq', dattended.astype(jnp.float32), attended.astype(jnp.float32))
        dprobs = jnp.einsum('qhd,khd->hqk', dattended.astype(jnp.float32), values.astype(jnp.float32))
        dscore = (probs * (dprobs - delta[:, :, None])).astype(jnp.bfloat16)
        dquery = (jnp.einsum('hqk,khd->qhd', dscore.astype(jnp.float32), keys.astype(jnp.float32)) * scale).astype(jnp.bfloat16).reshape(SEGS, inner)
        dkey = (jnp.einsum('hqk,qhd->khd', dscore.astype(jnp.float32), query.astype(jnp.float32)) * scale).astype(jnp.bfloat16).reshape(SEGS, inner)
        dvalue = jnp.einsum('hqk,qhd->khd', probs_b.astype(jnp.float32), dattended.astype(jnp.float32)).astype(jnp.bfloat16).reshape(SEGS, inner)
        dnormin = jnp.dot(dquery, w_query.T, preferred_element_type=jnp.float32)
        dnormin = dnormin + jnp.dot(dkey, w_key.T, preferred_element_type=jnp.float32)
        dnormin = dnormin + jnp.dot(dvalue, w_value.T, preferred_element_type=jnp.float32)
        scaled = dnormin * gain
        dpooled = dout + (scaled - normed * lax.optimization_barrier(jnp.mean(scaled * normed, axis=-1, keepdims=True))) / rms
        per_seg = dpooled / count[:, None]
        return (grad_out.astype(jnp.float32) + per_seg[seg]).astype(jnp.bfloat16)
    return lax.map(one_sequence, (tokens, starts, cotangent))
```

```python
import functools
import math

import jax
import jax.numpy as jnp
from jax import lax
from jax.experimental import pallas as pl
from jax.experimental.pallas import tpu as pltpu
from jax.sharding import PartitionSpec as P

HEAD = 128
CORES = 2
RING = 8
HALVES = 2
CTX = HALVES * RING * CORES
NEG = -1e30


def place(half, ring, core):
    return (half * RING + ring) * CORES + core


def devices():
    return [(h, r, k) for h in range(HALVES) for r in range(RING) for k in range(CORES)]


def along(value, steps):
    pairs = [(i, i + steps) for i in range(CTX) if 0 <= i + steps < CTX]
    return lax.ppermute(value, "ctx", pairs)


def around(value, steps):
    pairs = [(place(h, r, k), place(h, (r + steps) % RING, k)) for h, r, k in devices()]
    return lax.ppermute(value, "ctx", pairs)


def other_core(value):
    pairs = [(place(h, r, k), place(h, r, 1 - k)) for h, r, k in devices()]
    return lax.ppermute(value, "ctx", pairs)


def across(value, source):
    pairs = [
        (place(h, r, k), place(1 - h, r, k)) for h, r, k in devices() if h == source
    ]
    return lax.ppermute(value, "ctx", pairs)


def contract_last(left, right):
    return lax.dot_general(
        left, right, (((1,), (1,)), ((), ())), preferred_element_type=jnp.float32
    )


def contract_first(left, right):
    return lax.dot_general(
        left, right, (((0,), (0,)), ((), ())), preferred_element_type=jnp.float32
    )


def head_weights(w_query, w_key, w_value, w_out, ring, core):
    rows, width = w_query.shape
    half = rows // CORES
    at = core * half
    cut = [
        lax.dynamic_slice(w, (at, ring * HEAD), (half, HEAD)) for w in (w_query, w_key, w_value)
    ]
    cut.append(lax.dynamic_slice(w_out, (at, 0), (half, width)))
    gathered = lax.all_gather(jnp.concatenate(cut, axis=1), "dp", axis=0, tiled=False)
    mine_in = gathered[:, :, : 3 * HEAD]
    mine_out = lax.dynamic_index_in_dim(gathered[:, :, 3 * HEAD :], ring, 0, keepdims=False)
    theirs_in = other_core(mine_in)
    theirs_out = other_core(mine_out)
    first = core == 0
    w_in = jnp.stack(
        [jnp.where(first, mine_in, theirs_in), jnp.where(first, theirs_in, mine_in)], axis=1
    ).reshape(-1, 3 * HEAD)
    w_back = jnp.concatenate(
        [jnp.where(first, mine_out, theirs_out), jnp.where(first, theirs_out, mine_out)], axis=0
    )
    return w_in, w_back


def attention_kernel(tile, seg, q_ref, kv_ref, da_ref, place_ref, dq_ref, dkv_ref, dkt, dvt):
    half, ring, core = place_ref[0], place_ref[1], place_ref[2]
    queries, keys = q_ref.shape[0], kv_ref.shape[0]
    group = keys // 4
    spot = lax.broadcasted_iota(jnp.int32, (1, keys), 1)
    block = spot // group
    slot = (spot % group) // seg
    key_half = jnp.where(block < 2, half, 1 - half)
    key_core = jnp.where(block % 2 == 0, core, 1 - core)
    key_ring = (ring - slot + RING) % RING
    key_at = ((key_half * RING + key_ring) * CORES + key_core) * seg + spot % seg
    turn = math.log2(math.e) / math.sqrt(HEAD)
    scale = 1.0 / math.sqrt(HEAD)
    k = kv_ref[:, :HEAD]
    v = kv_ref[:, HEAD:]
    for step in range(queries // tile):
        rows = slice(step * tile, (step + 1) * tile)
        place_row = lax.broadcasted_iota(jnp.int32, (tile, 1), 0) + step * tile
        query_ring = (ring - place_row // seg + RING) % RING
        query_at = ((half * RING + query_ring) * CORES + core) * seg + place_row % seg
        q = q_ref[rows, :]
        da = da_ref[rows, :]
        score = jnp.where(key_at <= query_at, contract_last(q, k), NEG)
        peak = jnp.max(score, axis=1, keepdims=True)
        expo = jnp.exp2((score - peak) * turn)
        probs = expo * (1.0 / jnp.sum(expo, axis=1, keepdims=True))
        probs_b = probs.astype(jnp.bfloat16)
        attended = jnp.dot(probs_b, v, preferred_element_type=jnp.float32).astype(jnp.bfloat16)
        delta = jnp.sum(
            da.astype(jnp.float32) * attended.astype(jnp.float32), axis=1, keepdims=True
        )
        dscore = (probs * (contract_last(da, v) - delta)).astype(jnp.bfloat16)
        dq = jnp.dot(dscore, k, preferred_element_type=jnp.float32) * scale
        dq_ref[rows, :] = dq.astype(jnp.bfloat16)
        dk_part = contract_first(q, dscore)
        dv_part = contract_first(da, probs_b)
        if step == 0:
            dkt[...] = dk_part
            dvt[...] = dv_part
        else:
            dkt[...] += dk_part
            dvt[...] += dv_part
    dkv_ref[:, :HEAD] = (dkt[...] * scale).T.astype(jnp.bfloat16)
    dkv_ref[:, HEAD:] = dvt[...].T.astype(jnp.bfloat16)


def attention(q, kv, da, where, seg):
    queries, keys = q.shape[0], kv.shape[0]
    return pl.pallas_call(
        functools.partial(attention_kernel, 128, seg),
        out_shape=(
            jax.ShapeDtypeStruct((queries, HEAD), jnp.bfloat16),
            jax.ShapeDtypeStruct((keys, 2 * HEAD), jnp.bfloat16),
        ),
        in_specs=[
            pl.BlockSpec(memory_space=pltpu.VMEM),
            pl.BlockSpec(memory_space=pltpu.VMEM),
            pl.BlockSpec(memory_space=pltpu.VMEM),
            pl.BlockSpec(memory_space=pltpu.SMEM),
        ],
        out_specs=(
            pl.BlockSpec(memory_space=pltpu.VMEM),
            pl.BlockSpec(memory_space=pltpu.VMEM),
        ),
        scratch_shapes=[
            pltpu.VMEM((HEAD, keys), jnp.float32),
            pltpu.VMEM((HEAD, keys), jnp.float32),
        ],
        compiler_params=pltpu.CompilerParams(vmem_limit_bytes=48 * 1024 * 1024),
        cost_estimate=pl.CostEstimate(
            flops=12 * queries * keys * HEAD,
            bytes_accessed=2 * HEAD * (3 * queries + 4 * keys),
            transcendentals=queries * keys,
        ),
    )(q, kv, da, where)


def gather_ring(shard):
    rows = shard.shape[0]
    right, left = [shard], [shard]
    for _ in range(RING // 2 - 1):
        right.append(around(right[-1], 1))
        left.append(around(left[-1], -1))
    far = jnp.concatenate(
        [around(right[-1][: rows // 2], 1), around(left[-1][rows // 2 :], -1)], axis=0
    )
    return right + [far] + left[:0:-1]


def scatter_ring(parts):
    wire = jnp.bfloat16
    middle = RING // 2
    cut = parts[0].shape[0] // 2
    right = around(parts[middle][:cut].astype(wire), 1)
    left = around(parts[middle][cut:].astype(wire), -1)
    right = jnp.concatenate(
        [parts[middle + 1][:cut] + right.astype(jnp.float32), parts[middle + 1][cut:]], axis=0
    )
    left = jnp.concatenate(
        [parts[middle - 1][:cut], parts[middle - 1][cut:] + left.astype(jnp.float32)], axis=0
    )
    for step in range(1, middle):
        right = around(right.astype(wire), 1).astype(jnp.float32)
        left = around(left.astype(wire), -1).astype(jnp.float32)
        if step < middle - 1:
            right = parts[middle + 1 + step] + right
            left = parts[middle - 1 - step] + left
    return parts[0] + right + left


def per_device(tokens, starts, gain, w_query, w_key, w_value, w_out, cotangent):
    token_rows = tokens[0]
    grad_out = cotangent[0]
    own_starts = starts[0]
    rows, width = token_rows.shape
    seg = own_starts.shape[0]
    length = rows * CTX
    ctx = lax.axis_index("ctx")
    half, ring, core = ctx // (RING * CORES), (ctx // CORES) % RING, ctx % CORES
    w_in, w_back = head_weights(w_query, w_key, w_value, w_out, ring, core)

    before = jnp.where(ctx == 0, -1, along(own_starts, 1))
    after = jnp.where(ctx == CTX - 1, length, along(own_starts, -1))
    window = jnp.concatenate([before, own_starts, after])
    positions = ctx * rows + lax.iota(jnp.int32, rows)
    ends = jnp.concatenate([window[1:], jnp.full((1,), length, jnp.int32)])
    member = (
        (window[None, :] <= positions[:, None]) & (positions[:, None] < ends[None, :])
    ).astype(jnp.bfloat16)
    token_sum = contract_first(member, token_rows)
    grad_sum = contract_first(member, grad_out)
    wire = jnp.bfloat16
    lower = jnp.concatenate([token_sum[:seg], grad_sum[1 : seg + 1]], axis=1).astype(wire)
    tail = jnp.concatenate([grad_sum[2 * seg + 1 :], jnp.zeros((1, width), jnp.float32)], axis=0)
    upper = jnp.concatenate([token_sum[2 * seg :], tail], axis=1).astype(wire)
    from_after = along(lower, -1).astype(jnp.float32)
    from_before = along(upper, 1).astype(jnp.float32)
    from_second = along(grad_sum[:1].astype(wire), -2).astype(jnp.float32)
    count = (ends - window)[seg : 2 * seg].astype(jnp.float32)
    pooled = token_sum[seg : 2 * seg] + from_after[:, :width] + from_before[:, :width]
    pooled = pooled / count[:, None]
    last = lax.broadcasted_iota(jnp.int32, (seg, 1), 0) == seg - 1
    dout = grad_sum[seg + 1 : 2 * seg + 1] + from_after[:, width:] + from_before[:, width:]
    dout = dout + jnp.where(last, from_second, 0.0)
    rms = jnp.sqrt(jnp.mean(pooled * pooled, axis=-1, keepdims=True) + 1e-06)
    normed = pooled / rms
    normin = (normed * gain).astype(jnp.bfloat16)

    both = jnp.concatenate(
        gather_ring(jnp.concatenate([normin, dout.astype(jnp.bfloat16)], axis=1)), axis=0
    )
    qkv = jnp.dot(both[:, :width], w_in, preferred_element_type=jnp.float32).astype(jnp.bfloat16)
    kv_own = qkv[:, HEAD:]
    kv_far = across(kv_own, 0)
    da = contract_last(both[:, width:], w_back).astype(jnp.bfloat16)
    kv = jnp.concatenate([kv_own, other_core(kv_own), kv_far, other_core(kv_far)], axis=0)
    dq, dkv = attention(qkv[:, :HEAD], kv, da, jnp.stack([half, ring, core]), seg)
    group = qkv.shape[0]
    parts = [dkv[i * group : (i + 1) * group] for i in range(4)]
    far = parts[2].astype(jnp.float32) + other_core(parts[3]).astype(jnp.float32)
    far = across(far.astype(wire), 1).astype(jnp.float32)
    near = parts[0].astype(jnp.float32) + other_core(parts[1]).astype(jnp.float32)
    dkv_own = (near + far).astype(jnp.bfloat16)
    partial = contract_last(jnp.concatenate([dq, dkv_own], axis=1), w_in)
    dnormin = scatter_ring([partial[i * seg : (i + 1) * seg] for i in range(RING)])

    scaled = dnormin * gain
    dpooled = dout + (scaled - normed * jnp.mean(scaled * normed, axis=-1, keepdims=True)) / rms
    per_seg = (dpooled / count[:, None]).astype(wire)
    per_window = jnp.concatenate([along(per_seg, 1), per_seg, along(per_seg, -1)], axis=0)
    spread = jnp.dot(member, per_window, preferred_element_type=jnp.float32)
    return (grad_out.astype(jnp.float32) + spread).astype(jnp.bfloat16)[None]


def solution(mesh):
    return jax.shard_map(
        per_device,
        mesh=mesh,
        in_specs=(
            P("dp", "ctx", None),
            P("dp", "ctx"),
            P(),
            P("dp", None),
            P("dp", None),
            P("dp", None),
            P("dp", None),
            P("dp", "ctx", None),
        ),
        out_specs=P("dp", "ctx", None),
        check_vma=False,
    )
```

```python
import functools
import math

import jax
import jax.numpy as jnp
from jax import lax
from jax.experimental import pallas as pl
from jax.experimental.pallas import tpu as pltpu
from jax.sharding import PartitionSpec as P

HEAD = 128
HALVES, TURNS, PAIR, CORES = 2, 4, 2, 2
CTX = HALVES * TURNS * PAIR * CORES
ROWS_X, ROWS_Y = 2, 4
NEG = -1e30
WIRE = jnp.bfloat16
F32 = jnp.float32
VMEM = pl.BlockSpec(memory_space=pltpu.VMEM)
SMEM = pl.BlockSpec(memory_space=pltpu.SMEM)
PARAMS = pltpu.CompilerParams(vmem_limit_bytes=48 * 1024 * 1024)


def place(half, turn, pair, core):
    return ((half * TURNS + turn % TURNS) * PAIR + pair) * CORES + core


def moved(value, to):
    spots = [
        (h, t, p, k)
        for h in range(HALVES)
        for t in range(TURNS)
        for p in range(PAIR)
        for k in range(CORES)
    ]
    pairs = [(place(*s), place(*to(*s))) for s in spots if to(*s) is not None]
    return lax.ppermute(value, "ctx", pairs)


def along(value, steps):
    pairs = [(i, i + steps) for i in range(CTX) if 0 <= i + steps < CTX]
    return lax.ppermute(value, "ctx", pairs)


def other_core(value):
    return moved(value, lambda h, t, p, k: (h, t, p, 1 - k))


def other_pair(value):
    return moved(value, lambda h, t, p, k: (h, t, 1 - p, k))


def across(value, source):
    return moved(value, lambda h, t, p, k: (1 - h, t, p, k) if h == source else None)


def turned(value, way):
    return moved(value, lambda h, t, p, k: (h, t + way * (1 - 2 * k), p, k))


def contract_last(left, right):
    return lax.dot_general(left, right, (((1,), (1,)), ((), ())), preferred_element_type=F32)


def contract_first(left, right):
    return lax.dot_general(left, right, (((0,), (0,)), ((), ())), preferred_element_type=F32)


def cut_kernel(head_ref, q_ref, k_ref, v_ref, out_ref):
    out_ref[:, :HEAD] = q_ref[...]
    out_ref[:, HEAD : 2 * HEAD] = k_ref[...]
    out_ref[:, 2 * HEAD :] = v_ref[...]


def columns_in(w_query, w_key, w_value, head):
    rows = w_query.shape[0]
    block = pl.BlockSpec((rows, HEAD), lambda i, h: (0, h[0]))
    mine = pl.pallas_call(
        cut_kernel,
        grid_spec=pltpu.PrefetchScalarGridSpec(
            num_scalar_prefetch=1,
            grid=(1,),
            in_specs=[block] * 3,
            out_specs=pl.BlockSpec((rows, 3 * HEAD), lambda i, h: (0, 0)),
        ),
        out_shape=jax.ShapeDtypeStruct((rows, 3 * HEAD), w_query.dtype),
    )(head[None], w_query, w_key, w_value)
    count = ROWS_X * ROWS_Y
    swap = [(d, (d + ROWS_Y) % count) for d in range(count)]
    both = jnp.concatenate([mine, lax.ppermute(mine, "dp", swap)], axis=0)

    def shifted(step):
        pairs = [(d, d // ROWS_Y * ROWS_Y + (d + step) % ROWS_Y) for d in range(count)]
        return lax.ppermute(both, "dp", pairs)

    return [both, shifted(1), shifted(-1), shifted(2)]


def rows_out(w_out, turn, core):
    rows = w_out.shape[0] // CORES
    half = lax.dynamic_slice(w_out, (core * rows, 0), (rows, w_out.shape[1]))
    gathered = lax.all_gather(half, "dp", axis=0, tiled=False)
    mine = lax.dynamic_index_in_dim(gathered, turn * CORES + core, 0, keepdims=False)
    theirs = lax.dynamic_index_in_dim(gathered, turn * CORES + 1 - core, 0, keepdims=False)
    return mine, other_core(theirs)


def gathered_rows(shard):
    swapped = other_core(shard)
    near = turned(jnp.concatenate([shard, swapped], axis=0), 1)
    far = turned(near[: shard.shape[0]], 1)
    return [shard, swapped, near, other_core(near), far, other_core(far)]


def rows_at(row, half, turn, pair, core, seg):
    slot = row // seg
    two = slot // 2
    way = 1 - 2 * core
    step = jnp.where(two == 0, 0, jnp.where(two == 1, way, jnp.where(two == 2, -way, 2)))
    flip = jnp.where(two == 2, 1 - slot % 2, slot % 2)
    its_core = jnp.where(flip == 1, 1 - core, core)
    its_turn = (turn - step + TURNS) % TURNS
    return place(half, its_turn, pair, its_core) * seg + row % seg


def fill(out_ref, pieces):
    at = 0
    for piece in pieces:
        out_ref[at : at + piece.shape[0], :] = piece[...]
        at += piece.shape[0]


def project_kernel(*refs):
    place_ref, pieces, weights = refs[0], refs[1:7], refs[7:11]
    q_ref, top_ref, bottom_ref, w_ref, rows = refs[11:]
    fill(rows, pieces)
    dp = place_ref[4]
    x, y = dp // ROWS_Y, dp % ROWS_Y
    depth = weights[0].shape[0] // ROWS_X
    for weight, step in zip(weights, (0, 1, -1, 2)):
        its_y = (y - step + ROWS_Y) % ROWS_Y
        for i in range(ROWS_X):
            its_x = x if i == 0 else 1 - x
            at = pl.multiple_of((its_x * ROWS_Y + its_y) * depth, depth)
            w_ref[pl.ds(at, depth), :] = weight[i * depth : (i + 1) * depth, :]
    out = jnp.dot(rows[...], w_ref[...], preferred_element_type=F32).astype(jnp.bfloat16)
    cut = out.shape[0] // 2
    q_ref[...] = out[:, :HEAD]
    top_ref[...] = out[:cut, HEAD:]
    bottom_ref[...] = out[cut:, HEAD:]


def project(where, pieces, weights):
    rows = sum(piece.shape[0] for piece in pieces)
    width = pieces[0].shape[1]
    bf16 = lambda *shape: jax.ShapeDtypeStruct(shape, jnp.bfloat16)
    return pl.pallas_call(
        project_kernel,
        out_shape=(
            bf16(rows, HEAD),
            bf16(rows // 2, 2 * HEAD),
            bf16(rows // 2, 2 * HEAD),
            bf16(width, 3 * HEAD),
        ),
        in_specs=[SMEM] + [VMEM] * 10,
        out_specs=(VMEM,) * 4,
        scratch_shapes=[pltpu.VMEM((rows, width), jnp.bfloat16)],
        compiler_params=PARAMS,
    )(where, *pieces, *weights)


def dattended_kernel(*refs):
    place_ref, pieces, mine, theirs, da_ref, rows, weight = (
        refs[0],
        refs[1:7],
        refs[7],
        refs[8],
        refs[9],
        refs[10],
        refs[11],
    )
    core = place_ref[3]
    half = mine.shape[0]
    fill(rows, pieces)
    weight[pl.ds(pl.multiple_of(core * half, half), half), :] = mine[...]
    weight[pl.ds(pl.multiple_of((1 - core) * half, half), half), :] = theirs[...]
    da_ref[...] = contract_last(rows[...], weight[...]).astype(jnp.bfloat16)


def dattended(where, pieces, mine, theirs):
    rows = sum(piece.shape[0] for piece in pieces)
    width = pieces[0].shape[1]
    return pl.pallas_call(
        dattended_kernel,
        out_shape=jax.ShapeDtypeStruct((rows, HEAD), jnp.bfloat16),
        in_specs=[SMEM] + [VMEM] * 8,
        out_specs=VMEM,
        scratch_shapes=[
            pltpu.VMEM((rows, width), jnp.bfloat16),
            pltpu.VMEM((HEAD, width), jnp.bfloat16),
        ],
        compiler_params=PARAMS,
    )(where, *pieces, mine, theirs)


def attention_kernel(tile, seg, *refs):
    place_ref, q_ref, da_ref, blocks = refs[0], refs[1], refs[2], refs[3:11]
    dq_ref, outs, kv, dkt, dvt = refs[11], refs[12:20], refs[20], refs[21], refs[22]
    half, turn, pair, core = place_ref[0], place_ref[1], place_ref[2], place_ref[3]
    queries, keys = q_ref.shape[0], kv.shape[0]
    fill(kv, blocks)
    spot = lax.broadcasted_iota(jnp.int32, (1, keys), 1)
    block = spot // queries
    key_half = jnp.where(block < 2, half, 1 - half)
    key_pair = jnp.where(block % 2 == 0, pair, 1 - pair)
    key_at = rows_at(spot % queries, key_half, turn, key_pair, core, seg)
    turn_up = math.log2(math.e) / math.sqrt(HEAD)
    scale = 1.0 / math.sqrt(HEAD)
    k = kv[:, :HEAD]
    v = kv[:, HEAD:]
    for step in range(queries // tile):
        rows = slice(step * tile, (step + 1) * tile)
        query = lax.broadcasted_iota(jnp.int32, (tile, 1), 0) + step * tile
        query_at = rows_at(query, half, turn, pair, core, seg)
        q = q_ref[rows, :]
        da = da_ref[rows, :]
        score = jnp.where(key_at <= query_at, contract_last(q, k), NEG)
        peak = jnp.max(score, axis=1, keepdims=True)
        expo = jnp.exp2((score - peak) * turn_up)
        probs = expo * (1.0 / jnp.sum(expo, axis=1, keepdims=True))
        probs_b = probs.astype(jnp.bfloat16)
        attended = jnp.dot(probs_b, v, preferred_element_type=F32).astype(jnp.bfloat16)
        delta = jnp.sum(da.astype(F32) * attended.astype(F32), axis=1, keepdims=True)
        dscore = (probs * (contract_last(da, v) - delta)).astype(jnp.bfloat16)
        dq = jnp.dot(dscore, k, preferred_element_type=F32) * scale
        dq_ref[rows, :] = dq.astype(jnp.bfloat16)
        dk_part = contract_first(q, dscore)
        dv_part = contract_first(da, probs_b)
        if step == 0:
            dkt[...] = dk_part
            dvt[...] = dv_part
        else:
            dkt[...] += dk_part
            dvt[...] += dv_part
    part = keys // len(outs)
    for i, out in enumerate(outs):
        lanes = slice(i * part, (i + 1) * part)
        out[:, :HEAD] = (dkt[:, lanes] * scale).T.astype(jnp.bfloat16)
        out[:, HEAD:] = dvt[:, lanes].T.astype(jnp.bfloat16)


def attention(where, q, da, blocks, seg):
    queries = q.shape[0]
    keys = sum(block.shape[0] for block in blocks)
    part = jax.ShapeDtypeStruct(blocks[0].shape, jnp.bfloat16)
    return pl.pallas_call(
        functools.partial(attention_kernel, 128, seg),
        out_shape=(jax.ShapeDtypeStruct((queries, HEAD), jnp.bfloat16),) + (part,) * 8,
        in_specs=[SMEM] + [VMEM] * 10,
        out_specs=(VMEM,) * 9,
        scratch_shapes=[
            pltpu.VMEM((keys, 2 * HEAD), jnp.bfloat16),
            pltpu.VMEM((HEAD, keys), F32),
            pltpu.VMEM((HEAD, keys), F32),
        ],
        compiler_params=PARAMS,
        cost_estimate=pl.CostEstimate(
            flops=12 * queries * keys * HEAD,
            bytes_accessed=2 * HEAD * (3 * queries + 4 * keys),
            transcendentals=queries * keys,
        ),
    )(where, q, da, *blocks)


def unproject_kernel(seg, dq_ref, *refs):
    dkv_parts, w_ref = refs[:6], refs[6]
    swap_ref, far_ref, near_ref, own_ref = refs[7:11]
    top = sum(ref[...].astype(F32) for ref in dkv_parts[0::2])
    bottom = sum(ref[...].astype(F32) for ref in dkv_parts[1::2])
    dkv = jnp.concatenate([top, bottom], axis=0).astype(jnp.bfloat16)
    left = jnp.concatenate([dq_ref[...], dkv], axis=1)
    out = contract_last(left, w_ref[...])
    own_ref[...] = out[: 2 * seg]
    near_ref[...] = out[2 * seg : 4 * seg]
    swap_ref[: 2 * seg, :] = out[4 * seg : 6 * seg].astype(WIRE)
    far_ref[...] = out[6 * seg : 7 * seg]
    swap_ref[2 * seg :, :] = out[7 * seg :].astype(WIRE)


def unproject(dq, dkv_parts, w_full, seg):
    width = w_full.shape[0]
    return pl.pallas_call(
        functools.partial(unproject_kernel, seg),
        out_shape=(
            jax.ShapeDtypeStruct((3 * seg, width), WIRE),
            jax.ShapeDtypeStruct((seg, width), F32),
            jax.ShapeDtypeStruct((2 * seg, width), F32),
            jax.ShapeDtypeStruct((2 * seg, width), F32),
        ),
        in_specs=[VMEM] * 8,
        out_specs=(VMEM,) * 4,
        compiler_params=PARAMS,
    )(dq, *dkv_parts, w_full)


def summed_rows(swap, far, near, own, seg):
    swapped = other_core(swap).astype(F32)
    back = turned((far + swapped[2 * seg :]).astype(WIRE), -1).astype(F32)
    near = near + swapped[: 2 * seg] + jnp.pad(back, ((0, seg), (0, 0)))
    own = own + turned(near.astype(WIRE), -1).astype(F32)
    return own[:seg] + other_core(own[seg:].astype(WIRE)).astype(F32)


def per_device(tokens, starts, gain, w_query, w_key, w_value, w_out, cotangent):
    token_rows = tokens[0]
    grad_out = cotangent[0]
    own_starts = starts[0]
    rows, width = token_rows.shape
    seg = own_starts.shape[0]
    length = rows * CTX
    ctx = lax.axis_index("ctx")
    core, pair = ctx % CORES, ctx // CORES % PAIR
    turn, half = ctx // (CORES * PAIR) % TURNS, ctx // (CORES * PAIR * TURNS)
    where = jnp.stack([half, turn, pair, core, lax.axis_index("dp")])

    before = jnp.where(ctx == 0, -1, along(own_starts, 1))
    after = jnp.where(ctx == CTX - 1, length, along(own_starts, -1))
    weights = columns_in(w_query, w_key, w_value, turn * CORES + core)
    out_mine, out_theirs = rows_out(w_out, turn, core)
    window = jnp.concatenate([before, own_starts, after])
    positions = ctx * rows + lax.iota(jnp.int32, rows)
    ends = jnp.concatenate([window[1:], jnp.full((1,), length, jnp.int32)])
    member = (
        (window[None, :] <= positions[:, None]) & (positions[:, None] < ends[None, :])
    ).astype(jnp.bfloat16)
    token_sum = contract_first(member, token_rows)
    grad_sum = contract_first(member, grad_out)
    lower = jnp.concatenate([token_sum[:seg], grad_sum[1 : seg + 1]], axis=1).astype(WIRE)
    tail = jnp.concatenate([grad_sum[2 * seg + 1 :], jnp.zeros((1, width), F32)], axis=0)
    upper = jnp.concatenate([token_sum[2 * seg :], tail], axis=1).astype(WIRE)
    from_after = along(lower, -1).astype(F32)
    from_before = along(upper, 1).astype(F32)
    from_second = along(grad_sum[:1].astype(WIRE), -2).astype(F32)
    count = (ends - window)[seg : 2 * seg].astype(F32)
    pooled = token_sum[seg : 2 * seg] + from_after[:, :width] + from_before[:, :width]
    pooled = pooled / count[:, None]
    last = lax.broadcasted_iota(jnp.int32, (seg, 1), 0) == seg - 1
    dout = grad_sum[seg + 1 : 2 * seg + 1] + from_after[:, width:] + from_before[:, width:]
    dout = dout + jnp.where(last, from_second, 0.0)
    rms = jnp.sqrt(jnp.mean(pooled * pooled, axis=-1, keepdims=True) + 1e-06)
    normed = pooled / rms
    normin = (normed * gain).astype(jnp.bfloat16)

    pieces = gathered_rows(normin)
    q, own_top, own_bottom, w_full = project(where, pieces, weights)
    dout_b, _ = lax.optimization_barrier((dout.astype(jnp.bfloat16), pieces[4]))
    da = dattended(where, gathered_rows(dout_b), out_mine, out_theirs)
    pair_top, far_bottom = other_pair(own_top), across(own_bottom, 0)
    pair_bottom, far_top = other_pair(own_bottom), across(own_top, 0)
    cross_top, cross_bottom = across(pair_top, 0), other_pair(far_bottom)
    blocks = (
        own_top,
        own_bottom,
        pair_top,
        pair_bottom,
        far_top,
        far_bottom,
        cross_top,
        cross_bottom,
    )
    dq, *grads = attention(where, q, da, blocks, seg)
    own_top, own_bottom, pair_top, pair_bottom, far_top, far_bottom, cross_top, cross_bottom = grads
    add = lambda a, b: (a.astype(F32) + b.astype(F32)).astype(WIRE)
    back_top, back_bottom = across(cross_top, 1), other_pair(cross_bottom)
    got_bottom, got_far_top = other_pair(pair_bottom), across(far_top, 1)
    got_top = other_pair(add(pair_top, back_top))
    got_far_bottom = across(add(far_bottom, back_bottom), 1)
    parts = (own_top, own_bottom, got_top, got_bottom, got_far_top, got_far_bottom)
    dnormin = summed_rows(*unproject(dq, parts, w_full, seg), seg)

    scaled = dnormin * gain
    dpooled = dout + (scaled - normed * jnp.mean(scaled * normed, axis=-1, keepdims=True)) / rms
    per_seg = (dpooled / count[:, None]).astype(WIRE)
    per_window = jnp.concatenate([along(per_seg, 1), per_seg, along(per_seg, -1)], axis=0)
    spread = jnp.dot(member, per_window, preferred_element_type=F32)
    return (grad_out.astype(F32) + spread).astype(jnp.bfloat16)[None]


def solution(mesh):
    return jax.shard_map(
        per_device,
        mesh=mesh,
        in_specs=(
            P("dp", "ctx", None),
            P("dp", "ctx"),
            P(),
            P("dp", None),
            P("dp", None),
            P("dp", None),
            P("dp", None),
            P("dp", "ctx", None),
        ),
        out_specs=P("dp", "ctx", None),
        check_vma=False,
    )
```

```python
import functools
import math

import jax
import jax.numpy as jnp
from jax import lax
from jax.experimental import pallas as pl
from jax.experimental.pallas import tpu as pltpu
from jax.sharding import PartitionSpec as P

HEAD = 128
HALVES, TURNS, PAIR, CORES = 2, 4, 2, 2
CTX = HALVES * TURNS * PAIR * CORES
ROWS_X, ROWS_Y = 2, 4
NEG = -1e30
WIRE = jnp.bfloat16
F32 = jnp.float32
VMEM = pl.BlockSpec(memory_space=pltpu.VMEM)
SMEM = pl.BlockSpec(memory_space=pltpu.SMEM)
ANY = pl.BlockSpec(memory_space=pl.ANY)
PARAMS = pltpu.CompilerParams(vmem_limit_bytes=48 * 1024 * 1024)


def place(half, turn, pair, core):
    return ((half * TURNS + turn % TURNS) * PAIR + pair) * CORES + core


def moved(value, to):
    spots = [
        (h, t, p, k)
        for h in range(HALVES)
        for t in range(TURNS)
        for p in range(PAIR)
        for k in range(CORES)
    ]
    pairs = [(place(*s), place(*to(*s))) for s in spots if to(*s) is not None]
    return lax.ppermute(value, "ctx", pairs)


def other_chip(value):
    pairs = [(i, i + 1 if i % CORES else i - 1) for i in range(1, CTX - 1)]
    return lax.ppermute(value, "ctx", pairs)


def two_back(value):
    return lax.ppermute(value, "ctx", [(i, i - CORES) for i in range(CORES, CTX)])


def other_core(value):
    return moved(value, lambda h, t, p, k: (h, t, p, 1 - k))


def other_pair(value):
    return moved(value, lambda h, t, p, k: (h, t, 1 - p, k))


def across(value, source):
    return moved(value, lambda h, t, p, k: (1 - h, t, p, k) if h == source else None)


def turned(value, way):
    return moved(value, lambda h, t, p, k: (h, t + way * (1 - 2 * k), p, k))


def contract_last(left, right):
    return lax.dot_general(left, right, (((1,), (1,)), ((), ())), preferred_element_type=F32)


def contract_first(left, right):
    return lax.dot_general(left, right, (((0,), (0,)), ((), ())), preferred_element_type=F32)


def cut_kernel(head_ref, q_ref, k_ref, v_ref, out_ref):
    out_ref[:, :HEAD] = q_ref[...]
    out_ref[:, HEAD : 2 * HEAD] = k_ref[...]
    out_ref[:, 2 * HEAD :] = v_ref[...]


def columns_in(w_query, w_key, w_value, head):
    rows = w_query.shape[0]
    block = pl.BlockSpec((rows, HEAD), lambda i, h: (0, h[0]))
    return pl.pallas_call(
        cut_kernel,
        grid_spec=pltpu.PrefetchScalarGridSpec(
            num_scalar_prefetch=1,
            grid=(1,),
            in_specs=[block] * 3,
            out_specs=pl.BlockSpec((rows, 3 * HEAD), lambda i, h: (0, 0)),
        ),
        out_shape=jax.ShapeDtypeStruct((rows, 3 * HEAD), w_query.dtype),
    )(head[None], w_query, w_key, w_value)


def other_x(value):
    count = ROWS_X * ROWS_Y
    return lax.ppermute(value, "dp", [(d, (d + ROWS_Y) % count) for d in range(count)])


def shifted_y(value, step):
    pairs = [(d, d // ROWS_Y * ROWS_Y + (d + step) % ROWS_Y) for d in range(ROWS_X * ROWS_Y)]
    return lax.ppermute(value, "dp", pairs)


def rows_out(w_out, turn, core):
    rows = w_out.shape[0] // CORES
    half = lax.dynamic_slice(w_out, (core * rows, 0), (rows, w_out.shape[1]))
    gathered = lax.all_gather(half, "dp", axis=0, tiled=False)
    mine = lax.dynamic_index_in_dim(gathered, turn * CORES + core, 0, keepdims=False)
    theirs = lax.dynamic_index_in_dim(gathered, turn * CORES + 1 - core, 0, keepdims=False)
    return mine, other_core(theirs)


def gathered_rows(shard):
    swapped = other_core(shard)
    near = turned(shard, 1)
    far = turned(near, 1)
    next_to = turned(swapped, 1)
    return [
        shard,
        swapped,
        near,
        next_to,
        other_core(near),
        other_core(next_to),
        far,
        other_core(far),
    ]


def rows_at(row, half, turn, pair, core, seg):
    slot = row // seg
    two = slot // 2
    way = 1 - 2 * core
    step = jnp.where(two == 0, 0, jnp.where(two == 1, way, jnp.where(two == 2, -way, 2)))
    flip = jnp.where(two == 2, 1 - slot % 2, slot % 2)
    its_core = jnp.where(flip == 1, 1 - core, core)
    its_turn = (turn - step + TURNS) % TURNS
    return place(half, its_turn, pair, its_core) * seg + row % seg


def fetched(copies, sems):
    started = []
    for i, (source, target) in enumerate(copies):
        started.append(pltpu.make_async_copy(source, target, sems.at[i]))
        started[-1].start()
    for copy in started:
        copy.wait()


def stacked(pieces, out_ref):
    copies, at = [], 0
    for piece in pieces:
        copies.append((piece, out_ref.at[at : at + piece.shape[0], :]))
        at += piece.shape[0]
    return copies


def window_kernel(place_ref, edge_ref, token_ref, grad_ref, mine_ref, theirs_ref, *outs):
    core_ref, chip_ref, mid_token, mid_grad, first_ref, both_ref = outs
    rows, width = token_ref.shape
    seg = mid_token.shape[0]
    ctx, core = place_ref[5], place_ref[3]
    at = lax.broadcasted_iota(jnp.int32, (1, rows), 1) + ctx * rows
    opens, ends, nexts = edge_ref[0], edge_ref[1], edge_ref[2]
    member = ((opens <= at) & (at < ends)).astype(jnp.bfloat16)
    earlier = ((ends <= at) & (at < nexts)).astype(jnp.bfloat16)
    token = jnp.dot(member, token_ref[...], preferred_element_type=F32)
    grad = jnp.dot(earlier, grad_ref[...], preferred_element_type=F32)
    first = jnp.dot(member[:16], grad_ref[...], preferred_element_type=F32)
    first_ref[...] = first[:1]
    mid_token[...] = token[seg : 2 * seg]
    mid_grad[...] = grad[seg : 2 * seg]
    both_ref[: mine_ref.shape[0], :] = mine_ref[...]
    both_ref[mine_ref.shape[0] :, :] = theirs_ref[...]

    def send(lower_ref, upper_ref):
        lower_ref[:, :width] = token[:seg].astype(WIRE)
        lower_ref[:, width:] = grad[:seg].astype(WIRE)
        upper_ref[:, :width] = token[2 * seg :].astype(WIRE)
        upper_ref[:, width:] = grad[2 * seg :].astype(WIRE)

    @pl.when(core == 0)
    def _():
        send(chip_ref, core_ref)

    @pl.when(core == 1)
    def _():
        send(core_ref, chip_ref)


def window_sums(where, edges, tokens, grads, mine, theirs, seg):
    width = tokens.shape[1]
    shape = jax.ShapeDtypeStruct
    return pl.pallas_call(
        window_kernel,
        out_shape=(
            shape((seg, 2 * width), WIRE),
            shape((seg, 2 * width), WIRE),
            shape((seg, width), F32),
            shape((seg, width), F32),
            shape((1, width), F32),
            shape((2 * mine.shape[0], mine.shape[1]), mine.dtype),
        ),
        in_specs=[SMEM] + [VMEM] * 5,
        out_specs=(VMEM,) * 6,
        compiler_params=PARAMS,
    )(where, edges, tokens, grads, mine, theirs)


def norm_kernel(core_ref, chip_ref, mid_token, mid_grad, count_ref, gain_ref, *refs):
    normin_ref, normed_ref, rms_ref, dout_ref = refs[-4:]
    width = mid_token.shape[1]
    got = core_ref[...].astype(F32) + chip_ref[...].astype(F32)
    pooled = (mid_token[...] + got[:, :width]) / count_ref[...]
    rms = jnp.sqrt(jnp.mean(pooled * pooled, axis=1, keepdims=True) + 1e-06)
    normed = pooled / rms
    normed_ref[...] = normed
    rms_ref[...] = rms
    normin_ref[...] = (normed * gain_ref[...]).astype(jnp.bfloat16)
    dout_ref[...] = mid_grad[...] + got[:, width:]


def norm(from_core, from_chip, mid_token, mid_grad, count, gain, ready):
    seg, width = mid_token.shape
    shape = jax.ShapeDtypeStruct
    return pl.pallas_call(
        norm_kernel,
        out_shape=(
            shape((seg, width), jnp.bfloat16),
            shape((seg, width), F32),
            shape((seg, 1), F32),
            shape((seg, width), F32),
        ),
        in_specs=[VMEM] * 6 + [ANY] * len(ready),
        out_specs=(VMEM,) * 4,
        compiler_params=PARAMS,
    )(from_core, from_chip, mid_token, mid_grad, count, gain, *ready)


def dout_kernel(dout_ref, second_ref, ready_ref, full_ref, half_ref):
    seg = dout_ref.shape[0]
    last = lax.broadcasted_iota(jnp.int32, (seg, 1), 0) == seg - 1
    dout = dout_ref[...] + jnp.where(last, second_ref[...].astype(F32), 0.0)
    full_ref[...] = dout
    half_ref[...] = dout.astype(jnp.bfloat16)


def whole_dout(dout, second, ready):
    shape = jax.ShapeDtypeStruct
    return pl.pallas_call(
        dout_kernel,
        out_shape=(shape(dout.shape, F32), shape(dout.shape, jnp.bfloat16)),
        in_specs=[VMEM, VMEM, ANY],
        out_specs=(VMEM, VMEM),
    )(dout, second, ready)


def project_kernel(*refs):
    place_ref, pieces, weights = refs[0], refs[1:9], refs[9:13]
    q_ref, top_ref, bottom_ref, w_ref, rows, sems = refs[13:]
    copies = stacked(pieces, rows)
    dp = place_ref[4]
    x, y = dp // ROWS_Y, dp % ROWS_Y
    depth = weights[0].shape[0] // ROWS_X
    for weight, step in zip(weights, (0, 1, -1, 2)):
        its_y = (y - step + ROWS_Y) % ROWS_Y
        for i in range(ROWS_X):
            its_x = x if i == 0 else 1 - x
            at = pl.multiple_of((its_x * ROWS_Y + its_y) * depth, depth)
            copies.append((weight.at[i * depth : (i + 1) * depth, :], w_ref.at[pl.ds(at, depth), :]))
    fetched(copies, sems)
    out = jnp.dot(rows[...], w_ref[...], preferred_element_type=F32).astype(jnp.bfloat16)
    cut = out.shape[0] // 2
    q_ref[...] = out[:, :HEAD]
    top_ref[...] = out[:cut, HEAD:]
    bottom_ref[...] = out[cut:, HEAD:]


def project(where, pieces, weights):
    rows = sum(piece.shape[0] for piece in pieces)
    width = pieces[0].shape[1]
    bf16 = lambda *shape: jax.ShapeDtypeStruct(shape, jnp.bfloat16)
    return pl.pallas_call(
        project_kernel,
        out_shape=(
            bf16(rows, HEAD),
            bf16(rows // 2, 2 * HEAD),
            bf16(rows // 2, 2 * HEAD),
            bf16(width, 3 * HEAD),
        ),
        in_specs=[SMEM] + [ANY] * 12,
        out_specs=(VMEM,) * 4,
        scratch_shapes=[
            pltpu.VMEM((rows, width), jnp.bfloat16),
            pltpu.SemaphoreType.DMA((16,)),
        ],
        compiler_params=PARAMS,
    )(where, *pieces, *weights)


def dattended_kernel(*refs):
    place_ref, pieces, mine, theirs = refs[0], refs[1:9], refs[9], refs[10]
    da_ref, rows, weight, sems = refs[11:]
    core = place_ref[3]
    half = mine.shape[0]
    spot = pl.multiple_of(core * half, half)
    other = pl.multiple_of((1 - core) * half, half)
    copies = stacked(pieces, rows)
    copies.append((mine, weight.at[pl.ds(spot, half), :]))
    copies.append((theirs, weight.at[pl.ds(other, half), :]))
    fetched(copies, sems)
    da_ref[...] = contract_last(rows[...], weight[...]).astype(jnp.bfloat16)


def dattended(where, pieces, mine, theirs):
    rows = sum(piece.shape[0] for piece in pieces)
    width = pieces[0].shape[1]
    return pl.pallas_call(
        dattended_kernel,
        out_shape=jax.ShapeDtypeStruct((rows, HEAD), jnp.bfloat16),
        in_specs=[SMEM] + [ANY] * 10,
        out_specs=VMEM,
        scratch_shapes=[
            pltpu.VMEM((rows, width), jnp.bfloat16),
            pltpu.VMEM((HEAD, width), jnp.bfloat16),
            pltpu.SemaphoreType.DMA((10,)),
        ],
        compiler_params=PARAMS,
    )(where, *pieces, mine, theirs)


def attention_kernel(tile, seg, *refs):
    place_ref, q_ref, da_ref, blocks = refs[0], refs[1], refs[2], refs[3:11]
    dq_ref, outs, (kv, dkt, dvt, sems) = refs[11], refs[12:20], refs[20:]
    half, turn, pair, core = place_ref[0], place_ref[1], place_ref[2], place_ref[3]
    queries, keys = q_ref.shape[0], kv.shape[0]
    fetched(stacked(blocks, kv), sems)
    spot = lax.broadcasted_iota(jnp.int32, (1, keys), 1)
    block = spot // queries
    key_half = jnp.where(block < 2, half, 1 - half)
    key_pair = jnp.where(block % 2 == 0, pair, 1 - pair)
    key_at = rows_at(spot % queries, key_half, turn, key_pair, core, seg)
    turn_up = math.log2(math.e) / math.sqrt(HEAD)
    scale = 1.0 / math.sqrt(HEAD)
    k = kv[:, :HEAD]
    v = kv[:, HEAD:]
    for step in range(queries // tile):
        rows = slice(step * tile, (step + 1) * tile)
        query = lax.broadcasted_iota(jnp.int32, (tile, 1), 0) + step * tile
        query_at = rows_at(query, half, turn, pair, core, seg)
        q = q_ref[rows, :]
        da = da_ref[rows, :]
        score = jnp.where(key_at <= query_at, contract_last(q, k), NEG)
        peak = jnp.max(score, axis=1, keepdims=True)
        expo = jnp.exp2((score - peak) * turn_up)
        probs = expo * (1.0 / jnp.sum(expo, axis=1, keepdims=True))
        probs_b = probs.astype(jnp.bfloat16)
        attended = jnp.dot(probs_b, v, preferred_element_type=F32).astype(jnp.bfloat16)
        delta = jnp.sum(da.astype(F32) * attended.astype(F32), axis=1, keepdims=True)
        dscore = (probs * (contract_last(da, v) - delta)).astype(jnp.bfloat16)
        dq = jnp.dot(dscore, k, preferred_element_type=F32) * scale
        dq_ref[rows, :] = dq.astype(jnp.bfloat16)
        dk_part = contract_first(q, dscore)
        dv_part = contract_first(da, probs_b)
        if step == 0:
            dkt[...] = dk_part
            dvt[...] = dv_part
        else:
            dkt[...] += dk_part
            dvt[...] += dv_part
    part = keys // len(outs)
    for i, out in enumerate(outs):
        lanes = slice(i * part, (i + 1) * part)
        out[:, :HEAD] = (dkt[:, lanes] * scale).T.astype(jnp.bfloat16)
        out[:, HEAD:] = dvt[:, lanes].T.astype(jnp.bfloat16)


def attention(where, q, da, blocks, seg):
    queries = q.shape[0]
    keys = sum(block.shape[0] for block in blocks)
    part = jax.ShapeDtypeStruct(blocks[0].shape, jnp.bfloat16)
    return pl.pallas_call(
        functools.partial(attention_kernel, 128, seg),
        out_shape=(jax.ShapeDtypeStruct((queries, HEAD), jnp.bfloat16),) + (part,) * 8,
        in_specs=[SMEM] + [VMEM] * 2 + [ANY] * 8,
        out_specs=(VMEM,) * 9,
        scratch_shapes=[
            pltpu.VMEM((keys, 2 * HEAD), jnp.bfloat16),
            pltpu.VMEM((HEAD, keys), F32),
            pltpu.VMEM((HEAD, keys), F32),
            pltpu.SemaphoreType.DMA((8,)),
        ],
        compiler_params=PARAMS,
        cost_estimate=pl.CostEstimate(
            flops=12 * queries * keys * HEAD,
            bytes_accessed=2 * HEAD * (3 * queries + 4 * keys),
            transcendentals=queries * keys,
        ),
    )(where, q, da, *blocks)


def unproject_kernel(seg, dq_ref, *refs):
    dkv_parts, w_ref, swap_ref, outs = refs[:6], refs[6], refs[7], refs[8:]
    top = sum(ref[...].astype(F32) for ref in dkv_parts[0::2])
    bottom = sum(ref[...].astype(F32) for ref in dkv_parts[1::2])
    dkv = jnp.concatenate([top, bottom], axis=0).astype(jnp.bfloat16)
    left = jnp.concatenate([dq_ref[...], dkv], axis=1)
    out = contract_last(left, w_ref[...])
    swap_ref[: 2 * seg, :] = out[4 * seg : 6 * seg].astype(WIRE)
    swap_ref[2 * seg :, :] = out[7 * seg :].astype(WIRE)
    for ref, slot in zip(outs, (0, 1, 2, 3, 6)):
        ref[...] = out[slot * seg : (slot + 1) * seg]


def unproject(dq, dkv_parts, w_full, seg):
    width = w_full.shape[0]
    return pl.pallas_call(
        functools.partial(unproject_kernel, seg),
        out_shape=(jax.ShapeDtypeStruct((3 * seg, width), WIRE),)
        + (jax.ShapeDtypeStruct((seg, width), F32),) * 5,
        in_specs=[VMEM] * 8,
        out_specs=(VMEM,) * 6,
        compiler_params=PARAMS,
    )(dq, *dkv_parts, w_full)


def summed_rows(swap, own, beside, near, next_to, far, seg):
    swapped = other_core(swap).astype(F32)
    far = turned((far + swapped[2 * seg :]).astype(WIRE), -1).astype(F32)
    next_to = turned((next_to + swapped[seg : 2 * seg]).astype(WIRE), -1).astype(F32)
    near = turned((near + swapped[:seg] + far).astype(WIRE), -1).astype(F32)
    beside = other_core((beside + next_to).astype(WIRE)).astype(F32)
    return own + near + beside


def per_device(tokens, starts, gain, w_query, w_key, w_value, w_out, cotangent):
    token_rows = tokens[0]
    grad_out = cotangent[0]
    own_starts = starts[0]
    rows, width = token_rows.shape
    seg = own_starts.shape[0]
    length = rows * CTX
    ctx = lax.axis_index("ctx")
    core, pair = ctx % CORES, ctx // CORES % PAIR
    turn, half = ctx // (CORES * PAIR) % TURNS, ctx // (CORES * PAIR * TURNS)
    where = jnp.stack([half, turn, pair, core, lax.axis_index("dp"), ctx])

    mine = columns_in(w_query, w_key, w_value, turn * CORES + core)
    theirs = other_x(mine)
    beside, facing = other_core(own_starts), other_chip(own_starts)
    before = jnp.where(core == 0, facing, beside)
    after = jnp.where(core == 0, beside, facing)
    before = jnp.where(ctx == 0, -1, before)
    after = jnp.where(ctx == CTX - 1, length, after)
    stop = jnp.full((2,), length, jnp.int32)
    window = jnp.concatenate([before, own_starts, after, stop])
    slots = 3 * seg
    opens, ends = window[:slots], window[1 : slots + 1]
    edges = jnp.stack([opens, ends, window[2:]])[:, :, None]
    count = (ends - opens)[seg : 2 * seg, None].astype(F32)
    to_core, to_chip, mid_token, mid_grad, first, both = window_sums(
        where, edges, token_rows, grad_out, mine, theirs, seg
    )
    weights = [both, shifted_y(both, 1), shifted_y(both, -1), shifted_y(both, 2)]
    second = two_back(first)
    normin, normed, rms, dout = norm(
        other_core(to_core),
        other_chip(to_chip),
        mid_token,
        mid_grad,
        count,
        gain[None],
        weights[1:],
    )
    pieces = gathered_rows(normin)
    q, own_top, own_bottom, w_full = project(where, pieces, weights)
    dout, dout_b = whole_dout(dout, second, pieces[6])
    out_mine, out_theirs = rows_out(w_out, turn, core)
    da = dattended(where, gathered_rows(dout_b), out_mine, out_theirs)
    pair_top, far_bottom = other_pair(own_top), across(own_bottom, 0)
    pair_bottom, far_top = other_pair(own_bottom), across(own_top, 0)
    cross_top, cross_bottom = across(pair_top, 0), other_pair(far_bottom)
    blocks = (
        own_top,
        own_bottom,
        pair_top,
        pair_bottom,
        far_top,
        far_bottom,
        cross_top,
        cross_bottom,
    )
    dq, *grads = attention(where, q, da, blocks, seg)
    own_top, own_bottom, pair_top, pair_bottom, far_top, far_bottom, cross_top, cross_bottom = grads
    add = lambda a, b: (a.astype(F32) + b.astype(F32)).astype(WIRE)
    back_top, back_bottom = across(cross_top, 1), other_pair(cross_bottom)
    got_bottom, got_far_top = other_pair(pair_bottom), across(far_top, 1)
    got_top = other_pair(add(pair_top, back_top))
    got_far_bottom = across(add(far_bottom, back_bottom), 1)
    parts = (own_top, own_bottom, got_top, got_bottom, got_far_top, got_far_bottom)
    dnormin = summed_rows(*unproject(dq, parts, w_full, seg), seg)

    scaled = dnormin * gain
    dpooled = dout + (scaled - normed * jnp.mean(scaled * normed, axis=-1, keepdims=True)) / rms
    per_seg = (dpooled / count).astype(WIRE)
    beside, facing = other_core(per_seg), other_chip(per_seg)
    before = jnp.where(core == 0, facing, beside)
    after = jnp.where(core == 0, beside, facing)
    per_window = jnp.concatenate([before, per_seg, after], axis=0)
    positions = (ctx * rows + lax.iota(jnp.int32, rows))[:, None]
    member = (opens[None] <= positions) & (positions < ends[None])
    spread = jnp.dot(member.astype(WIRE), per_window, preferred_element_type=F32)
    return (grad_out.astype(F32) + spread).astype(jnp.bfloat16)[None]


def solution(mesh):
    return jax.shard_map(
        per_device,
        mesh=mesh,
        in_specs=(
            P("dp", "ctx", None),
            P("dp", "ctx"),
            P(),
            P("dp", None),
            P("dp", None),
            P("dp", None),
            P("dp", None),
            P("dp", "ctx", None),
        ),
        out_specs=P("dp", "ctx", None),
        check_vma=False,
    )
```

```python
import functools
import math

import jax
import jax.numpy as jnp
from jax import lax
from jax.experimental import pallas as pl
from jax.experimental.pallas import tpu as pltpu
from jax.sharding import PartitionSpec as P

HEAD = 128
HALVES, TURNS, PAIR, CORES = 2, 4, 2, 2
CTX = HALVES * TURNS * PAIR * CORES
ROWS_X, ROWS_Y = 2, 4
NEG = -1e30
WIRE = jnp.bfloat16
F32 = jnp.float32
VMEM = pl.BlockSpec(memory_space=pltpu.VMEM)
SMEM = pl.BlockSpec(memory_space=pltpu.SMEM)
ANY = pl.BlockSpec(memory_space=pl.ANY)
PARAMS = pltpu.CompilerParams(vmem_limit_bytes=48 * 1024 * 1024)


def place(half, turn, pair, core):
    return ((half * TURNS + turn % TURNS) * PAIR + pair) * CORES + core


def moved(value, to):
    spots = [
        (h, t, p, k)
        for h in range(HALVES)
        for t in range(TURNS)
        for p in range(PAIR)
        for k in range(CORES)
    ]
    pairs = [(place(*s), place(*to(*s))) for s in spots if to(*s) is not None]
    return lax.ppermute(value, "ctx", pairs)


def other_chip(value):
    pairs = [(i, i + 1 if i % CORES else i - 1) for i in range(1, CTX - 1)]
    return lax.ppermute(value, "ctx", pairs)


def two_back(value):
    return lax.ppermute(value, "ctx", [(i, i - CORES) for i in range(CORES, CTX)])


def other_core(value):
    return moved(value, lambda h, t, p, k: (h, t, p, 1 - k))


def other_pair(value):
    return moved(value, lambda h, t, p, k: (h, t, 1 - p, k))


def across(value, source, cross):
    return moved(
        value,
        lambda h, t, p, k: (1 - h, t, 1 - p if cross else p, k) if h == source else None,
    )


def turned(value, way):
    return moved(value, lambda h, t, p, k: (h, t + way * (1 - 2 * k), p, k))


def turned_over(value):
    return moved(value, lambda h, t, p, k: (h, t - (1 - 2 * k), p, 1 - k))


def contract_last(left, right):
    return lax.dot_general(left, right, (((1,), (1,)), ((), ())), preferred_element_type=F32)


def contract_first(left, right):
    return lax.dot_general(left, right, (((0,), (0,)), ((), ())), preferred_element_type=F32)


def cut_kernel(head_ref, q_ref, k_ref, v_ref, start_ref, out_ref, start_out):
    out_ref[:, :HEAD] = q_ref[...]
    out_ref[:, HEAD : 2 * HEAD] = k_ref[...]
    out_ref[:, 2 * HEAD :] = v_ref[...]
    start_out[...] = start_ref[...]


def columns_in(w_query, w_key, w_value, starts, head):
    rows = w_query.shape[0]
    block = pl.BlockSpec((rows, HEAD), lambda i, h: (0, h[0]))
    whole = pl.BlockSpec(starts.shape, lambda i, h: (0, 0))
    return pl.pallas_call(
        cut_kernel,
        grid_spec=pltpu.PrefetchScalarGridSpec(
            num_scalar_prefetch=1,
            grid=(1,),
            in_specs=[block] * 3 + [whole],
            out_specs=(pl.BlockSpec((rows, 3 * HEAD), lambda i, h: (0, 0)), whole),
        ),
        out_shape=(
            jax.ShapeDtypeStruct((rows, 3 * HEAD), w_query.dtype),
            jax.ShapeDtypeStruct(starts.shape, starts.dtype),
        ),
        compiler_params=PARAMS,
    )(head[None], w_query, w_key, w_value, starts)


def other_x(value):
    count = ROWS_X * ROWS_Y
    return lax.ppermute(value, "dp", [(d, (d + ROWS_Y) % count) for d in range(count)])


def shifted_y(value, step):
    pairs = [(d, d // ROWS_Y * ROWS_Y + (d + step) % ROWS_Y) for d in range(ROWS_X * ROWS_Y)]
    return lax.ppermute(value, "dp", pairs)


def rows_out(half, turn, core):
    gathered = lax.all_gather(half, "dp", axis=0, tiled=False)
    mine = lax.dynamic_index_in_dim(gathered, turn * CORES + core, 0, keepdims=False)
    theirs = lax.dynamic_index_in_dim(gathered, turn * CORES + 1 - core, 0, keepdims=False)
    return mine, other_core(theirs)


def pass_kernel(value_ref, ready_ref, out_ref):
    out_ref[...] = value_ref[...]


def passed_on(value, ready):
    return pl.pallas_call(
        pass_kernel,
        out_shape=jax.ShapeDtypeStruct(value.shape, value.dtype),
        in_specs=[VMEM, ANY],
        out_specs=VMEM,
        compiler_params=PARAMS,
    )(value, ready)


def gathered_rows(shard, ready):
    near = turned(shard, 1)
    next_to = turned_over(shard)
    far = turned(passed_on(near, ready), 1)
    return [
        shard,
        other_core(shard),
        near,
        next_to,
        other_core(near),
        other_core(next_to),
        far,
        other_core(far),
    ]


def rows_at(row, half, turn, pair, core, seg):
    slot = row // seg
    two = slot // 2
    way = 1 - 2 * core
    step = jnp.where(two == 0, 0, jnp.where(two == 1, way, jnp.where(two == 2, -way, 2)))
    flip = jnp.where(two == 2, 1 - slot % 2, slot % 2)
    its_core = jnp.where(flip == 1, 1 - core, core)
    its_turn = (turn - step + TURNS) % TURNS
    return place(half, its_turn, pair, its_core) * seg + row % seg


def fetched(copies, sems):
    started = []
    for i, (source, target) in enumerate(copies):
        started.append(pltpu.make_async_copy(source, target, sems.at[i]))
        started[-1].start()
    for copy in started:
        copy.wait()


def stacked(pieces, out_ref):
    copies, at = [], 0
    for piece in pieces:
        copies.append((piece, out_ref.at[at : at + piece.shape[0], :]))
        at += piece.shape[0]
    return copies


def window_kernel(place_ref, edge_ref, token_hbm, grad_hbm, mine_hbm, theirs_hbm, *refs):
    core_ref, chip_ref, mid_token, mid_grad, first_ref, both_ref = refs[:6]
    token_ref, grad_ref, sems = refs[6:]
    rows, width = token_ref.shape
    seg = mid_token.shape[0]
    half = mine_hbm.shape[0]
    fetched(
        [
            (token_hbm, token_ref),
            (grad_hbm, grad_ref),
            (mine_hbm, both_ref.at[:half, :]),
            (theirs_hbm, both_ref.at[half:, :]),
        ],
        sems,
    )
    ctx, core = place_ref[5], place_ref[3]
    at = lax.broadcasted_iota(jnp.int32, (1, rows), 1) + ctx * rows
    opens, ends, nexts = edge_ref[0], edge_ref[1], edge_ref[2]
    member = ((opens <= at) & (at < ends)).astype(jnp.bfloat16)
    earlier = ((ends <= at) & (at < nexts)).astype(jnp.bfloat16)
    token = jnp.dot(member, token_ref[...], preferred_element_type=F32)
    grad = jnp.dot(earlier, grad_ref[...], preferred_element_type=F32)
    first = jnp.dot(member[:16], grad_ref[...], preferred_element_type=F32)
    first_ref[...] = first[:1]
    mid_token[...] = token[seg : 2 * seg]
    mid_grad[...] = grad[seg : 2 * seg]

    def send(lower_ref, upper_ref):
        lower_ref[:, :width] = token[:seg].astype(WIRE)
        lower_ref[:, width:] = grad[:seg].astype(WIRE)
        upper_ref[:, :width] = token[2 * seg :].astype(WIRE)
        upper_ref[:, width:] = grad[2 * seg :].astype(WIRE)

    @pl.when(core == 0)
    def _():
        send(chip_ref, core_ref)

    @pl.when(core == 1)
    def _():
        send(core_ref, chip_ref)


def window_sums(where, edges, tokens, grads, mine, theirs, seg):
    rows, width = tokens.shape
    shape = jax.ShapeDtypeStruct
    return pl.pallas_call(
        window_kernel,
        out_shape=(
            shape((seg, 2 * width), WIRE),
            shape((seg, 2 * width), WIRE),
            shape((seg, width), F32),
            shape((seg, width), F32),
            shape((1, width), F32),
            shape((2 * mine.shape[0], mine.shape[1]), mine.dtype),
        ),
        in_specs=[SMEM, VMEM] + [ANY] * 4,
        out_specs=(VMEM,) * 6,
        scratch_shapes=[
            pltpu.VMEM((rows, width), tokens.dtype),
            pltpu.VMEM((rows, width), grads.dtype),
            pltpu.SemaphoreType.DMA((4,)),
        ],
        compiler_params=PARAMS,
    )(where, edges, tokens, grads, mine, theirs)


def norm_kernel(place_ref, core_ref, chip_ref, mid_token, mid_grad, second_ref, count_ref, *refs):
    gain_ref, w_ref = refs[:2]
    both_ref, normed_ref, rms_ref, dout_ref, half_ref, sem = refs[-6:]
    seg, width = mid_token.shape
    rows = half_ref.shape[0]
    core = place_ref[3]
    at = pl.multiple_of(core * rows, rows)
    copy = pltpu.make_async_copy(w_ref.at[pl.ds(at, rows), :], half_ref, sem)
    copy.start()
    got = core_ref[...].astype(F32) + chip_ref[...].astype(F32)
    pooled = (mid_token[...] + got[:, :width]) / count_ref[...]
    rms = jnp.sqrt(jnp.mean(pooled * pooled, axis=1, keepdims=True) + 1e-06)
    normed = pooled / rms
    normed_ref[...] = normed
    rms_ref[...] = rms
    last = lax.broadcasted_iota(jnp.int32, (seg, 1), 0) == seg - 1
    dout = mid_grad[...] + got[:, width:] + jnp.where(last, second_ref[...], 0.0)
    dout_ref[...] = dout
    both_ref[:, :width] = (normed * gain_ref[...]).astype(jnp.bfloat16)
    both_ref[:, width:] = dout.astype(jnp.bfloat16)
    copy.wait()


def norm(where, from_core, from_chip, mid_token, mid_grad, second, count, gain, w_out, ready):
    seg, width = mid_token.shape
    shape = jax.ShapeDtypeStruct
    return pl.pallas_call(
        norm_kernel,
        out_shape=(
            shape((seg, 2 * width), jnp.bfloat16),
            shape((seg, width), F32),
            shape((seg, 1), F32),
            shape((seg, width), F32),
            shape((w_out.shape[0] // CORES, w_out.shape[1]), w_out.dtype),
        ),
        in_specs=[SMEM] + [VMEM] * 7 + [ANY] * (1 + len(ready)),
        out_specs=(VMEM,) * 5,
        scratch_shapes=[pltpu.SemaphoreType.DMA],
        compiler_params=PARAMS,
    )(where, from_core, from_chip, mid_token, mid_grad, second, count, gain, w_out, *ready)


def project_kernel(*refs):
    place_ref, pieces, weights = refs[0], refs[1:9], refs[9:13]
    q_ref, kv_ref, w_ref, rows, sems = refs[13:]
    copies = stacked([piece.at[:, : rows.shape[1]] for piece in pieces], rows)
    dp = place_ref[4]
    x, y = dp // ROWS_Y, dp % ROWS_Y
    depth = weights[0].shape[0] // ROWS_X
    for weight, step in zip(weights, (0, 1, -1, 2)):
        its_y = (y - step + ROWS_Y) % ROWS_Y
        for i in range(ROWS_X):
            its_x = x if i == 0 else 1 - x
            at = pl.multiple_of((its_x * ROWS_Y + its_y) * depth, depth)
            copies.append((weight.at[i * depth : (i + 1) * depth, :], w_ref.at[pl.ds(at, depth), :]))
    fetched(copies, sems)
    out = jnp.dot(rows[...], w_ref[...], preferred_element_type=F32).astype(jnp.bfloat16)
    q_ref[...] = out[:, :HEAD]
    kv_ref[...] = out[:, HEAD:]


def project(where, pieces, weights):
    rows = sum(piece.shape[0] for piece in pieces)
    width = pieces[0].shape[1] // 2
    bf16 = lambda *shape: jax.ShapeDtypeStruct(shape, jnp.bfloat16)
    return pl.pallas_call(
        project_kernel,
        out_shape=(
            bf16(rows, HEAD),
            bf16(rows, 2 * HEAD),
            bf16(width, 3 * HEAD),
        ),
        in_specs=[SMEM] + [ANY] * 12,
        out_specs=(VMEM,) * 3,
        scratch_shapes=[
            pltpu.VMEM((rows, width), jnp.bfloat16),
            pltpu.SemaphoreType.DMA((16,)),
        ],
        compiler_params=PARAMS,
    )(where, *pieces, *weights)


def dattended_kernel(*refs):
    place_ref, pieces, mine, theirs = refs[0], refs[1:9], refs[9], refs[10]
    da_ref, rows, weight, sems = refs[11:]
    core = place_ref[3]
    half = mine.shape[0]
    spot = pl.multiple_of(core * half, half)
    other = pl.multiple_of((1 - core) * half, half)
    copies = stacked([piece.at[:, rows.shape[1] :] for piece in pieces], rows)
    copies.append((mine, weight.at[pl.ds(spot, half), :]))
    copies.append((theirs, weight.at[pl.ds(other, half), :]))
    fetched(copies, sems)
    da_ref[...] = contract_last(rows[...], weight[...]).astype(jnp.bfloat16)


def dattended(where, pieces, mine, theirs):
    rows = sum(piece.shape[0] for piece in pieces)
    width = pieces[0].shape[1] // 2
    return pl.pallas_call(
        dattended_kernel,
        out_shape=jax.ShapeDtypeStruct((rows, HEAD), jnp.bfloat16),
        in_specs=[SMEM] + [ANY] * 10,
        out_specs=VMEM,
        scratch_shapes=[
            pltpu.VMEM((rows, width), jnp.bfloat16),
            pltpu.VMEM((HEAD, width), jnp.bfloat16),
            pltpu.SemaphoreType.DMA((10,)),
        ],
        compiler_params=PARAMS,
    )(where, *pieces, mine, theirs)


def attention_kernel(tile, seg, *refs):
    place_ref, q_ref, da_ref, blocks = refs[0], refs[1], refs[2], refs[3:7]
    dq_ref, outs, (kv, dkt, dvt, sems) = refs[7], refs[8:12], refs[12:]
    half, turn, pair, core = place_ref[0], place_ref[1], place_ref[2], place_ref[3]
    queries, keys = q_ref.shape[0], kv.shape[0]
    fetched(stacked(blocks, kv), sems)
    spot = lax.broadcasted_iota(jnp.int32, (1, keys), 1)
    block = spot // queries
    key_half = jnp.where(block < 2, half, 1 - half)
    key_pair = jnp.where(block % 2 == 0, pair, 1 - pair)
    key_at = rows_at(spot % queries, key_half, turn, key_pair, core, seg)
    turn_up = math.log2(math.e) / math.sqrt(HEAD)
    scale = 1.0 / math.sqrt(HEAD)
    k = kv[:, :HEAD]
    v = kv[:, HEAD:]
    for step in range(queries // tile):
        rows = slice(step * tile, (step + 1) * tile)
        query = lax.broadcasted_iota(jnp.int32, (tile, 1), 0) + step * tile
        query_at = rows_at(query, half, turn, pair, core, seg)
        q = q_ref[rows, :]
        da = da_ref[rows, :]
        score = jnp.where(key_at <= query_at, contract_last(q, k), NEG)
        peak = jnp.max(score, axis=1, keepdims=True)
        expo = jnp.exp2((score - peak) * turn_up)
        probs = expo * (1.0 / jnp.sum(expo, axis=1, keepdims=True))
        probs_b = probs.astype(jnp.bfloat16)
        attended = jnp.dot(probs_b, v, preferred_element_type=F32).astype(jnp.bfloat16)
        delta = jnp.sum(da.astype(F32) * attended.astype(F32), axis=1, keepdims=True)
        dscore = (probs * (contract_last(da, v) - delta)).astype(jnp.bfloat16)
        dq = jnp.dot(dscore, k, preferred_element_type=F32) * scale
        dq_ref[rows, :] = dq.astype(jnp.bfloat16)
        dk_part = contract_first(q, dscore)
        dv_part = contract_first(da, probs_b)
        if step == 0:
            dkt[...] = dk_part
            dvt[...] = dv_part
        else:
            dkt[...] += dk_part
            dvt[...] += dv_part
    part = keys // len(outs)
    for i, out in enumerate(outs):
        lanes = slice(i * part, (i + 1) * part)
        out[:, :HEAD] = (dkt[:, lanes] * scale).T.astype(jnp.bfloat16)
        out[:, HEAD:] = dvt[:, lanes].T.astype(jnp.bfloat16)


def attention(where, q, da, blocks, seg):
    queries = q.shape[0]
    keys = sum(block.shape[0] for block in blocks)
    part = jax.ShapeDtypeStruct(blocks[0].shape, jnp.bfloat16)
    return pl.pallas_call(
        functools.partial(attention_kernel, 128, seg),
        out_shape=(jax.ShapeDtypeStruct((queries, HEAD), jnp.bfloat16),) + (part,) * 4,
        in_specs=[SMEM] + [VMEM] * 2 + [ANY] * 4,
        out_specs=(VMEM,) * 5,
        scratch_shapes=[
            pltpu.VMEM((keys, 2 * HEAD), jnp.bfloat16),
            pltpu.VMEM((HEAD, keys), F32),
            pltpu.VMEM((HEAD, keys), F32),
            pltpu.SemaphoreType.DMA((4,)),
        ],
        compiler_params=PARAMS,
        cost_estimate=pl.CostEstimate(
            flops=12 * queries * keys * HEAD,
            bytes_accessed=2 * HEAD * (3 * queries + 4 * keys),
            transcendentals=queries * keys,
        ),
    )(where, q, da, *blocks)


def unproject_kernel(seg, dq_ref, *refs):
    parts, w_ref, swap_ref, outs = refs[:4], refs[4], refs[5], refs[6:]
    dkv = sum(ref[...].astype(F32) for ref in parts).astype(jnp.bfloat16)
    left = jnp.concatenate([dq_ref[...], dkv], axis=1)
    out = contract_last(left, w_ref[...])
    for i, slot in enumerate((1, 4, 5, 7)):
        swap_ref[i * seg : (i + 1) * seg, :] = out[slot * seg : (slot + 1) * seg].astype(WIRE)
    for ref, slot in zip(outs, (0, 2, 3, 6)):
        ref[...] = out[slot * seg : (slot + 1) * seg]


def unproject(dq, parts, w_full, seg):
    width = w_full.shape[0]
    return pl.pallas_call(
        functools.partial(unproject_kernel, seg),
        out_shape=(jax.ShapeDtypeStruct((4 * seg, width), WIRE),)
        + (jax.ShapeDtypeStruct((seg, width), F32),) * 4,
        in_specs=[VMEM] * 6,
        out_specs=(VMEM,) * 5,
        compiler_params=PARAMS,
    )(dq, *parts, w_full)


def join_kernel(swapped, own, near, next_to, far, own_out, near_out, next_out, far_out):
    seg = own.shape[0]
    own_out[...] = own[...] + swapped[:seg, :].astype(F32)
    near_out[...] = near[...] + swapped[seg : 2 * seg, :].astype(F32)
    next_out[...] = (next_to[...] + swapped[2 * seg : 3 * seg, :].astype(F32)).astype(WIRE)
    far_out[...] = (far[...] + swapped[3 * seg :, :].astype(F32)).astype(WIRE)


def joined(swapped, own, near, next_to, far):
    wide = jax.ShapeDtypeStruct(own.shape, F32)
    thin = jax.ShapeDtypeStruct(own.shape, WIRE)
    return pl.pallas_call(
        join_kernel,
        out_shape=(wide, wide, thin, thin),
        in_specs=[VMEM] * 5,
        out_specs=(VMEM,) * 4,
        compiler_params=PARAMS,
    )(swapped, own, near, next_to, far)


def summed_rows(swap, own, near, next_to, far):
    own, near, next_to, far = joined(other_core(swap), own, near, next_to, far)
    far = turned(far, -1).astype(F32)
    next_to = turned_over(next_to).astype(F32)
    near = turned((near + far).astype(WIRE), -1).astype(F32)
    return own + next_to + near


def per_device(tokens, starts, gain, w_query, w_key, w_value, w_out, cotangent):
    token_rows = tokens[0]
    grad_out = cotangent[0]
    rows, width = token_rows.shape
    seg = starts.shape[1]
    length = rows * CTX
    ctx = lax.axis_index("ctx")
    core, pair = ctx % CORES, ctx // CORES % PAIR
    turn, half = ctx // (CORES * PAIR) % TURNS, ctx // (CORES * PAIR * TURNS)
    where = jnp.stack([half, turn, pair, core, lax.axis_index("dp"), ctx])

    mine, own_starts = columns_in(w_query, w_key, w_value, starts, turn * CORES + core)
    own_starts = own_starts[0]
    theirs = other_x(mine)
    beside, facing = other_core(own_starts), other_chip(own_starts)
    before = jnp.where(core == 0, facing, beside)
    after = jnp.where(core == 0, beside, facing)
    before = jnp.where(ctx == 0, -1, before)
    after = jnp.where(ctx == CTX - 1, length, after)
    stop = jnp.full((2,), length, jnp.int32)
    window = jnp.concatenate([before, own_starts, after, stop])
    slots = 3 * seg
    opens, ends = window[:slots], window[1 : slots + 1]
    edges = jnp.stack([opens, ends, window[2:]])[:, :, None]
    count = (ends - opens)[seg : 2 * seg, None].astype(F32)
    to_core, to_chip, mid_token, mid_grad, first, both = window_sums(
        where, edges, token_rows, grad_out, mine, theirs, seg
    )
    weights = [both, shifted_y(both, 1), shifted_y(both, -1), shifted_y(both, 2)]
    second = two_back(first)
    both, normed, rms, dout, out_half = norm(
        where,
        other_core(to_core),
        other_chip(to_chip),
        mid_token,
        mid_grad,
        second,
        count,
        gain[None],
        w_out,
        weights[1:3],
    )
    pieces = gathered_rows(both, weights[3])
    q, own, w_full = project(where, pieces, weights)
    cross, far, beside = across(own, 0, True), across(own, 0, False), other_pair(own)
    out_mine, out_theirs = rows_out(out_half, turn, core)
    da = dattended(where, pieces, out_mine, out_theirs)
    dq, own, beside, far, cross = attention(where, q, da, (own, beside, far, cross), seg)
    parts = (own, other_pair(beside), across(far, 1, False), across(cross, 1, True))
    dnormin = summed_rows(*unproject(dq, parts, w_full, seg))

    scaled = dnormin * gain
    dpooled = dout + (scaled - normed * jnp.mean(scaled * normed, axis=-1, keepdims=True)) / rms
    per_seg = (dpooled / count).astype(WIRE)
    beside, facing = other_core(per_seg), other_chip(per_seg)
    before = jnp.where(core == 0, facing, beside)
    after = jnp.where(core == 0, beside, facing)
    per_window = jnp.concatenate([before, per_seg, after], axis=0)
    positions = (ctx * rows + lax.iota(jnp.int32, rows))[:, None]
    member = (opens[None] <= positions) & (positions < ends[None])
    spread = jnp.dot(member.astype(WIRE), per_window, preferred_element_type=F32)
    return (grad_out.astype(F32) + spread).astype(jnp.bfloat16)[None]


def solution(mesh):
    return jax.shard_map(
        per_device,
        mesh=mesh,
        in_specs=(
            P("dp", "ctx", None),
            P("dp", "ctx"),
            P(),
            P("dp", None),
            P("dp", None),
            P("dp", None),
            P("dp", None),
            P("dp", "ctx", None),
        ),
        out_specs=P("dp", "ctx", None),
        check_vma=False,
    )
```

```python
import functools
import math

import jax
import jax.numpy as jnp
from jax import lax
from jax.experimental import pallas as pl
from jax.experimental.pallas import tpu as pltpu
from jax.sharding import PartitionSpec as P

HEAD = 128
HALVES, TURNS, PAIR, CORES = 2, 4, 2, 2
CTX = HALVES * TURNS * PAIR * CORES
NEG = -1e30
WIRE = jnp.bfloat16
F32 = jnp.float32
VMEM = pl.BlockSpec(memory_space=pltpu.VMEM)
SMEM = pl.BlockSpec(memory_space=pltpu.SMEM)
ANY = pl.BlockSpec(memory_space=pl.ANY)
PARAMS = pltpu.CompilerParams(vmem_limit_bytes=48 * 1024 * 1024)


def place(half, turn, pair, core):
    return ((half * TURNS + turn % TURNS) * PAIR + pair) * CORES + core


def moved(value, to):
    spots = [
        (h, t, p, k)
        for h in range(HALVES)
        for t in range(TURNS)
        for p in range(PAIR)
        for k in range(CORES)
    ]
    pairs = [(place(*s), place(*to(*s))) for s in spots if to(*s) is not None]
    return lax.ppermute(value, "ctx", pairs)


def other_chip(value):
    pairs = [(i, i + 1 if i % CORES else i - 1) for i in range(1, CTX - 1)]
    return lax.ppermute(value, "ctx", pairs)


def two_back(value):
    return lax.ppermute(value, "ctx", [(i, i - CORES) for i in range(CORES, CTX)])


def other_core(value):
    return moved(value, lambda h, t, p, k: (h, t, p, 1 - k))


def other_pair(value):
    return moved(value, lambda h, t, p, k: (h, t, 1 - p, k))


def across(value, source, cross):
    return moved(
        value,
        lambda h, t, p, k: (1 - h, t, 1 - p if cross else p, k) if h == source else None,
    )


def turned(value, way):
    return moved(value, lambda h, t, p, k: (h, t + way * (1 - 2 * k), p, k))


def turned_over(value):
    return moved(value, lambda h, t, p, k: (h, t - (1 - 2 * k), p, 1 - k))


def contract_last(left, right):
    return lax.dot_general(left, right, (((1,), (1,)), ((), ())), preferred_element_type=F32)


def contract_first(left, right):
    return lax.dot_general(left, right, (((0,), (0,)), ((), ())), preferred_element_type=F32)


def cut_kernel(place_ref, q_ref, k_ref, v_ref, o_ref, start_ref, out_ref, start_out, sems):
    rows = out_ref.shape[0]
    half, width = rows // CORES, o_ref.shape[1]
    core = place_ref[3]
    lane = pl.multiple_of((place_ref[1] * CORES + core) * HEAD, HEAD)
    copies = [
        (w.at[:, pl.ds(lane, HEAD)], out_ref.at[:, i * HEAD : (i + 1) * HEAD])
        for i, w in enumerate((q_ref, k_ref, v_ref))
    ]
    at = pl.multiple_of(core * half, half)
    for i in range(2):
        lanes = slice(i * width // 2, (i + 1) * width // 2)
        copies.append(
            (o_ref.at[pl.ds(at, half), lanes], out_ref.at[i * half : (i + 1) * half, 3 * HEAD :])
        )
    copies.append((start_ref, start_out))
    fetched(copies, sems)


def cut_weights(where, w_query, w_key, w_value, w_out, starts):
    rows, width = w_out.shape
    return pl.pallas_call(
        cut_kernel,
        out_shape=(
            jax.ShapeDtypeStruct((rows, 3 * HEAD + width // 2), w_query.dtype),
            jax.ShapeDtypeStruct(starts.shape, starts.dtype),
        ),
        in_specs=[SMEM] + [ANY] * 5,
        out_specs=(VMEM, VMEM),
        scratch_shapes=[pltpu.SemaphoreType.DMA((6,))],
        compiler_params=PARAMS,
    )(where, w_query, w_key, w_value, w_out, starts)


def gathered_weights(mine):
    return lax.all_gather(mine, "dp", axis=0, tiled=False)


def rows_out(weights, turn, core):
    rows = weights[:, :, 3 * HEAD :]
    mine = lax.dynamic_index_in_dim(rows, turn * CORES + core, 0, keepdims=False)
    theirs = lax.dynamic_index_in_dim(rows, turn * CORES + 1 - core, 0, keepdims=False)
    return mine, other_core(theirs)


def gathered_rows(shard):
    near = turned(shard, 1)
    next_to = turned_over(shard)
    far = turned(near, 1)
    return [
        shard,
        other_core(shard),
        near,
        next_to,
        other_core(near),
        other_core(next_to),
        far,
        other_core(far),
    ]


def rows_at(row, half, turn, pair, core, seg):
    slot = row // seg
    two = slot // 2
    way = 1 - 2 * core
    step = jnp.where(two == 0, 0, jnp.where(two == 1, way, jnp.where(two == 2, -way, 2)))
    flip = jnp.where(two == 2, 1 - slot % 2, slot % 2)
    its_core = jnp.where(flip == 1, 1 - core, core)
    its_turn = (turn - step + TURNS) % TURNS
    return place(half, its_turn, pair, its_core) * seg + row % seg


def fetched(copies, sems):
    started = []
    for i, (source, target) in enumerate(copies):
        started.append(pltpu.make_async_copy(source, target, sems.at[i]))
        started[-1].start()
    for copy in started:
        copy.wait()


def stacked(pieces, out_ref):
    copies, at = [], 0
    for piece in pieces:
        copies.append((piece, out_ref.at[at : at + piece.shape[0], :]))
        at += piece.shape[0]
    return copies


def window_kernel(place_ref, edge_ref, token_hbm, grad_hbm, *refs):
    core_ref, chip_ref, mid_token, mid_grad, first_ref = refs[:5]
    token_ref, grad_ref, sems = refs[5:]
    rows, width = token_ref.shape
    seg = mid_token.shape[0]
    fetched([(token_hbm, token_ref), (grad_hbm, grad_ref)], sems)
    ctx, core = place_ref[5], place_ref[3]
    at = lax.broadcasted_iota(jnp.int32, (1, rows), 1) + ctx * rows
    opens, ends, nexts = edge_ref[0], edge_ref[1], edge_ref[2]
    member = ((opens <= at) & (at < ends)).astype(jnp.bfloat16)
    earlier = ((ends <= at) & (at < nexts)).astype(jnp.bfloat16)
    token = jnp.dot(member, token_ref[...], preferred_element_type=F32)
    grad = jnp.dot(earlier, grad_ref[...], preferred_element_type=F32)
    first = jnp.dot(member[:16], grad_ref[...], preferred_element_type=F32)
    first_ref[...] = first[:1]
    mid_token[...] = token[seg : 2 * seg]
    mid_grad[...] = grad[seg : 2 * seg]

    def send(lower_ref, upper_ref):
        lower_ref[:, :width] = token[:seg].astype(WIRE)
        lower_ref[:, width:] = grad[:seg].astype(WIRE)
        upper_ref[:, :width] = token[2 * seg :].astype(WIRE)
        upper_ref[:, width:] = grad[2 * seg :].astype(WIRE)

    @pl.when(core == 0)
    def _():
        send(chip_ref, core_ref)

    @pl.when(core == 1)
    def _():
        send(core_ref, chip_ref)


def window_sums(where, edges, tokens, grads, seg):
    rows, width = tokens.shape
    shape = jax.ShapeDtypeStruct
    return pl.pallas_call(
        window_kernel,
        out_shape=(
            shape((seg, 2 * width), WIRE),
            shape((seg, 2 * width), WIRE),
            shape((seg, width), F32),
            shape((seg, width), F32),
            shape((1, width), F32),
        ),
        in_specs=[SMEM, VMEM] + [ANY] * 2,
        out_specs=(VMEM,) * 5,
        scratch_shapes=[
            pltpu.VMEM((rows, width), tokens.dtype),
            pltpu.VMEM((rows, width), grads.dtype),
            pltpu.SemaphoreType.DMA((2,)),
        ],
        compiler_params=PARAMS,
    )(where, edges, tokens, grads)


def norm_kernel(core_ref, chip_ref, mid_token, mid_grad, count_ref, gain_ref, *outs):
    normin_ref, normed_ref, rms_ref, dout_ref = outs
    width = mid_token.shape[1]
    got = core_ref[...].astype(F32) + chip_ref[...].astype(F32)
    pooled = (mid_token[...] + got[:, :width]) / count_ref[...]
    rms = jnp.sqrt(jnp.mean(pooled * pooled, axis=1, keepdims=True) + 1e-06)
    normed = pooled / rms
    normed_ref[...] = normed
    rms_ref[...] = rms
    normin_ref[...] = (normed * gain_ref[...]).astype(jnp.bfloat16)
    dout_ref[...] = mid_grad[...] + got[:, width:]


def norm(from_core, from_chip, mid_token, mid_grad, count, gain):
    seg, width = mid_token.shape
    shape = jax.ShapeDtypeStruct
    return pl.pallas_call(
        norm_kernel,
        out_shape=(
            shape((seg, width), jnp.bfloat16),
            shape((seg, width), F32),
            shape((seg, 1), F32),
            shape((seg, width), F32),
        ),
        in_specs=[VMEM] * 6,
        out_specs=(VMEM,) * 4,
        compiler_params=PARAMS,
    )(from_core, from_chip, mid_token, mid_grad, count, gain)


def dout_kernel(dout_ref, second_ref, ready_ref, full_ref, half_ref):
    seg = dout_ref.shape[0]
    last = lax.broadcasted_iota(jnp.int32, (seg, 1), 0) == seg - 1
    dout = dout_ref[...] + jnp.where(last, second_ref[...], 0.0)
    full_ref[...] = dout
    half_ref[...] = dout.astype(jnp.bfloat16)


def whole_dout(dout, second, ready):
    shape = jax.ShapeDtypeStruct
    return pl.pallas_call(
        dout_kernel,
        out_shape=(shape(dout.shape, F32), shape(dout.shape, jnp.bfloat16)),
        in_specs=[VMEM, VMEM, ANY],
        out_specs=(VMEM, VMEM),
        compiler_params=PARAMS,
    )(dout, second, ready)


def project_kernel(*refs):
    pieces, weight = refs[:8], refs[8]
    q_ref, kv_ref, w_ref, rows, sems = refs[9:]
    copies = stacked(pieces, rows)
    depth = weight.shape[1]
    for i in range(weight.shape[0]):
        copies.append((weight.at[i, :, : 3 * HEAD], w_ref.at[i * depth : (i + 1) * depth, :]))
    fetched(copies, sems)
    out = jnp.dot(rows[...], w_ref[...], preferred_element_type=F32).astype(jnp.bfloat16)
    q_ref[...] = out[:, :HEAD]
    kv_ref[...] = out[:, HEAD:]


def project(pieces, weights):
    rows = sum(piece.shape[0] for piece in pieces)
    width = pieces[0].shape[1]
    bf16 = lambda *shape: jax.ShapeDtypeStruct(shape, jnp.bfloat16)
    return pl.pallas_call(
        project_kernel,
        out_shape=(
            bf16(rows, HEAD),
            bf16(rows, 2 * HEAD),
            bf16(width, 3 * HEAD),
        ),
        in_specs=[ANY] * 9,
        out_specs=(VMEM,) * 3,
        scratch_shapes=[
            pltpu.VMEM((rows, width), jnp.bfloat16),
            pltpu.SemaphoreType.DMA((16,)),
        ],
        compiler_params=PARAMS,
    )(*pieces, weights)


def dattended_kernel(*refs):
    place_ref, pieces, mine, theirs = refs[0], refs[1:9], refs[9], refs[10]
    da_ref, rows, weight, sems = refs[11:]
    core = place_ref[3]
    half, wide = mine.shape[0] // 2, mine.shape[1]
    spot = pl.multiple_of(core * half, half)
    other = pl.multiple_of((1 - core) * half, half)
    copies = stacked(pieces, rows)
    for i in range(2):
        part, lanes = slice(i * half, (i + 1) * half), slice(i * wide, (i + 1) * wide)
        copies.append((mine.at[part, :], weight.at[pl.ds(spot, half), lanes]))
        copies.append((theirs.at[part, :], weight.at[pl.ds(other, half), lanes]))
    fetched(copies, sems)
    da_ref[...] = contract_last(rows[...], weight[...]).astype(jnp.bfloat16)


def dattended(where, pieces, mine, theirs):
    rows = sum(piece.shape[0] for piece in pieces)
    width = pieces[0].shape[1]
    return pl.pallas_call(
        dattended_kernel,
        out_shape=jax.ShapeDtypeStruct((rows, HEAD), jnp.bfloat16),
        in_specs=[SMEM] + [ANY] * 10,
        out_specs=VMEM,
        scratch_shapes=[
            pltpu.VMEM((rows, width), jnp.bfloat16),
            pltpu.VMEM((HEAD, width), jnp.bfloat16),
            pltpu.SemaphoreType.DMA((12,)),
        ],
        compiler_params=PARAMS,
    )(where, *pieces, mine, theirs)


def attention_kernel(tile, seg, *refs):
    place_ref, q_ref, da_ref, blocks = refs[0], refs[1], refs[2], refs[3:7]
    dq_ref, outs, (kv, dkt, dvt, sems) = refs[7], refs[8:12], refs[12:]
    half, turn, pair, core = place_ref[0], place_ref[1], place_ref[2], place_ref[3]
    queries, keys = q_ref.shape[0], kv.shape[0]
    fetched(stacked(blocks, kv), sems)
    spot = lax.broadcasted_iota(jnp.int32, (1, keys), 1)
    block = spot // queries
    key_half = jnp.where(block < 2, half, 1 - half)
    key_pair = jnp.where(block % 2 == 0, pair, 1 - pair)
    key_at = rows_at(spot % queries, key_half, turn, key_pair, core, seg)
    turn_up = math.log2(math.e) / math.sqrt(HEAD)
    scale = 1.0 / math.sqrt(HEAD)
    k = kv[:, :HEAD]
    v = kv[:, HEAD:]
    for step in range(queries // tile):
        rows = slice(step * tile, (step + 1) * tile)
        query = lax.broadcasted_iota(jnp.int32, (tile, 1), 0) + step * tile
        query_at = rows_at(query, half, turn, pair, core, seg)
        q = q_ref[rows, :]
        da = da_ref[rows, :]
        score = jnp.where(key_at <= query_at, contract_last(q, k), NEG)
        peak = jnp.max(score, axis=1, keepdims=True)
        expo = jnp.exp2((score - peak) * turn_up)
        probs = expo * (1.0 / jnp.sum(expo, axis=1, keepdims=True))
        probs_b = probs.astype(jnp.bfloat16)
        attended = jnp.dot(probs_b, v, preferred_element_type=F32).astype(jnp.bfloat16)
        delta = jnp.sum(da.astype(F32) * attended.astype(F32), axis=1, keepdims=True)
        dscore = (probs * (contract_last(da, v) - delta)).astype(jnp.bfloat16)
        dq = jnp.dot(dscore, k, preferred_element_type=F32) * scale
        dq_ref[rows, :] = dq.astype(jnp.bfloat16)
        dk_part = contract_first(q, dscore)
        dv_part = contract_first(da, probs_b)
        if step == 0:
            dkt[...] = dk_part
            dvt[...] = dv_part
        else:
            dkt[...] += dk_part
            dvt[...] += dv_part
    part = keys // len(outs)
    for i, out in enumerate(outs):
        lanes = slice(i * part, (i + 1) * part)
        out[:, :HEAD] = (dkt[:, lanes] * scale).T.astype(jnp.bfloat16)
        out[:, HEAD:] = dvt[:, lanes].T.astype(jnp.bfloat16)


def attention(where, q, da, blocks, seg):
    queries = q.shape[0]
    keys = sum(block.shape[0] for block in blocks)
    part = jax.ShapeDtypeStruct(blocks[0].shape, jnp.bfloat16)
    return pl.pallas_call(
        functools.partial(attention_kernel, 128, seg),
        out_shape=(jax.ShapeDtypeStruct((queries, HEAD), jnp.bfloat16),) + (part,) * 4,
        in_specs=[SMEM] + [VMEM] * 2 + [ANY] * 4,
        out_specs=(VMEM,) * 5,
        scratch_shapes=[
            pltpu.VMEM((keys, 2 * HEAD), jnp.bfloat16),
            pltpu.VMEM((HEAD, keys), F32),
            pltpu.VMEM((HEAD, keys), F32),
            pltpu.SemaphoreType.DMA((4,)),
        ],
        compiler_params=PARAMS,
        cost_estimate=pl.CostEstimate(
            flops=12 * queries * keys * HEAD,
            bytes_accessed=2 * HEAD * (3 * queries + 4 * keys),
            transcendentals=queries * keys,
        ),
    )(where, q, da, *blocks)


def unproject_kernel(seg, dq_ref, *refs):
    parts, w_ref, swap_ref, outs = refs[:4], refs[4], refs[5], refs[6:]
    dkv = sum(ref[...].astype(F32) for ref in parts).astype(jnp.bfloat16)
    left = jnp.concatenate([dq_ref[...], dkv], axis=1)
    out = contract_last(left, w_ref[...])
    for i, slot in enumerate((1, 4, 5, 7)):
        swap_ref[i * seg : (i + 1) * seg, :] = out[slot * seg : (slot + 1) * seg].astype(WIRE)
    for ref, slot in zip(outs, (0, 2, 3, 6)):
        ref[...] = out[slot * seg : (slot + 1) * seg]


def unproject(dq, parts, w_full, seg):
    width = w_full.shape[0]
    return pl.pallas_call(
        functools.partial(unproject_kernel, seg),
        out_shape=(jax.ShapeDtypeStruct((4 * seg, width), WIRE),)
        + (jax.ShapeDtypeStruct((seg, width), F32),) * 4,
        in_specs=[VMEM] * 6,
        out_specs=(VMEM,) * 5,
        compiler_params=PARAMS,
    )(dq, *parts, w_full)


def join_kernel(swapped, own, near, next_to, far, own_out, near_out, next_out, far_out):
    seg = own.shape[0]
    own_out[...] = own[...] + swapped[:seg, :].astype(F32)
    near_out[...] = near[...] + swapped[seg : 2 * seg, :].astype(F32)
    next_out[...] = (next_to[...] + swapped[2 * seg : 3 * seg, :].astype(F32)).astype(WIRE)
    far_out[...] = (far[...] + swapped[3 * seg :, :].astype(F32)).astype(WIRE)


def joined(swapped, own, near, next_to, far):
    wide = jax.ShapeDtypeStruct(own.shape, F32)
    thin = jax.ShapeDtypeStruct(own.shape, WIRE)
    return pl.pallas_call(
        join_kernel,
        out_shape=(wide, wide, thin, thin),
        in_specs=[VMEM] * 5,
        out_specs=(VMEM,) * 4,
        compiler_params=PARAMS,
    )(swapped, own, near, next_to, far)


def summed_rows(swap, own, near, next_to, far):
    own, near, next_to, far = joined(other_core(swap), own, near, next_to, far)
    far = turned(far, -1).astype(F32)
    next_to = turned_over(next_to).astype(F32)
    near = turned((near + far).astype(WIRE), -1).astype(F32)
    return own + next_to + near


def per_device(tokens, starts, gain, w_query, w_key, w_value, w_out, cotangent):
    token_rows = tokens[0]
    grad_out = cotangent[0]
    rows, width = token_rows.shape
    seg = starts.shape[1]
    length = rows * CTX
    ctx = lax.axis_index("ctx")
    core, pair = ctx % CORES, ctx // CORES % PAIR
    turn, half = ctx // (CORES * PAIR) % TURNS, ctx // (CORES * PAIR * TURNS)
    where = jnp.stack([half, turn, pair, core, lax.axis_index("dp"), ctx])

    mine, own_starts = cut_weights(where, w_query, w_key, w_value, w_out, starts)
    own_starts = own_starts[0]
    weights = gathered_weights(mine)
    beside, facing = other_core(own_starts), other_chip(own_starts)
    before = jnp.where(core == 0, facing, beside)
    after = jnp.where(core == 0, beside, facing)
    before = jnp.where(ctx == 0, -1, before)
    after = jnp.where(ctx == CTX - 1, length, after)
    stop = jnp.full((2,), length, jnp.int32)
    window = jnp.concatenate([before, own_starts, after, stop])
    slots = 3 * seg
    opens, ends = window[:slots], window[1 : slots + 1]
    edges = jnp.stack([opens, ends, window[2:]])[:, :, None]
    count = (ends - opens)[seg : 2 * seg, None].astype(F32)
    to_core, to_chip, mid_token, mid_grad, first = window_sums(
        where, edges, token_rows, grad_out, seg
    )
    second = two_back(first)
    normin, normed, rms, dout = norm(
        other_core(to_core), other_chip(to_chip), mid_token, mid_grad, count, gain[None]
    )
    pieces = gathered_rows(normin)
    q, own, w_full = project(pieces, weights)
    dout, dout_b = whole_dout(dout, second, pieces[2])
    cross, far, beside = across(own, 0, True), across(own, 0, False), other_pair(own)
    out_mine, out_theirs = rows_out(weights, turn, core)
    da = dattended(where, gathered_rows(dout_b), out_mine, out_theirs)
    dq, own, beside, far, cross = attention(where, q, da, (own, beside, far, cross), seg)
    parts = (own, other_pair(beside), across(far, 1, False), across(cross, 1, True))
    dnormin = summed_rows(*unproject(dq, parts, w_full, seg))

    scaled = dnormin * gain
    dpooled = dout + (scaled - normed * jnp.mean(scaled * normed, axis=-1, keepdims=True)) / rms
    per_seg = (dpooled / count).astype(WIRE)
    beside, facing = other_core(per_seg), other_chip(per_seg)
    before = jnp.where(core == 0, facing, beside)
    after = jnp.where(core == 0, beside, facing)
    per_window = jnp.concatenate([before, per_seg, after], axis=0)
    positions = (ctx * rows + lax.iota(jnp.int32, rows))[:, None]
    member = (opens[None] <= positions) & (positions < ends[None])
    spread = jnp.dot(member.astype(WIRE), per_window, preferred_element_type=F32)
    return (grad_out.astype(F32) + spread).astype(jnp.bfloat16)[None]


def solution(mesh):
    return jax.shard_map(
        per_device,
        mesh=mesh,
        in_specs=(
            P("dp", "ctx", None),
            P("dp", "ctx"),
            P(),
            P("dp", None),
            P("dp", None),
            P("dp", None),
            P("dp", None),
            P("dp", "ctx", None),
        ),
        out_specs=P("dp", "ctx", None),
        check_vma=False,
    )
```

```python
import functools
import math

import jax
import jax.numpy as jnp
from jax import lax
from jax.experimental import pallas as pl
from jax.experimental.pallas import tpu as pltpu
from jax.sharding import PartitionSpec as P

HEAD = 128
HALVES, TURNS, PAIR, CORES = 2, 4, 2, 2
CTX = HALVES * TURNS * PAIR * CORES
NEG = -1e30
WIRE = jnp.bfloat16
F32 = jnp.float32
VMEM = pl.BlockSpec(memory_space=pltpu.VMEM)
SMEM = pl.BlockSpec(memory_space=pltpu.SMEM)
ANY = pl.BlockSpec(memory_space=pl.ANY)
HBM = pl.BlockSpec(memory_space=pltpu.HBM)


def room(mib):
    return pltpu.CompilerParams(vmem_limit_bytes=mib * 1024 * 1024)


def place(half, turn, pair, core):
    return ((half * TURNS + turn % TURNS) * PAIR + pair) * CORES + core


def moved(value, to):
    spots = [
        (h, t, p, k)
        for h in range(HALVES)
        for t in range(TURNS)
        for p in range(PAIR)
        for k in range(CORES)
    ]
    pairs = [(place(*s), place(*to(*s))) for s in spots if to(*s) is not None]
    return lax.ppermute(value, "ctx", pairs)


def other_chip(value):
    pairs = [(i, i + 1 if i % CORES else i - 1) for i in range(1, CTX - 1)]
    return lax.ppermute(value, "ctx", pairs)


def two_back(value):
    return lax.ppermute(value, "ctx", [(i, i - CORES) for i in range(CORES, CTX)])


def other_core(value):
    return moved(value, lambda h, t, p, k: (h, t, p, 1 - k))


def other_pair(value):
    return moved(value, lambda h, t, p, k: (h, t, 1 - p, k))


def across(value, source, cross):
    return moved(
        value,
        lambda h, t, p, k: (1 - h, t, 1 - p if cross else p, k) if h == source else None,
    )


def turned(value, way):
    return moved(value, lambda h, t, p, k: (h, t + way * (1 - 2 * k), p, k))


def turned_over(value):
    return moved(value, lambda h, t, p, k: (h, t - (1 - 2 * k), p, 1 - k))


def contract_last(left, right):
    return lax.dot_general(left, right, (((1,), (1,)), ((), ())), preferred_element_type=F32)


def contract_first(left, right):
    return lax.dot_general(left, right, (((0,), (0,)), ((), ())), preferred_element_type=F32)


def cut_kernel(place_ref, q_ref, k_ref, v_ref, o_ref, start_ref, out_ref, start_out, sems):
    rows = out_ref.shape[0]
    half, width = rows // CORES, o_ref.shape[1]
    core = place_ref[3]
    lane = pl.multiple_of((place_ref[1] * CORES + core) * HEAD, HEAD)
    copies = [
        (w.at[:, pl.ds(lane, HEAD)], out_ref.at[:, i * HEAD : (i + 1) * HEAD])
        for i, w in enumerate((q_ref, k_ref, v_ref))
    ]
    at = pl.multiple_of(core * half, half)
    for i in range(2):
        lanes = slice(i * width // 2, (i + 1) * width // 2)
        copies.append(
            (o_ref.at[pl.ds(at, half), lanes], out_ref.at[i * half : (i + 1) * half, 3 * HEAD :])
        )
    copies.append((start_ref, start_out))
    fetched(copies, sems)


def cut_weights(where, w_query, w_key, w_value, w_out, starts):
    rows, width = w_out.shape
    return pl.pallas_call(
        cut_kernel,
        out_shape=(
            jax.ShapeDtypeStruct((rows, 3 * HEAD + width // 2), w_query.dtype),
            jax.ShapeDtypeStruct(starts.shape, starts.dtype),
        ),
        in_specs=[SMEM] + [HBM] * 4 + [ANY],
        out_specs=(VMEM, VMEM),
        scratch_shapes=[pltpu.SemaphoreType.DMA((6,))],
        compiler_params=room(60),
    )(where, w_query, w_key, w_value, w_out, starts)


def gathered_weights(mine):
    return lax.all_gather(mine, "dp", axis=0, tiled=False)


def rows_out(weights, turn, core):
    rows = weights[:, :, 3 * HEAD :]
    mine = lax.dynamic_index_in_dim(rows, turn * CORES + core, 0, keepdims=False)
    theirs = lax.dynamic_index_in_dim(rows, turn * CORES + 1 - core, 0, keepdims=False)
    return mine, other_core(theirs)


def gathered_rows(shard):
    near = turned(shard, 1)
    next_to = turned_over(shard)
    far = turned(near, 1)
    return [
        shard,
        other_core(shard),
        near,
        next_to,
        other_core(near),
        other_core(next_to),
        far,
        other_core(far),
    ]


def rows_at(row, half, turn, pair, core, seg):
    slot = row // seg
    two = slot // 2
    way = 1 - 2 * core
    step = jnp.where(two == 0, 0, jnp.where(two == 1, way, jnp.where(two == 2, -way, 2)))
    flip = jnp.where(two == 2, 1 - slot % 2, slot % 2)
    its_core = jnp.where(flip == 1, 1 - core, core)
    its_turn = (turn - step + TURNS) % TURNS
    return place(half, its_turn, pair, its_core) * seg + row % seg


def fetched(copies, sems):
    started = []
    for i, (source, target) in enumerate(copies):
        started.append(pltpu.make_async_copy(source, target, sems.at[i]))
        started[-1].start()
    for copy in started:
        copy.wait()


def stacked(pieces, out_ref):
    copies, at = [], 0
    for piece in pieces:
        copies.append((piece, out_ref.at[at : at + piece.shape[0], :]))
        at += piece.shape[0]
    return copies


def window_kernel(place_ref, edge_ref, token_hbm, grad_hbm, *refs):
    core_ref, chip_ref, mid_token, mid_grad, first_ref, count_ref = refs[:6]
    token_ref, grad_ref, sems = refs[6:]
    rows, width = token_ref.shape
    seg = mid_token.shape[0]
    token_copy = pltpu.make_async_copy(token_hbm, token_ref, sems.at[0])
    grad_copy = pltpu.make_async_copy(grad_hbm, grad_ref, sems.at[1])
    token_copy.start()
    grad_copy.start()
    ctx, core = place_ref[5], place_ref[3]
    at = lax.broadcasted_iota(jnp.int32, (1, rows), 1) + ctx * rows
    opens, ends, nexts = edge_ref[0], edge_ref[1], edge_ref[2]
    count_ref[...] = (ends - opens)[seg : 2 * seg].astype(F32)
    member = ((opens <= at) & (at < ends)).astype(jnp.bfloat16)
    earlier = ((ends <= at) & (at < nexts)).astype(jnp.bfloat16)
    token_copy.wait()
    token = jnp.dot(member, token_ref[...], preferred_element_type=F32)
    grad_copy.wait()
    grad = jnp.dot(earlier, grad_ref[...], preferred_element_type=F32)
    first = jnp.dot(member[:16], grad_ref[...], preferred_element_type=F32)
    first_ref[...] = first[:1]
    mid_token[...] = token[seg : 2 * seg]
    mid_grad[...] = grad[seg : 2 * seg]

    def send(lower_ref, upper_ref):
        lower_ref[:, :width] = token[:seg].astype(WIRE)
        lower_ref[:, width:] = grad[:seg].astype(WIRE)
        upper_ref[:, :width] = token[2 * seg :].astype(WIRE)
        upper_ref[:, width:] = grad[2 * seg :].astype(WIRE)

    @pl.when(core == 0)
    def _():
        send(chip_ref, core_ref)

    @pl.when(core == 1)
    def _():
        send(core_ref, chip_ref)


def window_sums(where, edges, tokens, grads, seg):
    rows, width = tokens.shape
    shape = jax.ShapeDtypeStruct
    return pl.pallas_call(
        window_kernel,
        out_shape=(
            shape((seg, 2 * width), WIRE),
            shape((seg, 2 * width), WIRE),
            shape((seg, width), F32),
            shape((seg, width), F32),
            shape((1, width), F32),
            shape((seg, 1), F32),
        ),
        in_specs=[SMEM, VMEM] + [HBM] * 2,
        out_specs=(VMEM,) * 6,
        scratch_shapes=[
            pltpu.VMEM((rows, width), tokens.dtype),
            pltpu.VMEM((rows, width), grads.dtype),
            pltpu.SemaphoreType.DMA((2,)),
        ],
        compiler_params=room(60),
    )(where, edges, tokens, grads)


def norm_kernel(core_ref, chip_ref, mid_token, mid_grad, count_ref, gain_ref, *outs):
    normin_ref, normed_ref, rms_ref, dout_ref = outs
    width = mid_token.shape[1]
    got = core_ref[...].astype(F32) + chip_ref[...].astype(F32)
    pooled = (mid_token[...] + got[:, :width]) / count_ref[...]
    rms = jnp.sqrt(jnp.mean(pooled * pooled, axis=1, keepdims=True) + 1e-06)
    normed = pooled / rms
    normed_ref[...] = normed
    rms_ref[...] = rms
    normin_ref[...] = (normed * gain_ref[...]).astype(jnp.bfloat16)
    dout_ref[...] = mid_grad[...] + got[:, width:]


def norm(from_core, from_chip, mid_token, mid_grad, count, gain):
    seg, width = mid_token.shape
    shape = jax.ShapeDtypeStruct
    return pl.pallas_call(
        norm_kernel,
        out_shape=(
            shape((seg, width), jnp.bfloat16),
            shape((seg, width), F32),
            shape((seg, 1), F32),
            shape((seg, width), F32),
        ),
        in_specs=[VMEM] * 6,
        out_specs=(VMEM,) * 4,
        compiler_params=room(6),
    )(from_core, from_chip, mid_token, mid_grad, count, gain)


def dout_kernel(dout_ref, second_ref, ready_ref, full_ref, half_ref):
    seg = dout_ref.shape[0]
    last = lax.broadcasted_iota(jnp.int32, (seg, 1), 0) == seg - 1
    dout = dout_ref[...] + jnp.where(last, second_ref[...], 0.0)
    full_ref[...] = dout
    half_ref[...] = dout.astype(jnp.bfloat16)


def whole_dout(dout, second, ready):
    shape = jax.ShapeDtypeStruct
    return pl.pallas_call(
        dout_kernel,
        out_shape=(shape(dout.shape, F32), shape(dout.shape, jnp.bfloat16)),
        in_specs=[VMEM, VMEM, ANY],
        out_specs=(VMEM, VMEM),
        compiler_params=room(4),
    )(dout, second, ready)


def project_kernel(*refs):
    pieces, weight = refs[:8], refs[8]
    q_ref, kv_ref, w_ref, rows, sems = refs[9:]
    copies = stacked(pieces, rows)
    depth = weight.shape[1]
    for i in range(weight.shape[0]):
        copies.append((weight.at[i, :, : 3 * HEAD], w_ref.at[i * depth : (i + 1) * depth, :]))
    fetched(copies, sems)
    out = jnp.dot(rows[...], w_ref[...], preferred_element_type=F32).astype(jnp.bfloat16)
    q_ref[...] = out[:, :HEAD]
    kv_ref[...] = out[:, HEAD:]


def project(pieces, weights):
    rows = sum(piece.shape[0] for piece in pieces)
    width = pieces[0].shape[1]
    bf16 = lambda *shape: jax.ShapeDtypeStruct(shape, jnp.bfloat16)
    return pl.pallas_call(
        project_kernel,
        out_shape=(
            bf16(rows, HEAD),
            bf16(rows, 2 * HEAD),
            bf16(width, 3 * HEAD),
        ),
        in_specs=[ANY] * 9,
        out_specs=(VMEM,) * 3,
        scratch_shapes=[
            pltpu.VMEM((rows, width), jnp.bfloat16),
            pltpu.SemaphoreType.DMA((16,)),
        ],
        compiler_params=room(12),
    )(*pieces, weights)


def dattended_kernel(*refs):
    place_ref, pieces, mine, theirs = refs[0], refs[1:9], refs[9], refs[10]
    da_ref, rows, weight, sems = refs[11:]
    core = place_ref[3]
    half, wide = mine.shape[0] // 2, mine.shape[1]
    spot = pl.multiple_of(core * half, half)
    other = pl.multiple_of((1 - core) * half, half)
    copies = stacked(pieces, rows)
    for i in range(2):
        part, lanes = slice(i * half, (i + 1) * half), slice(i * wide, (i + 1) * wide)
        copies.append((mine.at[part, :], weight.at[pl.ds(spot, half), lanes]))
        copies.append((theirs.at[part, :], weight.at[pl.ds(other, half), lanes]))
    fetched(copies, sems)
    da_ref[...] = contract_last(rows[...], weight[...]).astype(jnp.bfloat16)


def dattended(where, pieces, mine, theirs):
    rows = sum(piece.shape[0] for piece in pieces)
    width = pieces[0].shape[1]
    return pl.pallas_call(
        dattended_kernel,
        out_shape=jax.ShapeDtypeStruct((rows, HEAD), jnp.bfloat16),
        in_specs=[SMEM] + [ANY] * 10,
        out_specs=VMEM,
        scratch_shapes=[
            pltpu.VMEM((rows, width), jnp.bfloat16),
            pltpu.VMEM((HEAD, width), jnp.bfloat16),
            pltpu.SemaphoreType.DMA((12,)),
        ],
        compiler_params=room(10),
    )(where, *pieces, mine, theirs)


def attention_kernel(tile, seg, *refs):
    place_ref, q_ref, da_ref, blocks = refs[0], refs[1], refs[2], refs[3:7]
    dq_ref, outs, (kv, dkt, dvt, sems) = refs[7], refs[8:12], refs[12:]
    half, turn, pair, core = place_ref[0], place_ref[1], place_ref[2], place_ref[3]
    queries, keys = q_ref.shape[0], kv.shape[0]
    fetched(stacked(blocks, kv), sems)
    spot = lax.broadcasted_iota(jnp.int32, (1, keys), 1)
    block = spot // queries
    key_half = jnp.where(block < 2, half, 1 - half)
    key_pair = jnp.where(block % 2 == 0, pair, 1 - pair)
    key_at = rows_at(spot % queries, key_half, turn, key_pair, core, seg)
    turn_up = math.log2(math.e) / math.sqrt(HEAD)
    scale = 1.0 / math.sqrt(HEAD)
    k = kv[:, :HEAD]
    v = kv[:, HEAD:]
    for step in range(queries // tile):
        rows = slice(step * tile, (step + 1) * tile)
        query = lax.broadcasted_iota(jnp.int32, (tile, 1), 0) + step * tile
        query_at = rows_at(query, half, turn, pair, core, seg)
        q = q_ref[rows, :]
        da = da_ref[rows, :]
        score = jnp.where(key_at <= query_at, contract_last(q, k), NEG)
        peak = jnp.max(score, axis=1, keepdims=True)
        expo = jnp.exp2((score - peak) * turn_up)
        probs = expo * (1.0 / jnp.sum(expo, axis=1, keepdims=True))
        probs_b = probs.astype(jnp.bfloat16)
        attended = jnp.dot(probs_b, v, preferred_element_type=F32).astype(jnp.bfloat16)
        delta = jnp.sum(da.astype(F32) * attended.astype(F32), axis=1, keepdims=True)
        dscore = (probs * (contract_last(da, v) - delta)).astype(jnp.bfloat16)
        dq = jnp.dot(dscore, k, preferred_element_type=F32) * scale
        dq_ref[rows, :] = dq.astype(jnp.bfloat16)
        dk_part = contract_first(q, dscore)
        dv_part = contract_first(da, probs_b)
        if step == 0:
            dkt[...] = dk_part
            dvt[...] = dv_part
        else:
            dkt[...] += dk_part
            dvt[...] += dv_part
    part = keys // len(outs)
    for i, out in enumerate(outs):
        lanes = slice(i * part, (i + 1) * part)
        out[:, :HEAD] = (dkt[:, lanes] * scale).T.astype(jnp.bfloat16)
        out[:, HEAD:] = dvt[:, lanes].T.astype(jnp.bfloat16)


def attention(where, q, da, blocks, seg):
    queries = q.shape[0]
    keys = sum(block.shape[0] for block in blocks)
    part = jax.ShapeDtypeStruct(blocks[0].shape, jnp.bfloat16)
    return pl.pallas_call(
        functools.partial(attention_kernel, 128, seg),
        out_shape=(jax.ShapeDtypeStruct((queries, HEAD), jnp.bfloat16),) + (part,) * 4,
        in_specs=[SMEM] + [VMEM] * 2 + [ANY] * 4,
        out_specs=(VMEM,) * 5,
        scratch_shapes=[
            pltpu.VMEM((keys, 2 * HEAD), jnp.bfloat16),
            pltpu.VMEM((HEAD, keys), F32),
            pltpu.VMEM((HEAD, keys), F32),
            pltpu.SemaphoreType.DMA((4,)),
        ],
        compiler_params=room(28),
        cost_estimate=pl.CostEstimate(
            flops=12 * queries * keys * HEAD,
            bytes_accessed=2 * HEAD * (3 * queries + 4 * keys),
            transcendentals=queries * keys,
        ),
    )(where, q, da, *blocks)


def unproject_kernel(seg, dq_ref, *refs):
    parts, w_ref, swap_ref, outs = refs[:4], refs[4], refs[5], refs[6:]
    dkv = sum(ref[...].astype(F32) for ref in parts).astype(jnp.bfloat16)
    left = jnp.concatenate([dq_ref[...], dkv], axis=1)
    out = contract_last(left, w_ref[...])
    for i, slot in enumerate((1, 4, 5, 7)):
        swap_ref[i * seg : (i + 1) * seg, :] = out[slot * seg : (slot + 1) * seg].astype(WIRE)
    for ref, slot in zip(outs, (0, 2, 3, 6)):
        ref[...] = out[slot * seg : (slot + 1) * seg]


def unproject(dq, parts, w_full, seg):
    width = w_full.shape[0]
    return pl.pallas_call(
        functools.partial(unproject_kernel, seg),
        out_shape=(jax.ShapeDtypeStruct((4 * seg, width), WIRE),)
        + (jax.ShapeDtypeStruct((seg, width), F32),) * 4,
        in_specs=[VMEM] * 6,
        out_specs=(VMEM,) * 5,
        compiler_params=room(16),
    )(dq, *parts, w_full)


def join_kernel(swapped, own, near, next_to, far, own_out, near_out, next_out, far_out):
    seg = own.shape[0]
    own_out[...] = own[...] + swapped[:seg, :].astype(F32)
    near_out[...] = near[...] + swapped[seg : 2 * seg, :].astype(F32)
    next_out[...] = (next_to[...] + swapped[2 * seg : 3 * seg, :].astype(F32)).astype(WIRE)
    far_out[...] = (far[...] + swapped[3 * seg :, :].astype(F32)).astype(WIRE)


def joined(swapped, own, near, next_to, far):
    wide = jax.ShapeDtypeStruct(own.shape, F32)
    thin = jax.ShapeDtypeStruct(own.shape, WIRE)
    return pl.pallas_call(
        join_kernel,
        out_shape=(wide, wide, thin, thin),
        in_specs=[VMEM] * 5,
        out_specs=(VMEM,) * 4,
        compiler_params=room(6),
    )(swapped, own, near, next_to, far)


def summed_rows(swap, own, near, next_to, far):
    own, near, next_to, far = joined(other_core(swap), own, near, next_to, far)
    far = turned(far, -1).astype(F32)
    next_to = turned_over(next_to).astype(F32)
    near = turned((near + far).astype(WIRE), -1).astype(F32)
    return own + next_to + near


def per_device(tokens, starts, gain, w_query, w_key, w_value, w_out, cotangent):
    token_rows = tokens[0]
    grad_out = cotangent[0]
    rows, width = token_rows.shape
    seg = starts.shape[1]
    length = rows * CTX
    ctx = lax.axis_index("ctx")
    core, pair = ctx % CORES, ctx // CORES % PAIR
    turn, half = ctx // (CORES * PAIR) % TURNS, ctx // (CORES * PAIR * TURNS)
    where = jnp.stack([half, turn, pair, core, lax.axis_index("dp"), ctx])

    mine, own_starts = cut_weights(where, w_query, w_key, w_value, w_out, starts)
    own_starts = own_starts[0]
    weights = gathered_weights(mine)
    beside, facing = other_core(own_starts), other_chip(own_starts)
    before = jnp.where(core == 0, facing, beside)
    after = jnp.where(core == 0, beside, facing)
    before = jnp.where(ctx == 0, -1, before)
    after = jnp.where(ctx == CTX - 1, length, after)
    stop = jnp.full((2,), length, jnp.int32)
    window = jnp.concatenate([before, own_starts, after, stop])
    slots = 3 * seg
    opens, ends = window[:slots], window[1 : slots + 1]
    edges = jnp.stack([opens, ends, window[2:]])[:, :, None]
    to_core, to_chip, mid_token, mid_grad, first, count = window_sums(
        where, edges, token_rows, grad_out, seg
    )
    second = two_back(first)
    normin, normed, rms, dout = norm(
        other_core(to_core), other_chip(to_chip), mid_token, mid_grad, count, gain[None]
    )
    pieces = gathered_rows(normin)
    q, own, w_full = project(pieces, weights)
    dout, dout_b = whole_dout(dout, second, pieces[2])
    cross, far, beside = across(own, 0, True), across(own, 0, False), other_pair(own)
    out_mine, out_theirs = rows_out(weights, turn, core)
    da = dattended(where, gathered_rows(dout_b), out_mine, out_theirs)
    dq, own, beside, far, cross = attention(where, q, da, (own, beside, far, cross), seg)
    parts = (own, other_pair(beside), across(far, 1, False), across(cross, 1, True))
    dnormin = summed_rows(*unproject(dq, parts, w_full, seg))

    scaled = dnormin * gain
    dpooled = dout + (scaled - normed * jnp.mean(scaled * normed, axis=-1, keepdims=True)) / rms
    per_seg = (dpooled / count).astype(WIRE)
    beside, facing = other_core(per_seg), other_chip(per_seg)
    before = jnp.where(core == 0, facing, beside)
    after = jnp.where(core == 0, beside, facing)
    per_window = jnp.concatenate([before, per_seg, after], axis=0)
    positions = (ctx * rows + lax.iota(jnp.int32, rows))[:, None]
    member = (opens[None] <= positions) & (positions < ends[None])
    spread = jnp.dot(member.astype(WIRE), per_window, preferred_element_type=F32)
    return (grad_out.astype(F32) + spread).astype(jnp.bfloat16)[None]


def solution(mesh):
    return jax.shard_map(
        per_device,
        mesh=mesh,
        in_specs=(
            P("dp", "ctx", None),
            P("dp", "ctx"),
            P(),
            P("dp", None),
            P("dp", None),
            P("dp", None),
            P("dp", None),
            P("dp", "ctx", None),
        ),
        out_specs=P("dp", "ctx", None),
        check_vma=False,
    )
```

```python
import functools
import math

import jax
import jax.numpy as jnp
from jax import lax
from jax.experimental import pallas as pl
from jax.experimental.pallas import tpu as pltpu
from jax.sharding import PartitionSpec as P

HEAD = 128
HALVES, TURNS, PAIR, CORES = 2, 4, 2, 2
CTX = HALVES * TURNS * PAIR * CORES
NEG = -1e30
WIRE = jnp.bfloat16
F32 = jnp.float32
VMEM = pl.BlockSpec(memory_space=pltpu.VMEM)
SMEM = pl.BlockSpec(memory_space=pltpu.SMEM)
ANY = pl.BlockSpec(memory_space=pl.ANY)
HBM = pl.BlockSpec(memory_space=pltpu.HBM)


def room(mib):
    return pltpu.CompilerParams(vmem_limit_bytes=mib * 1024 * 1024)


def place(half, turn, pair, core):
    return ((half * TURNS + turn % TURNS) * PAIR + pair) * CORES + core


def moved(value, to):
    spots = [
        (h, t, p, k)
        for h in range(HALVES)
        for t in range(TURNS)
        for p in range(PAIR)
        for k in range(CORES)
    ]
    pairs = [(place(*s), place(*to(*s))) for s in spots if to(*s) is not None]
    return lax.ppermute(value, "ctx", pairs)


def other_chip(value):
    pairs = [(i, i + 1 if i % CORES else i - 1) for i in range(1, CTX - 1)]
    return lax.ppermute(value, "ctx", pairs)


def two_back(value):
    return lax.ppermute(value, "ctx", [(i, i - CORES) for i in range(CORES, CTX)])


def other_core(value):
    return moved(value, lambda h, t, p, k: (h, t, p, 1 - k))


def other_pair(value):
    return moved(value, lambda h, t, p, k: (h, t, 1 - p, k))


def across(value, source, cross):
    return moved(
        value,
        lambda h, t, p, k: (1 - h, t, 1 - p if cross else p, k) if h == source else None,
    )


def turned(value, way):
    return moved(value, lambda h, t, p, k: (h, t + way * (1 - 2 * k), p, k))


def turned_over(value):
    return moved(value, lambda h, t, p, k: (h, t - (1 - 2 * k), p, 1 - k))


def contract_last(left, right):
    return lax.dot_general(left, right, (((1,), (1,)), ((), ())), preferred_element_type=F32)


def contract_first(left, right):
    return lax.dot_general(left, right, (((0,), (0,)), ((), ())), preferred_element_type=F32)


def cut_kernel(place_ref, q_ref, k_ref, v_ref, o_ref, start_ref, out_ref, start_out, sems):
    rows = out_ref.shape[0]
    half, width = rows // CORES, o_ref.shape[1]
    core = place_ref[3]
    lane = pl.multiple_of((place_ref[1] * CORES + core) * HEAD, HEAD)
    copies = [
        (w.at[:, pl.ds(lane, HEAD)], out_ref.at[:, i * HEAD : (i + 1) * HEAD])
        for i, w in enumerate((q_ref, k_ref, v_ref))
    ]
    at = pl.multiple_of(core * half, half)
    for i in range(2):
        lanes = slice(i * width // 2, (i + 1) * width // 2)
        copies.append(
            (o_ref.at[pl.ds(at, half), lanes], out_ref.at[i * half : (i + 1) * half, 3 * HEAD :])
        )
    copies.append((start_ref, start_out))
    fetched(copies, sems)


def cut_weights(where, w_query, w_key, w_value, w_out, starts):
    rows, width = w_out.shape
    return pl.pallas_call(
        cut_kernel,
        out_shape=(
            jax.ShapeDtypeStruct((rows, 3 * HEAD + width // 2), w_query.dtype),
            jax.ShapeDtypeStruct(starts.shape, starts.dtype),
        ),
        in_specs=[SMEM] + [HBM] * 4 + [ANY],
        out_specs=(VMEM, VMEM),
        scratch_shapes=[pltpu.SemaphoreType.DMA((6,))],
        compiler_params=room(60),
    )(where, w_query, w_key, w_value, w_out, starts)


def gathered_weights(mine):
    return lax.all_gather(mine, "dp", axis=0, tiled=False)


def gathered_rows(shard):
    near = turned(shard, 1)
    next_to = turned_over(shard)
    far = turned(near, 1)
    return [
        shard,
        other_core(shard),
        near,
        next_to,
        other_core(near),
        other_core(next_to),
        far,
        other_core(far),
    ]


def rows_at(row, half, turn, pair, core, seg):
    slot = row // seg
    two = slot // 2
    way = 1 - 2 * core
    step = jnp.where(two == 0, 0, jnp.where(two == 1, way, jnp.where(two == 2, -way, 2)))
    flip = jnp.where(two == 2, 1 - slot % 2, slot % 2)
    its_core = jnp.where(flip == 1, 1 - core, core)
    its_turn = (turn - step + TURNS) % TURNS
    return place(half, its_turn, pair, its_core) * seg + row % seg


def fetched(copies, sems):
    started = []
    for i, (source, target) in enumerate(copies):
        started.append(pltpu.make_async_copy(source, target, sems.at[i]))
        started[-1].start()
    for copy in started:
        copy.wait()


def stacked(pieces, out_ref):
    copies, at = [], 0
    for piece in pieces:
        copies.append((piece, out_ref.at[at : at + piece.shape[0], :]))
        at += piece.shape[0]
    return copies


def window_kernel(place_ref, edge_ref, token_hbm, grad_hbm, *refs):
    core_ref, chip_ref, mid_token, mid_grad, first_ref, count_ref = refs[:6]
    token_ref, grad_ref, sems = refs[6:]
    rows, width = token_ref.shape
    seg = mid_token.shape[0]
    token_copy = pltpu.make_async_copy(token_hbm, token_ref, sems.at[0])
    grad_copy = pltpu.make_async_copy(grad_hbm, grad_ref, sems.at[1])
    token_copy.start()
    grad_copy.start()
    ctx, core = place_ref[5], place_ref[3]
    at = lax.broadcasted_iota(jnp.int32, (1, rows), 1) + ctx * rows
    opens, ends, nexts = edge_ref[0], edge_ref[1], edge_ref[2]
    count_ref[...] = (ends - opens)[seg : 2 * seg].astype(F32)
    member = ((opens <= at) & (at < ends)).astype(jnp.bfloat16)
    earlier = ((ends <= at) & (at < nexts)).astype(jnp.bfloat16)
    token_copy.wait()
    token = jnp.dot(member, token_ref[...], preferred_element_type=F32)
    grad_copy.wait()
    grad = jnp.dot(earlier, grad_ref[...], preferred_element_type=F32)
    first = jnp.dot(member[:16], grad_ref[...], preferred_element_type=F32)
    first_ref[...] = first[:1]
    mid_token[...] = token[seg : 2 * seg]
    mid_grad[...] = grad[seg : 2 * seg]

    def send(lower_ref, upper_ref):
        lower_ref[:, :width] = token[:seg].astype(WIRE)
        lower_ref[:, width:] = grad[:seg].astype(WIRE)
        upper_ref[:, :width] = token[2 * seg :].astype(WIRE)
        upper_ref[:, width:] = grad[2 * seg :].astype(WIRE)

    @pl.when(core == 0)
    def _():
        send(chip_ref, core_ref)

    @pl.when(core == 1)
    def _():
        send(core_ref, chip_ref)


def window_sums(where, edges, tokens, grads, seg):
    rows, width = tokens.shape
    shape = jax.ShapeDtypeStruct
    return pl.pallas_call(
        window_kernel,
        out_shape=(
            shape((seg, 2 * width), WIRE),
            shape((seg, 2 * width), WIRE),
            shape((seg, width), F32),
            shape((seg, width), F32),
            shape((1, width), F32),
            shape((seg, 1), F32),
        ),
        in_specs=[SMEM, VMEM] + [HBM] * 2,
        out_specs=(VMEM,) * 6,
        scratch_shapes=[
            pltpu.VMEM((rows, width), tokens.dtype),
            pltpu.VMEM((rows, width), grads.dtype),
            pltpu.SemaphoreType.DMA((2,)),
        ],
        compiler_params=room(16),
    )(where, edges, tokens, grads)


def norm_kernel(core_ref, chip_ref, mid_token, mid_grad, second_ref, count_ref, gain_ref, *outs):
    both_ref, normed_ref, rms_ref, dout_ref = outs
    seg, width = mid_token.shape
    got = core_ref[...].astype(F32) + chip_ref[...].astype(F32)
    pooled = (mid_token[...] + got[:, :width]) / count_ref[...]
    rms = jnp.sqrt(jnp.mean(pooled * pooled, axis=1, keepdims=True) + 1e-06)
    normed = pooled / rms
    normed_ref[...] = normed
    rms_ref[...] = rms
    last = lax.broadcasted_iota(jnp.int32, (seg, 1), 0) == seg - 1
    dout = mid_grad[...] + got[:, width:] + jnp.where(last, second_ref[...], 0.0)
    dout_ref[...] = dout
    both_ref[:, :width] = (normed * gain_ref[...]).astype(jnp.bfloat16)
    both_ref[:, width:] = dout.astype(jnp.bfloat16)


def norm(from_core, from_chip, mid_token, mid_grad, second, count, gain):
    seg, width = mid_token.shape
    shape = jax.ShapeDtypeStruct
    return pl.pallas_call(
        norm_kernel,
        out_shape=(
            shape((seg, 2 * width), jnp.bfloat16),
            shape((seg, width), F32),
            shape((seg, 1), F32),
            shape((seg, width), F32),
        ),
        in_specs=[VMEM] * 7,
        out_specs=(VMEM,) * 4,
        compiler_params=room(6),
    )(from_core, from_chip, mid_token, mid_grad, second, count, gain)


def project_kernel(seg, *refs):
    place_ref, pieces, weight = refs[0], refs[1:9], refs[9]
    q_ref, kv_ref, mine_ref, theirs_ref, rows, w_in, w_back, sems = refs[10:]
    core, head = place_ref[3], place_ref[1] * CORES
    half, wide = seg, rows.shape[1] // 4
    depth = weight.shape[1]
    copies = stacked(pieces, rows)
    for i in range(weight.shape[0]):
        copies.append((weight.at[i, :, : 3 * HEAD], w_in.at[i * depth : (i + 1) * depth, :]))
    for j, its_head in enumerate((head + core, head + 1 - core)):
        for i in range(2):
            source = weight.at[its_head, i * half : (i + 1) * half, 3 * HEAD :]
            lanes = slice(i * wide, (i + 1) * wide)
            copies.append((source, w_back.at[j * half : (j + 1) * half, lanes]))
    fetched(copies, sems)
    width = rows.shape[1] // 2
    out = jnp.dot(rows[:, :width], w_in[...], preferred_element_type=F32).astype(jnp.bfloat16)
    q_ref[...] = out[:, :HEAD]
    kv_ref[...] = out[:, HEAD:]
    da = contract_last(rows[:, width:], w_back[...]).astype(jnp.bfloat16)
    mine_ref[...] = da[:, :half]
    for slot, its_slot in enumerate((1, 0, 4, 5, 2, 3, 7, 6)):
        its_rows = slice(its_slot * seg, (its_slot + 1) * seg)
        theirs_ref[its_rows, :] = da[slot * seg : (slot + 1) * seg, half:]


def project(where, pieces, weights):
    seg, width = pieces[0].shape
    rows = seg * len(pieces)
    half = HEAD // CORES
    bf16 = lambda *shape: jax.ShapeDtypeStruct(shape, jnp.bfloat16)
    return pl.pallas_call(
        functools.partial(project_kernel, half),
        out_shape=(bf16(rows, HEAD), bf16(rows, 2 * HEAD), bf16(rows, half), bf16(rows, half)),
        in_specs=[SMEM] + [ANY] * 9,
        out_specs=(VMEM,) * 4,
        scratch_shapes=[
            pltpu.VMEM((rows, width), jnp.bfloat16),
            pltpu.VMEM((width // 2, 3 * HEAD), jnp.bfloat16),
            pltpu.VMEM((HEAD, width // 2), jnp.bfloat16),
            pltpu.SemaphoreType.DMA((20,)),
        ],
        compiler_params=room(12),
    )(where, *pieces, weights)


def attention_kernel(tile, seg, *refs):
    place_ref, q_ref, mine_ref, theirs_ref, blocks = *refs[:4], refs[4:8]
    dq_ref, outs, (kv, da_ref, dkt, dvt, sems) = refs[8], refs[9:13], refs[13:]
    half, turn, pair, core = place_ref[0], place_ref[1], place_ref[2], place_ref[3]
    queries, keys = q_ref.shape[0], kv.shape[0]
    fetched(stacked(blocks, kv), sems)

    @pl.when(core == 0)
    def _():
        da_ref[:, : HEAD // 2] = mine_ref[...]
        da_ref[:, HEAD // 2 :] = theirs_ref[...]

    @pl.when(core == 1)
    def _():
        da_ref[:, : HEAD // 2] = theirs_ref[...]
        da_ref[:, HEAD // 2 :] = mine_ref[...]

    spot = lax.broadcasted_iota(jnp.int32, (1, keys), 1)
    block = spot // queries
    key_half = jnp.where(block < 2, half, 1 - half)
    key_pair = jnp.where(block % 2 == 0, pair, 1 - pair)
    key_at = rows_at(spot % queries, key_half, turn, key_pair, core, seg)
    turn_up = math.log2(math.e) / math.sqrt(HEAD)
    scale = 1.0 / math.sqrt(HEAD)
    k = kv[:, :HEAD]
    v = kv[:, HEAD:]
    for step in range(queries // tile):
        rows = slice(step * tile, (step + 1) * tile)
        query = lax.broadcasted_iota(jnp.int32, (tile, 1), 0) + step * tile
        query_at = rows_at(query, half, turn, pair, core, seg)
        q = q_ref[rows, :]
        da = da_ref[rows, :]
        score = jnp.where(key_at <= query_at, contract_last(q, k), NEG)
        peak = jnp.max(score, axis=1, keepdims=True)
        expo = jnp.exp2((score - peak) * turn_up)
        probs = expo * (1.0 / jnp.sum(expo, axis=1, keepdims=True))
        probs_b = probs.astype(jnp.bfloat16)
        attended = jnp.dot(probs_b, v, preferred_element_type=F32).astype(jnp.bfloat16)
        delta = jnp.sum(da.astype(F32) * attended.astype(F32), axis=1, keepdims=True)
        dscore = (probs * (contract_last(da, v) - delta)).astype(jnp.bfloat16)
        dq = jnp.dot(dscore, k, preferred_element_type=F32) * scale
        dq_ref[rows, :] = dq.astype(jnp.bfloat16)
        dk_part = contract_first(q, dscore)
        dv_part = contract_first(da, probs_b)
        if step == 0:
            dkt[...] = dk_part
            dvt[...] = dv_part
        else:
            dkt[...] += dk_part
            dvt[...] += dv_part
    part = keys // len(outs)
    for i, out in enumerate(outs):
        lanes = slice(i * part, (i + 1) * part)
        out[:, :HEAD] = (dkt[:, lanes] * scale).T.astype(jnp.bfloat16)
        out[:, HEAD:] = dvt[:, lanes].T.astype(jnp.bfloat16)


def attention(where, q, mine, theirs, blocks, seg):
    queries = q.shape[0]
    keys = sum(block.shape[0] for block in blocks)
    part = jax.ShapeDtypeStruct(blocks[0].shape, jnp.bfloat16)
    return pl.pallas_call(
        functools.partial(attention_kernel, 128, seg),
        out_shape=(jax.ShapeDtypeStruct((queries, HEAD), jnp.bfloat16),) + (part,) * 4,
        in_specs=[SMEM] + [VMEM] * 3 + [ANY] * 4,
        out_specs=(VMEM,) * 5,
        scratch_shapes=[
            pltpu.VMEM((keys, 2 * HEAD), jnp.bfloat16),
            pltpu.VMEM((queries, HEAD), jnp.bfloat16),
            pltpu.VMEM((HEAD, keys), F32),
            pltpu.VMEM((HEAD, keys), F32),
            pltpu.SemaphoreType.DMA((4,)),
        ],
        compiler_params=room(28),
        cost_estimate=pl.CostEstimate(
            flops=12 * queries * keys * HEAD,
            bytes_accessed=2 * HEAD * (3 * queries + 4 * keys),
            transcendentals=queries * keys,
        ),
    )(where, q, mine, theirs, *blocks)


def unproject_kernel(seg, dq_ref, *refs):
    parts, weight, swap_ref, outs, (w_in, sems) = refs[:4], refs[4], refs[5], refs[6:10], refs[10:]
    depth = weight.shape[1]
    fetched(
        [
            (weight.at[i, :, : 3 * HEAD], w_in.at[i * depth : (i + 1) * depth, :])
            for i in range(weight.shape[0])
        ],
        sems,
    )
    dkv = sum(ref[...].astype(F32) for ref in parts).astype(jnp.bfloat16)
    left = jnp.concatenate([dq_ref[...], dkv], axis=1)
    out = contract_last(left, w_in[...])
    for i, slot in enumerate((1, 4, 5, 7)):
        swap_ref[i * seg : (i + 1) * seg, :] = out[slot * seg : (slot + 1) * seg].astype(WIRE)
    for ref, slot in zip(outs, (0, 2, 3, 6)):
        ref[...] = out[slot * seg : (slot + 1) * seg]


def unproject(dq, parts, weights, seg):
    width = weights.shape[0] * weights.shape[1]
    return pl.pallas_call(
        functools.partial(unproject_kernel, seg),
        out_shape=(jax.ShapeDtypeStruct((4 * seg, width), WIRE),)
        + (jax.ShapeDtypeStruct((seg, width), F32),) * 4,
        in_specs=[VMEM] * 5 + [ANY],
        out_specs=(VMEM,) * 5,
        scratch_shapes=[
            pltpu.VMEM((width, 3 * HEAD), jnp.bfloat16),
            pltpu.SemaphoreType.DMA((weights.shape[0],)),
        ],
        compiler_params=room(16),
    )(dq, *parts, weights)


def join_kernel(swapped, own, near, next_to, far, own_out, near_out, next_out, far_out):
    seg = own.shape[0]
    own_out[...] = own[...] + swapped[:seg, :].astype(F32)
    near_out[...] = near[...] + swapped[seg : 2 * seg, :].astype(F32)
    next_out[...] = (next_to[...] + swapped[2 * seg : 3 * seg, :].astype(F32)).astype(WIRE)
    far_out[...] = (far[...] + swapped[3 * seg :, :].astype(F32)).astype(WIRE)


def joined(swapped, own, near, next_to, far):
    wide = jax.ShapeDtypeStruct(own.shape, F32)
    thin = jax.ShapeDtypeStruct(own.shape, WIRE)
    return pl.pallas_call(
        join_kernel,
        out_shape=(wide, wide, thin, thin),
        in_specs=[VMEM] * 5,
        out_specs=(VMEM,) * 4,
        compiler_params=room(6),
    )(swapped, own, near, next_to, far)


def summed_rows(swap, own, near, next_to, far):
    own, near, next_to, far = joined(other_core(swap), own, near, next_to, far)
    far = turned(far, -1).astype(F32)
    next_to = turned_over(next_to).astype(F32)
    near = turned((near + far).astype(WIRE), -1).astype(F32)
    return own + next_to + near


def per_device(tokens, starts, gain, w_query, w_key, w_value, w_out, cotangent):
    token_rows = tokens[0]
    grad_out = cotangent[0]
    rows, width = token_rows.shape
    seg = starts.shape[1]
    length = rows * CTX
    ctx = lax.axis_index("ctx")
    core, pair = ctx % CORES, ctx // CORES % PAIR
    turn, half = ctx // (CORES * PAIR) % TURNS, ctx // (CORES * PAIR * TURNS)
    where = jnp.stack([half, turn, pair, core, lax.axis_index("dp"), ctx])

    mine, own_starts = cut_weights(where, w_query, w_key, w_value, w_out, starts)
    own_starts = own_starts[0]
    weights = gathered_weights(mine)
    beside, facing = other_core(own_starts), other_chip(own_starts)
    before = jnp.where(core == 0, facing, beside)
    after = jnp.where(core == 0, beside, facing)
    before = jnp.where(ctx == 0, -1, before)
    after = jnp.where(ctx == CTX - 1, length, after)
    stop = jnp.full((2,), length, jnp.int32)
    window = jnp.concatenate([before, own_starts, after, stop])
    slots = 3 * seg
    opens, ends = window[:slots], window[1 : slots + 1]
    edges = jnp.stack([opens, ends, window[2:]])[:, :, None]
    to_core, to_chip, mid_token, mid_grad, first, count = window_sums(
        where, edges, token_rows, grad_out, seg
    )
    second = two_back(first)
    both, normed, rms, dout = norm(
        other_core(to_core), other_chip(to_chip), mid_token, mid_grad, second, count, gain[None]
    )
    q, own, mine, theirs = project(where, gathered_rows(both), weights)
    cross, far, beside = across(own, 0, True), across(own, 0, False), other_pair(own)
    theirs = other_core(theirs)
    blocks = (own, beside, far, cross)
    dq, own, beside, far, cross = attention(where, q, mine, theirs, blocks, seg)
    parts = (own, other_pair(beside), across(far, 1, False), across(cross, 1, True))
    dnormin = summed_rows(*unproject(dq, parts, weights, seg))

    scaled = dnormin * gain
    dpooled = dout + (scaled - normed * jnp.mean(scaled * normed, axis=-1, keepdims=True)) / rms
    per_seg = (dpooled / count).astype(WIRE)
    beside, facing = other_core(per_seg), other_chip(per_seg)
    before = jnp.where(core == 0, facing, beside)
    after = jnp.where(core == 0, beside, facing)
    per_window = jnp.concatenate([before, per_seg, after], axis=0)
    positions = (ctx * rows + lax.iota(jnp.int32, rows))[:, None]
    member = (opens[None] <= positions) & (positions < ends[None])
    spread = jnp.dot(member.astype(WIRE), per_window, preferred_element_type=F32)
    return (grad_out.astype(F32) + spread).astype(jnp.bfloat16)[None]


def solution(mesh):
    return jax.shard_map(
        per_device,
        mesh=mesh,
        in_specs=(
            P("dp", "ctx", None),
            P("dp", "ctx"),
            P(),
            P("dp", None),
            P("dp", None),
            P("dp", None),
            P("dp", None),
            P("dp", "ctx", None),
        ),
        out_specs=P("dp", "ctx", None),
        check_vma=False,
    )
```

```python
import functools
import math

import jax
import jax.numpy as jnp
from jax import lax
from jax.experimental import pallas as pl
from jax.experimental.pallas import tpu as pltpu
from jax.sharding import PartitionSpec as P

HEAD = 128
HALVES, TURNS, PAIR, CORES = 2, 4, 2, 2
CTX = HALVES * TURNS * PAIR * CORES
NEG = -1e30
WIRE = jnp.bfloat16
F32 = jnp.float32
VMEM = pl.BlockSpec(memory_space=pltpu.VMEM)
ANY = pl.BlockSpec(memory_space=pl.ANY)
HBM = pl.BlockSpec(memory_space=pltpu.HBM)


def room(mib):
    return pltpu.CompilerParams(vmem_limit_bytes=mib * 1024 * 1024)


def place(half, turn, pair, core):
    return ((half * TURNS + turn % TURNS) * PAIR + pair) * CORES + core


def here():
    ctx = lax.axis_index("ctx")
    core, pair = ctx % CORES, ctx // CORES % PAIR
    return ctx // (CORES * PAIR * TURNS), ctx // (CORES * PAIR) % TURNS, pair, core


def moved(value, to):
    spots = [
        (h, t, p, k)
        for h in range(HALVES)
        for t in range(TURNS)
        for p in range(PAIR)
        for k in range(CORES)
    ]
    pairs = [(place(*s), place(*to(*s))) for s in spots if to(*s) is not None]
    return lax.ppermute(value, "ctx", pairs)


def other_chip(value):
    pairs = [(i, i + 1 if i % CORES else i - 1) for i in range(1, CTX - 1)]
    return lax.ppermute(value, "ctx", pairs)


def two_back(value):
    return lax.ppermute(value, "ctx", [(i, i - CORES) for i in range(CORES, CTX)])


def other_core(value):
    return moved(value, lambda h, t, p, k: (h, t, p, 1 - k))


def other_pair(value):
    return moved(value, lambda h, t, p, k: (h, t, 1 - p, k))


def across(value, source, cross):
    return moved(
        value,
        lambda h, t, p, k: (1 - h, t, 1 - p if cross else p, k) if h == source else None,
    )


def turned(value, way):
    return moved(value, lambda h, t, p, k: (h, t + way * (1 - 2 * k), p, k))


def turned_over(value):
    return moved(value, lambda h, t, p, k: (h, t - (1 - 2 * k), p, 1 - k))


def contract_last(left, right):
    return lax.dot_general(left, right, (((1,), (1,)), ((), ())), preferred_element_type=F32)


def contract_first(left, right):
    return lax.dot_general(left, right, (((0,), (0,)), ((), ())), preferred_element_type=F32)


def cut_kernel(q_ref, k_ref, v_ref, o_ref, start_ref, out_ref, start_out, sems):
    rows = out_ref.shape[0]
    half, width = rows // CORES, o_ref.shape[1]
    _, turn, _, core = here()
    lane = pl.multiple_of((turn * CORES + core) * HEAD, HEAD)
    copies = [
        (w.at[:, pl.ds(lane, HEAD)], out_ref.at[:, i * HEAD : (i + 1) * HEAD])
        for i, w in enumerate((q_ref, k_ref, v_ref))
    ]
    at = pl.multiple_of(core * half, half)
    for i in range(2):
        lanes = slice(i * width // 2, (i + 1) * width // 2)
        copies.append(
            (o_ref.at[pl.ds(at, half), lanes], out_ref.at[i * half : (i + 1) * half, 3 * HEAD :])
        )
    copies.append((start_ref, start_out))
    fetched(copies, sems)


def cut_weights(w_query, w_key, w_value, w_out, starts):
    rows, width = w_out.shape
    return pl.pallas_call(
        cut_kernel,
        out_shape=(
            jax.ShapeDtypeStruct((rows, 3 * HEAD + width // 2), w_query.dtype),
            jax.ShapeDtypeStruct(starts.shape, starts.dtype),
        ),
        in_specs=[HBM] * 4 + [ANY],
        out_specs=(VMEM, VMEM),
        scratch_shapes=[pltpu.SemaphoreType.DMA((6,))],
        compiler_params=room(60),
    )(w_query, w_key, w_value, w_out, starts)


def gathered_weights(mine):
    return lax.all_gather(mine, "dp", axis=0, tiled=False)


def pass_kernel(value_ref, ready_ref, out_ref):
    out_ref[...] = value_ref[...]


def passed_on(value, ready):
    return pl.pallas_call(
        pass_kernel,
        out_shape=jax.ShapeDtypeStruct(value.shape, value.dtype),
        in_specs=[VMEM, ANY],
        out_specs=VMEM,
        compiler_params=room(4),
    )(value, ready)


def gathered_rows(shard):
    near = turned(shard, 1)
    next_to = turned_over(passed_on(shard, near))
    far = turned(near, 1)
    return [
        shard,
        other_core(shard),
        near,
        next_to,
        other_core(near),
        other_core(next_to),
        far,
        other_core(far),
    ]


def rows_at(row, half, turn, pair, core, seg):
    slot = row // seg
    two = slot // 2
    way = 1 - 2 * core
    step = jnp.where(two == 0, 0, jnp.where(two == 1, way, jnp.where(two == 2, -way, 2)))
    flip = jnp.where(two == 2, 1 - slot % 2, slot % 2)
    its_core = jnp.where(flip == 1, 1 - core, core)
    its_turn = (turn - step + TURNS) % TURNS
    return place(half, its_turn, pair, its_core) * seg + row % seg


def fetched(copies, sems):
    started = []
    for i, (source, target) in enumerate(copies):
        started.append(pltpu.make_async_copy(source, target, sems.at[i]))
        started[-1].start()
    for copy in started:
        copy.wait()


def stacked(pieces, out_ref):
    copies, at = [], 0
    for piece in pieces:
        copies.append((piece, out_ref.at[at : at + piece.shape[0], :]))
        at += piece.shape[0]
    return copies


def window_kernel(own_ref, beside_ref, facing_ref, token_hbm, grad_hbm, *refs):
    core_ref, chip_ref, mid_token, mid_grad, first_ref = refs[:5]
    token_ref, grad_ref, sems = refs[5:]
    rows, width = token_ref.shape
    seg = mid_token.shape[0]
    token_copy = pltpu.make_async_copy(token_hbm, token_ref, sems.at[0])
    grad_copy = pltpu.make_async_copy(grad_hbm, grad_ref, sems.at[1])
    token_copy.start()
    grad_copy.start()
    ctx, core = lax.axis_index("ctx"), here()[3]
    at = lax.broadcasted_iota(jnp.int32, (rows, 1), 0) + ctx * rows
    before = jnp.where(core == 0, facing_ref[...], beside_ref[...])
    after = jnp.where(core == 0, beside_ref[...], facing_ref[...])
    before = jnp.where(ctx == 0, -1, before)
    after = jnp.where(ctx == CTX - 1, rows * CTX, after)
    begun = [(part <= at).astype(jnp.int32) for part in (before, own_ref[...], after)]
    slot = sum(jnp.sum(part, axis=1, keepdims=True) for part in begun) - 1
    slots = lax.broadcasted_iota(jnp.int32, (1, 3 * seg), 1)
    member = (slots == slot).astype(jnp.bfloat16)
    earlier = (slots == slot - 1).astype(jnp.bfloat16)
    token_copy.wait()
    token = contract_first(member, token_ref[...])
    grad_copy.wait()
    grad = contract_first(earlier, grad_ref[...])
    outside = jnp.broadcast_to((slot == 0).astype(jnp.bfloat16), (rows, HEAD))
    first_ref[...] = contract_first(outside, grad_ref[...])[:1]
    mid_token[...] = token[seg : 2 * seg]
    mid_grad[...] = grad[seg : 2 * seg]

    def send(lower_ref, upper_ref):
        lower_ref[:, :width] = token[:seg].astype(WIRE)
        lower_ref[:, width:] = grad[:seg].astype(WIRE)
        upper_ref[:, :width] = token[2 * seg :].astype(WIRE)
        upper_ref[:, width:] = grad[2 * seg :].astype(WIRE)

    @pl.when(core == 0)
    def _():
        send(chip_ref, core_ref)

    @pl.when(core == 1)
    def _():
        send(core_ref, chip_ref)


def window_sums(own, beside, facing, tokens, grads):
    rows, width = tokens.shape
    seg = own.shape[1]
    shape = jax.ShapeDtypeStruct
    return pl.pallas_call(
        window_kernel,
        out_shape=(
            shape((seg, 2 * width), WIRE),
            shape((seg, 2 * width), WIRE),
            shape((seg, width), F32),
            shape((seg, width), F32),
            shape((1, width), F32),
        ),
        in_specs=[VMEM] * 3 + [HBM] * 2,
        out_specs=(VMEM,) * 5,
        scratch_shapes=[
            pltpu.VMEM((rows, width), tokens.dtype),
            pltpu.VMEM((rows, width), grads.dtype),
            pltpu.SemaphoreType.DMA((2,)),
        ],
        compiler_params=room(16),
    )(own, beside, facing, tokens, grads)


def norm_kernel(core_ref, chip_ref, mid_token, mid_grad, second_ref, count_ref, gain_ref, *outs):
    both_ref, normed_ref, rms_ref, dout_ref = outs
    seg, width = mid_token.shape
    got = core_ref[...].astype(F32) + chip_ref[...].astype(F32)
    pooled = (mid_token[...] + got[:, :width]) / count_ref[...]
    rms = jnp.sqrt(jnp.mean(pooled * pooled, axis=1, keepdims=True) + 1e-06)
    normed = pooled / rms
    normed_ref[...] = normed
    rms_ref[...] = rms
    last = lax.broadcasted_iota(jnp.int32, (seg, 1), 0) == seg - 1
    dout = mid_grad[...] + got[:, width:] + jnp.where(last, second_ref[...], 0.0)
    dout_ref[...] = dout
    both_ref[:, :width] = (normed * gain_ref[...]).astype(jnp.bfloat16)
    both_ref[:, width:] = dout.astype(jnp.bfloat16)


def norm(from_core, from_chip, mid_token, mid_grad, second, count, gain):
    seg, width = mid_token.shape
    shape = jax.ShapeDtypeStruct
    return pl.pallas_call(
        norm_kernel,
        out_shape=(
            shape((seg, 2 * width), jnp.bfloat16),
            shape((seg, width), F32),
            shape((seg, 1), F32),
            shape((seg, width), F32),
        ),
        in_specs=[VMEM] * 7,
        out_specs=(VMEM,) * 4,
        compiler_params=room(6),
    )(from_core, from_chip, mid_token, mid_grad, second, count, gain)


def project_kernel(seg, *refs):
    pieces, weight = refs[:8], refs[8]
    q_ref, kv_ref, mine_ref, theirs_ref, rows, w_in, w_back, sems = refs[9:]
    _, turn, _, core = here()
    head = turn * CORES
    half, wide = seg, rows.shape[1] // 4
    depth = weight.shape[1]
    copies = stacked(pieces, rows)
    for i in range(weight.shape[0]):
        copies.append((weight.at[i, :, : 3 * HEAD], w_in.at[i * depth : (i + 1) * depth, :]))
    for j, its_head in enumerate((head + core, head + 1 - core)):
        for i in range(2):
            source = weight.at[its_head, i * half : (i + 1) * half, 3 * HEAD :]
            lanes = slice(i * wide, (i + 1) * wide)
            copies.append((source, w_back.at[j * half : (j + 1) * half, lanes]))
    fetched(copies, sems)
    width = rows.shape[1] // 2
    out = jnp.dot(rows[:, :width], w_in[...], preferred_element_type=F32).astype(jnp.bfloat16)
    q_ref[...] = out[:, :HEAD]
    kv_ref[...] = out[:, HEAD:]
    da = contract_last(rows[:, width:], w_back[...]).astype(jnp.bfloat16)
    mine_ref[...] = da[:, :half]
    for slot, its_slot in enumerate((1, 0, 4, 5, 2, 3, 7, 6)):
        its_rows = slice(its_slot * seg, (its_slot + 1) * seg)
        theirs_ref[its_rows, :] = da[slot * seg : (slot + 1) * seg, half:]


def project(pieces, weights):
    seg, width = pieces[0].shape
    rows = seg * len(pieces)
    half = HEAD // CORES
    bf16 = lambda *shape: jax.ShapeDtypeStruct(shape, jnp.bfloat16)
    return pl.pallas_call(
        functools.partial(project_kernel, half),
        out_shape=(bf16(rows, HEAD), bf16(rows, 2 * HEAD), bf16(rows, half), bf16(rows, half)),
        in_specs=[ANY] * 9,
        out_specs=(VMEM,) * 4,
        scratch_shapes=[
            pltpu.VMEM((rows, width), jnp.bfloat16),
            pltpu.VMEM((width // 2, 3 * HEAD), jnp.bfloat16),
            pltpu.VMEM((HEAD, width // 2), jnp.bfloat16),
            pltpu.SemaphoreType.DMA((20,)),
        ],
        compiler_params=room(40),
    )(*pieces, weights)


def attention_kernel(tile, seg, *refs):
    q_ref, mine_ref, theirs_ref, blocks = *refs[:3], refs[3:7]
    dq_ref, outs, (kv, da_ref, dkt, dvt, sems) = refs[7], refs[8:12], refs[12:]
    half, turn, pair, core = here()
    queries, keys = q_ref.shape[0], kv.shape[0]
    fetched(stacked(blocks, kv), sems)

    @pl.when(core == 0)
    def _():
        da_ref[:, : HEAD // 2] = mine_ref[...]
        da_ref[:, HEAD // 2 :] = theirs_ref[...]

    @pl.when(core == 1)
    def _():
        da_ref[:, : HEAD // 2] = theirs_ref[...]
        da_ref[:, HEAD // 2 :] = mine_ref[...]

    spot = lax.broadcasted_iota(jnp.int32, (1, keys), 1)
    block = spot // queries
    key_half = jnp.where(block < 2, half, 1 - half)
    key_pair = jnp.where(block % 2 == 0, pair, 1 - pair)
    key_at = rows_at(spot % queries, key_half, turn, key_pair, core, seg)
    turn_up = math.log2(math.e) / math.sqrt(HEAD)
    scale = 1.0 / math.sqrt(HEAD)
    k = kv[:, :HEAD]
    v = kv[:, HEAD:]
    for step in range(queries // tile):
        rows = slice(step * tile, (step + 1) * tile)
        query = lax.broadcasted_iota(jnp.int32, (tile, 1), 0) + step * tile
        query_at = rows_at(query, half, turn, pair, core, seg)
        q = q_ref[rows, :]
        da = da_ref[rows, :]
        score = jnp.where(key_at <= query_at, contract_last(q, k), NEG)
        peak = jnp.max(score, axis=1, keepdims=True)
        expo = jnp.exp2((score - peak) * turn_up)
        probs = expo * (1.0 / jnp.sum(expo, axis=1, keepdims=True))
        probs_b = probs.astype(jnp.bfloat16)
        attended = jnp.dot(probs_b, v, preferred_element_type=F32).astype(jnp.bfloat16)
        delta = jnp.sum(da.astype(F32) * attended.astype(F32), axis=1, keepdims=True)
        dscore = (probs * (contract_last(da, v) - delta)).astype(jnp.bfloat16)
        dq = jnp.dot(dscore, k, preferred_element_type=F32) * scale
        dq_ref[rows, :] = dq.astype(jnp.bfloat16)
        dk_part = contract_first(q, dscore)
        dv_part = contract_first(da, probs_b)
        if step == 0:
            dkt[...] = dk_part
            dvt[...] = dv_part
        else:
            dkt[...] += dk_part
            dvt[...] += dv_part
    part = keys // len(outs)
    for i, out in enumerate(outs):
        lanes = slice(i * part, (i + 1) * part)
        out[:, :HEAD] = (dkt[:, lanes] * scale).T.astype(jnp.bfloat16)
        out[:, HEAD:] = dvt[:, lanes].T.astype(jnp.bfloat16)


def attention(q, mine, theirs, blocks, seg):
    queries = q.shape[0]
    keys = sum(block.shape[0] for block in blocks)
    part = jax.ShapeDtypeStruct(blocks[0].shape, jnp.bfloat16)
    return pl.pallas_call(
        functools.partial(attention_kernel, 256, seg),
        out_shape=(jax.ShapeDtypeStruct((queries, HEAD), jnp.bfloat16),) + (part,) * 4,
        in_specs=[VMEM] * 3 + [ANY] * 4,
        out_specs=(VMEM,) * 5,
        scratch_shapes=[
            pltpu.VMEM((keys, 2 * HEAD), jnp.bfloat16),
            pltpu.VMEM((queries, HEAD), jnp.bfloat16),
            pltpu.VMEM((HEAD, keys), F32),
            pltpu.VMEM((HEAD, keys), F32),
            pltpu.SemaphoreType.DMA((4,)),
        ],
        compiler_params=room(36),
        cost_estimate=pl.CostEstimate(
            flops=12 * queries * keys * HEAD,
            bytes_accessed=2 * HEAD * (3 * queries + 4 * keys),
            transcendentals=queries * keys,
        ),
    )(q, mine, theirs, *blocks)


def unproject_kernel(seg, dq_ref, *refs):
    parts, weight, swap_ref, outs, (w_in, sems) = refs[:4], refs[4], refs[5], refs[6:10], refs[10:]
    depth = weight.shape[1]
    fetched(
        [
            (weight.at[i, :, : 3 * HEAD], w_in.at[i * depth : (i + 1) * depth, :])
            for i in range(weight.shape[0])
        ],
        sems,
    )
    dkv = sum(ref[...].astype(F32) for ref in parts).astype(jnp.bfloat16)
    left = jnp.concatenate([dq_ref[...], dkv], axis=1)
    out = contract_last(left, w_in[...])
    for i, slot in enumerate((1, 4, 5, 7)):
        swap_ref[i * seg : (i + 1) * seg, :] = out[slot * seg : (slot + 1) * seg].astype(WIRE)
    for ref, slot in zip(outs, (0, 2, 3, 6)):
        ref[...] = out[slot * seg : (slot + 1) * seg]


def unproject(dq, parts, weights, seg):
    width = weights.shape[0] * weights.shape[1]
    return pl.pallas_call(
        functools.partial(unproject_kernel, seg),
        out_shape=(jax.ShapeDtypeStruct((4 * seg, width), WIRE),)
        + (jax.ShapeDtypeStruct((seg, width), F32),) * 4,
        in_specs=[VMEM] * 5 + [ANY],
        out_specs=(VMEM,) * 5,
        scratch_shapes=[
            pltpu.VMEM((width, 3 * HEAD), jnp.bfloat16),
            pltpu.SemaphoreType.DMA((weights.shape[0],)),
        ],
        compiler_params=room(16),
    )(dq, *parts, weights)


def join_kernel(swapped, own, near, next_to, far, own_out, near_out, next_out, far_out):
    seg = own.shape[0]
    own_out[...] = own[...] + swapped[:seg, :].astype(F32)
    near_out[...] = near[...] + swapped[seg : 2 * seg, :].astype(F32)
    next_out[...] = (next_to[...] + swapped[2 * seg : 3 * seg, :].astype(F32)).astype(WIRE)
    far_out[...] = (far[...] + swapped[3 * seg :, :].astype(F32)).astype(WIRE)


def joined(swapped, own, near, next_to, far):
    wide = jax.ShapeDtypeStruct(own.shape, F32)
    thin = jax.ShapeDtypeStruct(own.shape, WIRE)
    return pl.pallas_call(
        join_kernel,
        out_shape=(wide, wide, thin, thin),
        in_specs=[VMEM] * 5,
        out_specs=(VMEM,) * 4,
        compiler_params=room(6),
    )(swapped, own, near, next_to, far)


def summed_rows(swap, own, near, next_to, far):
    own, near, next_to, far = joined(other_core(swap), own, near, next_to, far)
    far = turned(far, -1).astype(F32)
    next_to = turned_over(next_to).astype(F32)
    near = turned((near + far).astype(WIRE), -1).astype(F32)
    return own + next_to + near


def per_device(tokens, starts, gain, w_query, w_key, w_value, w_out, cotangent):
    token_rows = tokens[0]
    grad_out = cotangent[0]
    rows, width = token_rows.shape
    seg = starts.shape[1]
    length = rows * CTX
    ctx, core = lax.axis_index("ctx"), here()[3]

    mine, own_starts = cut_weights(w_query, w_key, w_value, w_out, starts)
    weights = gathered_weights(mine)
    beside, facing = other_core(own_starts), other_chip(own_starts)
    to_core, to_chip, mid_token, mid_grad, first = window_sums(
        own_starts, beside, facing, token_rows, grad_out
    )
    before = jnp.where(core == 0, facing, beside)[0]
    after = jnp.where(core == 0, beside, facing)[0]
    before = jnp.where(ctx == 0, -1, before)
    after = jnp.where(ctx == CTX - 1, length, after)
    stop = jnp.full((1,), length, jnp.int32)
    window = jnp.concatenate([before, own_starts[0], after, stop])
    opens, ends = window[:-1], window[1:]
    count = (ends - opens)[seg : 2 * seg, None].astype(F32)
    second = two_back(first)
    both, normed, rms, dout = norm(
        other_core(to_core), other_chip(to_chip), mid_token, mid_grad, second, count, gain[None]
    )
    q, own, mine, theirs = project(gathered_rows(both), weights)
    cross, far, beside = across(own, 0, True), across(own, 0, False), other_pair(own)
    theirs = other_core(theirs)
    blocks = (own, beside, far, cross)
    dq, own, beside, far, cross = attention(q, mine, theirs, blocks, seg)
    parts = (own, other_pair(beside), across(far, 1, False), across(cross, 1, True))
    dnormin = summed_rows(*unproject(dq, parts, weights, seg))

    scaled = dnormin * gain
    dpooled = dout + (scaled - normed * jnp.mean(scaled * normed, axis=-1, keepdims=True)) / rms
    per_seg = (dpooled / count).astype(WIRE)
    beside, facing = other_core(per_seg), other_chip(per_seg)
    before = jnp.where(core == 0, facing, beside)
    after = jnp.where(core == 0, beside, facing)
    per_window = jnp.concatenate([before, per_seg, after], axis=0)
    positions = (ctx * rows + lax.iota(jnp.int32, rows))[:, None]
    member = (opens[None] <= positions) & (positions < ends[None])
    spread = jnp.dot(member.astype(WIRE), per_window, preferred_element_type=F32)
    return (grad_out.astype(F32) + spread).astype(jnp.bfloat16)[None]


def solution(mesh):
    return jax.shard_map(
        per_device,
        mesh=mesh,
        in_specs=(
            P("dp", "ctx", None),
            P("dp", "ctx"),
            P(),
            P("dp", None),
            P("dp", None),
            P("dp", None),
            P("dp", None),
            P("dp", "ctx", None),
        ),
        out_specs=P("dp", "ctx", None),
        check_vma=False,
    )
```

```python
import functools
import math

import jax
import jax.numpy as jnp
from jax import lax
from jax.experimental import pallas as pl
from jax.experimental.pallas import tpu as pltpu
from jax.sharding import PartitionSpec as P

HEAD = 128
HALVES, TURNS, PAIR, CORES = 2, 4, 2, 2
CTX = HALVES * TURNS * PAIR * CORES
ROWS_X, ROWS_Y = 2, 4
NEG = -1e30
WIRE = jnp.bfloat16
F32 = jnp.float32
VMEM = pl.BlockSpec(memory_space=pltpu.VMEM)
ANY = pl.BlockSpec(memory_space=pl.ANY)
HBM = pl.BlockSpec(memory_space=pltpu.HBM)


def room(mib):
    return pltpu.CompilerParams(vmem_limit_bytes=mib * 1024 * 1024)


def place(half, turn, pair, core):
    return ((half * TURNS + turn % TURNS) * PAIR + pair) * CORES + core


def here():
    ctx = lax.axis_index("ctx")
    core, pair = ctx % CORES, ctx // CORES % PAIR
    return ctx // (CORES * PAIR * TURNS), ctx // (CORES * PAIR) % TURNS, pair, core


def moved(value, to):
    spots = [
        (h, t, p, k)
        for h in range(HALVES)
        for t in range(TURNS)
        for p in range(PAIR)
        for k in range(CORES)
    ]
    pairs = [(place(*s), place(*to(*s))) for s in spots if to(*s) is not None]
    return lax.ppermute(value, "ctx", pairs)


def other_chip(value):
    pairs = [(i, i + 1 if i % CORES else i - 1) for i in range(1, CTX - 1)]
    return lax.ppermute(value, "ctx", pairs)


def two_back(value):
    return lax.ppermute(value, "ctx", [(i, i - CORES) for i in range(CORES, CTX)])


def other_core(value):
    return moved(value, lambda h, t, p, k: (h, t, p, 1 - k))


def other_pair(value):
    return moved(value, lambda h, t, p, k: (h, t, 1 - p, k))


def across(value, source, cross):
    return moved(
        value,
        lambda h, t, p, k: (1 - h, t, 1 - p if cross else p, k) if h == source else None,
    )


def turned(value, way):
    return moved(value, lambda h, t, p, k: (h, t + way * (1 - 2 * k), p, k))


def turned_over(value):
    return moved(value, lambda h, t, p, k: (h, t - (1 - 2 * k), p, 1 - k))


def contract_last(left, right):
    return lax.dot_general(left, right, (((1,), (1,)), ((), ())), preferred_element_type=F32)


def contract_first(left, right):
    return lax.dot_general(left, right, (((0,), (0,)), ((), ())), preferred_element_type=F32)


def cut_kernel(q_ref, k_ref, v_ref, o_ref, start_ref, out_ref, half_ref, start_out, sems):
    _, turn, _, core = here()
    lane = pl.multiple_of((turn * CORES + core) * HEAD, HEAD)
    copies = [
        (w.at[:, pl.ds(lane, HEAD)], out_ref.at[:, i * HEAD : (i + 1) * HEAD])
        for i, w in enumerate((q_ref, k_ref, v_ref))
    ]
    half = half_ref.shape[0]
    copies.append((o_ref.at[pl.ds(pl.multiple_of(core * half, half), half), :], half_ref))
    copies.append((start_ref, start_out))
    fetched(copies, sems)


def cut_weights(w_query, w_key, w_value, w_out, starts):
    rows, width = w_out.shape
    return pl.pallas_call(
        cut_kernel,
        out_shape=(
            jax.ShapeDtypeStruct((rows, 3 * HEAD), w_query.dtype),
            jax.ShapeDtypeStruct((rows // CORES, width), w_out.dtype),
            jax.ShapeDtypeStruct(starts.shape, starts.dtype),
        ),
        in_specs=[HBM] * 4 + [ANY],
        out_specs=(VMEM, VMEM, VMEM),
        scratch_shapes=[pltpu.SemaphoreType.DMA((5,))],
        compiler_params=room(60),
    )(w_query, w_key, w_value, w_out, starts)


def other_x(value):
    count = ROWS_X * ROWS_Y
    return lax.ppermute(value, "dp", [(d, (d + ROWS_Y) % count) for d in range(count)])


def shifted_y(value, step):
    pairs = [(d, d // ROWS_Y * ROWS_Y + (d + step) % ROWS_Y) for d in range(ROWS_X * ROWS_Y)]
    return lax.ppermute(value, "dp", pairs)


def gathered_halves(half):
    return lax.all_gather(half, "dp", axis=0, tiled=False)


def pass_kernel(value_ref, *refs):
    refs[-1][...] = value_ref[...]


def passed_on(value, *ready):
    return pl.pallas_call(
        pass_kernel,
        out_shape=jax.ShapeDtypeStruct(value.shape, value.dtype),
        in_specs=[VMEM] + [ANY] * len(ready),
        out_specs=VMEM,
        compiler_params=room(4),
    )(value, *ready)


def gathered_rows(shard, first_ready, last_ready):
    near = turned(shard, 1)
    next_to = turned_over(passed_on(shard, near))
    far = passed_on(turned(passed_on(near, *first_ready), 1), *last_ready)
    return [
        shard,
        other_core(shard),
        near,
        next_to,
        other_core(near),
        other_core(next_to),
        far,
        other_core(far),
    ]


def rows_at(row, half, turn, pair, core, seg):
    slot = row // seg
    two = slot // 2
    way = 1 - 2 * core
    step = jnp.where(two == 0, 0, jnp.where(two == 1, way, jnp.where(two == 2, -way, 2)))
    flip = jnp.where(two == 2, 1 - slot % 2, slot % 2)
    its_core = jnp.where(flip == 1, 1 - core, core)
    its_turn = (turn - step + TURNS) % TURNS
    return place(half, its_turn, pair, its_core) * seg + row % seg


def fetched(copies, sems):
    started = []
    for i, (source, target) in enumerate(copies):
        started.append(pltpu.make_async_copy(source, target, sems.at[i]))
        started[-1].start()
    for copy in started:
        copy.wait()


def stacked(pieces, out_ref):
    copies, at = [], 0
    for piece in pieces:
        copies.append((piece, out_ref.at[at : at + piece.shape[0], :]))
        at += piece.shape[0]
    return copies


def window_kernel(own_ref, beside_ref, facing_ref, token_hbm, grad_hbm, *refs):
    core_ref, chip_ref, mid_token, mid_grad, first_ref = refs[:5]
    token_ref, grad_ref, sems = refs[5:]
    rows, width = token_ref.shape
    seg = mid_token.shape[0]
    token_copy = pltpu.make_async_copy(token_hbm, token_ref, sems.at[0])
    grad_copy = pltpu.make_async_copy(grad_hbm, grad_ref, sems.at[1])
    token_copy.start()
    grad_copy.start()
    ctx, core = lax.axis_index("ctx"), here()[3]
    at = lax.broadcasted_iota(jnp.int32, (rows, 1), 0) + ctx * rows
    before = jnp.where(core == 0, facing_ref[...], beside_ref[...])
    after = jnp.where(core == 0, beside_ref[...], facing_ref[...])
    before = jnp.where(ctx == 0, -1, before)
    after = jnp.where(ctx == CTX - 1, rows * CTX, after)
    begun = [(part <= at).astype(jnp.int32) for part in (before, own_ref[...], after)]
    slot = sum(jnp.sum(part, axis=1, keepdims=True) for part in begun) - 1
    slots = lax.broadcasted_iota(jnp.int32, (1, 3 * seg), 1)
    member = (slots == slot).astype(jnp.bfloat16)
    earlier = (slots == slot - 1).astype(jnp.bfloat16)
    token_copy.wait()
    token = contract_first(member, token_ref[...])
    grad_copy.wait()
    grad = contract_first(earlier, grad_ref[...])
    outside = jnp.broadcast_to((slot == 0).astype(jnp.bfloat16), (rows, HEAD))
    first_ref[...] = contract_first(outside, grad_ref[...])[:1]
    mid_token[...] = token[seg : 2 * seg]
    mid_grad[...] = grad[seg : 2 * seg]

    def send(lower_ref, upper_ref):
        lower_ref[:, :width] = token[:seg].astype(WIRE)
        lower_ref[:, width:] = grad[:seg].astype(WIRE)
        upper_ref[:, :width] = token[2 * seg :].astype(WIRE)
        upper_ref[:, width:] = grad[2 * seg :].astype(WIRE)

    @pl.when(core == 0)
    def _():
        send(chip_ref, core_ref)

    @pl.when(core == 1)
    def _():
        send(core_ref, chip_ref)


def window_sums(own, beside, facing, tokens, grads):
    rows, width = tokens.shape
    seg = own.shape[1]
    shape = jax.ShapeDtypeStruct
    return pl.pallas_call(
        window_kernel,
        out_shape=(
            shape((seg, 2 * width), WIRE),
            shape((seg, 2 * width), WIRE),
            shape((seg, width), F32),
            shape((seg, width), F32),
            shape((1, width), F32),
        ),
        in_specs=[VMEM] * 3 + [HBM] * 2,
        out_specs=(VMEM,) * 5,
        scratch_shapes=[
            pltpu.VMEM((rows, width), tokens.dtype),
            pltpu.VMEM((rows, width), grads.dtype),
            pltpu.SemaphoreType.DMA((2,)),
        ],
        compiler_params=room(16),
    )(own, beside, facing, tokens, grads)


def norm_kernel(core_ref, chip_ref, mid_token, mid_grad, count_ref, gain_ref, *refs):
    mine_ref, theirs_ref, normin_ref, normed_ref, rms_ref, dout_ref, pair_ref = refs
    width = mid_token.shape[1]
    rows = mine_ref.shape[0]
    pair_ref[:rows, :] = mine_ref[...]
    pair_ref[rows:, :] = theirs_ref[...]
    got = core_ref[...].astype(F32) + chip_ref[...].astype(F32)
    pooled = (mid_token[...] + got[:, :width]) / count_ref[...]
    rms = jnp.sqrt(jnp.mean(pooled * pooled, axis=1, keepdims=True) + 1e-06)
    normed = pooled / rms
    normed_ref[...] = normed
    rms_ref[...] = rms
    normin_ref[...] = (normed * gain_ref[...]).astype(jnp.bfloat16)
    dout_ref[...] = mid_grad[...] + got[:, width:]


def norm(from_core, from_chip, mid_token, mid_grad, count, gain, mine, theirs):
    seg, width = mid_token.shape
    shape = jax.ShapeDtypeStruct
    return pl.pallas_call(
        norm_kernel,
        out_shape=(
            shape((seg, width), jnp.bfloat16),
            shape((seg, width), F32),
            shape((seg, 1), F32),
            shape((seg, width), F32),
            shape((2 * mine.shape[0], mine.shape[1]), mine.dtype),
        ),
        in_specs=[VMEM] * 8,
        out_specs=(VMEM,) * 5,
        compiler_params=room(8),
    )(from_core, from_chip, mid_token, mid_grad, count, gain, mine, theirs)


def dout_kernel(dout_ref, second_ref, ready_ref, full_ref, half_ref):
    seg = dout_ref.shape[0]
    last = lax.broadcasted_iota(jnp.int32, (seg, 1), 0) == seg - 1
    dout = dout_ref[...] + jnp.where(last, second_ref[...], 0.0)
    full_ref[...] = dout
    half_ref[...] = dout.astype(jnp.bfloat16)


def whole_dout(dout, second, ready):
    shape = jax.ShapeDtypeStruct
    return pl.pallas_call(
        dout_kernel,
        out_shape=(shape(dout.shape, F32), shape(dout.shape, jnp.bfloat16)),
        in_specs=[VMEM, VMEM, ANY],
        out_specs=(VMEM, VMEM),
        compiler_params=room(4),
    )(dout, second, ready)


def dattended_kernel(own_ref, other_ref, weight_ref, ready_ref, *refs):
    outs, rows, weight, sems = refs[:TURNS], *refs[TURNS:]
    heads, half = weight_ref.shape[:2]
    copies = stacked([own_ref, other_ref], rows)
    copies += [(weight_ref.at[i], weight.at[i * half : (i + 1) * half, :]) for i in range(heads)]
    fetched(copies, sems)
    turn = here()[1]
    for step, out in enumerate(outs):
        at = pl.multiple_of((turn + step) % TURNS * CORES * half, CORES * half)
        part = weight[pl.ds(at, CORES * half), :]
        out[...] = contract_last(rows[...], part).astype(jnp.bfloat16)


def dattended(own, other, halves, ready):
    heads, half, width = halves.shape
    rows = 2 * own.shape[0]
    return pl.pallas_call(
        dattended_kernel,
        out_shape=(jax.ShapeDtypeStruct((rows, CORES * half), jnp.bfloat16),) * TURNS,
        in_specs=[ANY] * 4,
        out_specs=(VMEM,) * TURNS,
        scratch_shapes=[
            pltpu.VMEM((rows, width), jnp.bfloat16),
            pltpu.VMEM((heads * half, width), jnp.bfloat16),
            pltpu.SemaphoreType.DMA((2 + heads,)),
        ],
        compiler_params=room(12),
    )(own, other, halves, ready)


def project_kernel(*refs):
    pieces, weights = refs[:8], refs[8:12]
    q_ref, kv_ref, w_ref, rows, sems = refs[12:]
    copies = stacked(pieces, rows)
    dp = lax.axis_index("dp")
    x, y = dp // ROWS_Y, dp % ROWS_Y
    depth = weights[0].shape[0] // ROWS_X
    for weight, step in zip(weights, (0, 1, -1, 2)):
        its_y = (y - step + ROWS_Y) % ROWS_Y
        for i in range(ROWS_X):
            its_x = x if i == 0 else 1 - x
            at = pl.multiple_of((its_x * ROWS_Y + its_y) * depth, depth)
            copies.append((weight.at[i * depth : (i + 1) * depth, :], w_ref.at[pl.ds(at, depth), :]))
    fetched(copies, sems)
    out = jnp.dot(rows[...], w_ref[...], preferred_element_type=F32).astype(jnp.bfloat16)
    q_ref[...] = out[:, :HEAD]
    kv_ref[...] = out[:, HEAD:]


def project(pieces, weights):
    seg, width = pieces[0].shape
    rows = seg * len(pieces)
    bf16 = lambda *shape: jax.ShapeDtypeStruct(shape, jnp.bfloat16)
    return pl.pallas_call(
        project_kernel,
        out_shape=(bf16(rows, HEAD), bf16(rows, 2 * HEAD), bf16(width, 3 * HEAD)),
        in_specs=[ANY] * 12,
        out_specs=(VMEM,) * 3,
        scratch_shapes=[
            pltpu.VMEM((rows, width), jnp.bfloat16),
            pltpu.SemaphoreType.DMA((16,)),
        ],
        compiler_params=room(12),
    )(*pieces, *weights)


def place_dattended(core, seg, here_refs, there_refs, out_ref):
    half = out_ref.shape[1] // CORES
    mine = slice(core * half, (core + 1) * half)
    other = slice((1 - core) * half, (2 - core) * half)
    slots = ((0, 1), (2, 3), (6, 7), (5, 4)) if core == 0 else ((0, 1), (5, 4), (6, 7), (2, 3))
    for refs in zip(here_refs, there_refs, slots):
        for i, slot in enumerate(refs[2]):
            rows = slice(slot * seg, (slot + 1) * seg)
            out_ref[rows, mine] = refs[0][i * seg : (i + 1) * seg, mine]
            out_ref[rows, other] = refs[1][(1 - i) * seg : (2 - i) * seg, mine]


def attention_kernel(tile, seg, *refs):
    q_ref, here_refs, there_refs, blocks = refs[0], refs[1:5], refs[5:9], refs[9:13]
    dq_ref, outs, (kv, da_ref, dkt, dvt, sems) = refs[13], refs[14:18], refs[18:]
    half, turn, pair, core = here()
    queries, keys = q_ref.shape[0], kv.shape[0]
    fetched(stacked(blocks, kv), sems)

    for which in range(CORES):

        @pl.when(core == which)
        def _(which=which):
            place_dattended(which, seg, here_refs, there_refs, da_ref)

    spot = lax.broadcasted_iota(jnp.int32, (1, keys), 1)
    block = spot // queries
    key_half = jnp.where(block < 2, half, 1 - half)
    key_pair = jnp.where(block % 2 == 0, pair, 1 - pair)
    key_at = rows_at(spot % queries, key_half, turn, key_pair, core, seg)
    turn_up = math.log2(math.e) / math.sqrt(HEAD)
    scale = 1.0 / math.sqrt(HEAD)
    k = kv[:, :HEAD]
    v = kv[:, HEAD:]
    for step in range(queries // tile):
        rows = slice(step * tile, (step + 1) * tile)
        query = lax.broadcasted_iota(jnp.int32, (tile, 1), 0) + step * tile
        query_at = rows_at(query, half, turn, pair, core, seg)
        q = q_ref[rows, :]
        da = da_ref[rows, :]
        score = jnp.where(key_at <= query_at, contract_last(q, k), NEG)
        peak = jnp.max(score, axis=1, keepdims=True)
        expo = jnp.exp2((score - peak) * turn_up)
        probs = expo * (1.0 / jnp.sum(expo, axis=1, keepdims=True))
        probs_b = probs.astype(jnp.bfloat16)
        attended = jnp.dot(probs_b, v, preferred_element_type=F32).astype(jnp.bfloat16)
        delta = jnp.sum(da.astype(F32) * attended.astype(F32), axis=1, keepdims=True)
        dscore = (probs * (contract_last(da, v) - delta)).astype(jnp.bfloat16)
        dq = jnp.dot(dscore, k, preferred_element_type=F32) * scale
        dq_ref[rows, :] = dq.astype(jnp.bfloat16)
        dk_part = contract_first(q, dscore)
        dv_part = contract_first(da, probs_b)
        if step == 0:
            dkt[...] = dk_part
            dvt[...] = dv_part
        else:
            dkt[...] += dk_part
            dvt[...] += dv_part
    part = keys // len(outs)
    for i, out in enumerate(outs):
        lanes = slice(i * part, (i + 1) * part)
        out[:, :HEAD] = (dkt[:, lanes] * scale).T.astype(jnp.bfloat16)
        out[:, HEAD:] = dvt[:, lanes].T.astype(jnp.bfloat16)


def attention(q, da_here, da_there, blocks, seg):
    queries = q.shape[0]
    keys = sum(block.shape[0] for block in blocks)
    part = jax.ShapeDtypeStruct(blocks[0].shape, jnp.bfloat16)
    return pl.pallas_call(
        functools.partial(attention_kernel, 256, seg),
        out_shape=(jax.ShapeDtypeStruct((queries, HEAD), jnp.bfloat16),) + (part,) * 4,
        in_specs=[VMEM] * 9 + [ANY] * 4,
        out_specs=(VMEM,) * 5,
        scratch_shapes=[
            pltpu.VMEM((keys, 2 * HEAD), jnp.bfloat16),
            pltpu.VMEM((queries, HEAD), jnp.bfloat16),
            pltpu.VMEM((HEAD, keys), F32),
            pltpu.VMEM((HEAD, keys), F32),
            pltpu.SemaphoreType.DMA((4,)),
        ],
        compiler_params=room(36),
        cost_estimate=pl.CostEstimate(
            flops=12 * queries * keys * HEAD,
            bytes_accessed=2 * HEAD * (3 * queries + 4 * keys),
            transcendentals=queries * keys,
        ),
    )(q, *da_here, *da_there, *blocks)


def unproject_kernel(seg, dq_ref, *refs):
    parts, w_ref, swap_ref, outs = refs[:4], refs[4], refs[5], refs[6:]
    dkv = sum(ref[...].astype(F32) for ref in parts).astype(jnp.bfloat16)
    left = jnp.concatenate([dq_ref[...], dkv], axis=1)
    out = contract_last(left, w_ref[...])
    for i, slot in enumerate((1, 4, 5, 7)):
        swap_ref[i * seg : (i + 1) * seg, :] = out[slot * seg : (slot + 1) * seg].astype(WIRE)
    for ref, slot in zip(outs, (0, 2, 3, 6)):
        ref[...] = out[slot * seg : (slot + 1) * seg]


def unproject(dq, parts, w_full, seg):
    width = w_full.shape[0]
    return pl.pallas_call(
        functools.partial(unproject_kernel, seg),
        out_shape=(jax.ShapeDtypeStruct((4 * seg, width), WIRE),)
        + (jax.ShapeDtypeStruct((seg, width), F32),) * 4,
        in_specs=[VMEM] * 6,
        out_specs=(VMEM,) * 5,
        compiler_params=room(16),
    )(dq, *parts, w_full)


def join_kernel(swapped, own, near, next_to, far, own_out, near_out, next_out, far_out):
    seg = own.shape[0]
    own_out[...] = own[...] + swapped[:seg, :].astype(F32)
    near_out[...] = near[...] + swapped[seg : 2 * seg, :].astype(F32)
    next_out[...] = (next_to[...] + swapped[2 * seg : 3 * seg, :].astype(F32)).astype(WIRE)
    far_out[...] = (far[...] + swapped[3 * seg :, :].astype(F32)).astype(WIRE)


def joined(swapped, own, near, next_to, far):
    wide = jax.ShapeDtypeStruct(own.shape, F32)
    thin = jax.ShapeDtypeStruct(own.shape, WIRE)
    return pl.pallas_call(
        join_kernel,
        out_shape=(wide, wide, thin, thin),
        in_specs=[VMEM] * 5,
        out_specs=(VMEM,) * 4,
        compiler_params=room(6),
    )(swapped, own, near, next_to, far)


def summed_rows(swap, own, near, next_to, far):
    own, near, next_to, far = joined(other_core(swap), own, near, next_to, far)
    far = turned(far, -1).astype(F32)
    next_to = turned_over(next_to).astype(F32)
    near = turned((near + far).astype(WIRE), -1).astype(F32)
    return own + next_to + near


def per_device(tokens, starts, gain, w_query, w_key, w_value, w_out, cotangent):
    token_rows = tokens[0]
    grad_out = cotangent[0]
    rows, width = token_rows.shape
    seg = starts.shape[1]
    length = rows * CTX
    ctx, core = lax.axis_index("ctx"), here()[3]

    mine, half, own_starts = cut_weights(w_query, w_key, w_value, w_out, starts)
    halves = gathered_halves(half)
    theirs = other_x(mine)
    beside, facing = other_core(own_starts), other_chip(own_starts)
    to_core, to_chip, mid_token, mid_grad, first = window_sums(
        own_starts, beside, facing, token_rows, grad_out
    )
    before = jnp.where(core == 0, facing, beside)[0]
    after = jnp.where(core == 0, beside, facing)[0]
    before = jnp.where(ctx == 0, -1, before)
    after = jnp.where(ctx == CTX - 1, length, after)
    stop = jnp.full((1,), length, jnp.int32)
    window = jnp.concatenate([before, own_starts[0], after, stop])
    opens, ends = window[:-1], window[1:]
    count = (ends - opens)[seg : 2 * seg, None].astype(F32)
    second = two_back(first)
    normin, normed, rms, dout, both = norm(
        other_core(to_core), other_chip(to_chip), mid_token, mid_grad, count, gain[None], mine, theirs
    )
    weights = [both, shifted_y(both, 1), shifted_y(both, -1), shifted_y(both, 2)]
    pieces = gathered_rows(normin, weights[1:3], weights[3:])
    q, own, w_full = project(pieces, weights)
    cross, far, beside = across(own, 0, True), across(own, 0, False), other_pair(own)
    dout, dout_b = whole_dout(dout, second, pieces[2])
    da = dattended(dout_b, other_core(dout_b), halves, beside)
    da_here = [da[0]] + [
        moved(da[i], lambda h, t, p, k, i=i: (h, t + i, p, k)) for i in range(1, TURNS)
    ]
    da_there = [other_core(piece) for piece in da_here]
    blocks = (own, beside, far, cross)
    dq, own, beside, far, cross = attention(q, da_here, da_there, blocks, seg)
    parts = (own, other_pair(beside), across(far, 1, False), across(cross, 1, True))
    dnormin = summed_rows(*unproject(dq, parts, w_full, seg))

    scaled = dnormin * gain
    dpooled = dout + (scaled - normed * jnp.mean(scaled * normed, axis=-1, keepdims=True)) / rms
    per_seg = (dpooled / count).astype(WIRE)
    beside, facing = other_core(per_seg), other_chip(per_seg)
    before = jnp.where(core == 0, facing, beside)
    after = jnp.where(core == 0, beside, facing)
    per_window = jnp.concatenate([before, per_seg, after], axis=0)
    positions = (ctx * rows + lax.iota(jnp.int32, rows))[:, None]
    member = (opens[None] <= positions) & (positions < ends[None])
    spread = jnp.dot(member.astype(WIRE), per_window, preferred_element_type=F32)
    return (grad_out.astype(F32) + spread).astype(jnp.bfloat16)[None]


def solution(mesh):
    return jax.shard_map(
        per_device,
        mesh=mesh,
        in_specs=(
            P("dp", "ctx", None),
            P("dp", "ctx"),
            P(),
            P("dp", None),
            P("dp", None),
            P("dp", None),
            P("dp", None),
            P("dp", "ctx", None),
        ),
        out_specs=P("dp", "ctx", None),
        check_vma=False,
    )
```

```python
import functools
import math

import jax
import jax.numpy as jnp
from jax import lax
from jax.experimental import pallas as pl
from jax.experimental.pallas import tpu as pltpu
from jax.sharding import PartitionSpec as P

HEAD = 128
HALVES, TURNS, PAIR, CORES = 2, 4, 2, 2
CTX = HALVES * TURNS * PAIR * CORES
ROWS_X, ROWS_Y = 2, 4
NEG = -1e30
WIRE = jnp.bfloat16
F32 = jnp.float32
VMEM = pl.BlockSpec(memory_space=pltpu.VMEM)
ANY = pl.BlockSpec(memory_space=pl.ANY)
HBM = pl.BlockSpec(memory_space=pltpu.HBM)


def room(mib):
    return pltpu.CompilerParams(vmem_limit_bytes=mib * 1024 * 1024)


def place(half, turn, pair, core):
    return ((half * TURNS + turn % TURNS) * PAIR + pair) * CORES + core


def here():
    ctx = lax.axis_index("ctx")
    core, pair = ctx % CORES, ctx // CORES % PAIR
    return ctx // (CORES * PAIR * TURNS), ctx // (CORES * PAIR) % TURNS, pair, core


def moved(value, to):
    spots = [
        (h, t, p, k)
        for h in range(HALVES)
        for t in range(TURNS)
        for p in range(PAIR)
        for k in range(CORES)
    ]
    pairs = [(place(*s), place(*to(*s))) for s in spots if to(*s) is not None]
    return lax.ppermute(value, "ctx", pairs)


def other_chip(value):
    pairs = [(i, i + 1 if i % CORES else i - 1) for i in range(1, CTX - 1)]
    return lax.ppermute(value, "ctx", pairs)


def two_back(value):
    return lax.ppermute(value, "ctx", [(i, i - CORES) for i in range(CORES, CTX)])


def other_core(value):
    return moved(value, lambda h, t, p, k: (h, t, p, 1 - k))


def other_pair(value):
    return moved(value, lambda h, t, p, k: (h, t, 1 - p, k))


def across(value, source, cross):
    return moved(
        value,
        lambda h, t, p, k: (1 - h, t, 1 - p if cross else p, k) if h == source else None,
    )


def turned(value, way):
    return moved(value, lambda h, t, p, k: (h, t + way * (1 - 2 * k), p, k))


def turned_over(value):
    return moved(value, lambda h, t, p, k: (h, t - (1 - 2 * k), p, 1 - k))


def contract_last(left, right):
    return lax.dot_general(left, right, (((1,), (1,)), ((), ())), preferred_element_type=F32)


def contract_first(left, right):
    return lax.dot_general(left, right, (((0,), (0,)), ((), ())), preferred_element_type=F32)


def cut_kernel(q_ref, k_ref, v_ref, o_ref, start_ref, out_ref, half_ref, start_out, sems):
    _, turn, _, core = here()
    lane = pl.multiple_of((turn * CORES + core) * HEAD, HEAD)
    copies = [
        (w.at[:, pl.ds(lane, HEAD)], out_ref.at[:, i * HEAD : (i + 1) * HEAD])
        for i, w in enumerate((q_ref, k_ref, v_ref))
    ]
    half = half_ref.shape[0]
    copies.append((o_ref.at[pl.ds(pl.multiple_of(core * half, half), half), :], half_ref))
    copies.append((start_ref, start_out))
    fetched(copies, sems)


def cut_weights(w_query, w_key, w_value, w_out, starts):
    rows, width = w_out.shape
    return pl.pallas_call(
        cut_kernel,
        out_shape=(
            jax.ShapeDtypeStruct((rows, 3 * HEAD), w_query.dtype),
            jax.ShapeDtypeStruct((rows // CORES, width), w_out.dtype),
            jax.ShapeDtypeStruct(starts.shape, starts.dtype),
        ),
        in_specs=[HBM] * 4 + [ANY],
        out_specs=(VMEM, VMEM, VMEM),
        scratch_shapes=[pltpu.SemaphoreType.DMA((5,))],
        compiler_params=room(60),
    )(w_query, w_key, w_value, w_out, starts)


def other_x(value):
    count = ROWS_X * ROWS_Y
    return lax.ppermute(value, "dp", [(d, (d + ROWS_Y) % count) for d in range(count)])


def shifted_y(value, step):
    pairs = [(d, d // ROWS_Y * ROWS_Y + (d + step) % ROWS_Y) for d in range(ROWS_X * ROWS_Y)]
    return lax.ppermute(value, "dp", pairs)


def gathered_halves(half):
    return lax.all_gather(half, "dp", axis=0, tiled=False)


def pass_kernel(value_ref, *refs):
    refs[-1][...] = value_ref[...]


def passed_on(value, *ready):
    return pl.pallas_call(
        pass_kernel,
        out_shape=jax.ShapeDtypeStruct(value.shape, value.dtype),
        in_specs=[VMEM] + [ANY] * len(ready),
        out_specs=VMEM,
        compiler_params=room(4),
    )(value, *ready)


def gathered_rows(shard, first_ready, last_ready):
    near = turned(shard, 1)
    next_to = turned_over(passed_on(shard, near))
    far = passed_on(turned(passed_on(near, *first_ready), 1), *last_ready)
    return [
        shard,
        other_core(shard),
        near,
        next_to,
        other_core(near),
        other_core(next_to),
        far,
        other_core(far),
    ]


def rows_at(row, half, turn, pair, core, seg):
    slot = row // seg
    two = slot // 2
    way = 1 - 2 * core
    step = jnp.where(two == 0, 0, jnp.where(two == 1, way, jnp.where(two == 2, -way, 2)))
    flip = jnp.where(two == 2, 1 - slot % 2, slot % 2)
    its_core = jnp.where(flip == 1, 1 - core, core)
    its_turn = (turn - step + TURNS) % TURNS
    return place(half, its_turn, pair, its_core) * seg + row % seg


def fetched(copies, sems):
    started = []
    for i, (source, target) in enumerate(copies):
        started.append(pltpu.make_async_copy(source, target, sems.at[i]))
        started[-1].start()
    for copy in started:
        copy.wait()


def stacked(pieces, out_ref):
    copies, at = [], 0
    for piece in pieces:
        copies.append((piece, out_ref.at[at : at + piece.shape[0], :]))
        at += piece.shape[0]
    return copies


def window_kernel(own_ref, beside_ref, facing_ref, token_hbm, grad_hbm, *refs):
    core_ref, chip_ref, mid_token, mid_grad, first_ref = refs[:5]
    token_ref, grad_ref, sems = refs[5:]
    rows, width = token_ref.shape
    seg = mid_token.shape[0]
    token_copy = pltpu.make_async_copy(token_hbm, token_ref, sems.at[0])
    grad_copy = pltpu.make_async_copy(grad_hbm, grad_ref, sems.at[1])
    token_copy.start()
    grad_copy.start()
    ctx, core = lax.axis_index("ctx"), here()[3]
    at = lax.broadcasted_iota(jnp.int32, (rows, 1), 0) + ctx * rows
    before = jnp.where(core == 0, facing_ref[...], beside_ref[...])
    after = jnp.where(core == 0, beside_ref[...], facing_ref[...])
    before = jnp.where(ctx == 0, -1, before)
    after = jnp.where(ctx == CTX - 1, rows * CTX, after)
    begun = [(part <= at).astype(jnp.int32) for part in (before, own_ref[...], after)]
    slot = sum(jnp.sum(part, axis=1, keepdims=True) for part in begun) - 1
    slots = lax.broadcasted_iota(jnp.int32, (1, 3 * seg), 1)
    member = (slots == slot).astype(jnp.bfloat16)
    earlier = (slots == slot - 1).astype(jnp.bfloat16)
    token_copy.wait()
    token = contract_first(member, token_ref[...])
    grad_copy.wait()
    grad = contract_first(earlier, grad_ref[...])
    outside = jnp.broadcast_to((slot == 0).astype(jnp.bfloat16), (rows, HEAD))
    first_ref[...] = contract_first(outside, grad_ref[...])[:1]
    mid_token[...] = token[seg : 2 * seg]
    mid_grad[...] = grad[seg : 2 * seg]

    def send(lower_ref, upper_ref):
        lower_ref[:, :width] = token[:seg].astype(WIRE)
        lower_ref[:, width:] = grad[:seg].astype(WIRE)
        upper_ref[:, :width] = token[2 * seg :].astype(WIRE)
        upper_ref[:, width:] = grad[2 * seg :].astype(WIRE)

    @pl.when(core == 0)
    def _():
        send(chip_ref, core_ref)

    @pl.when(core == 1)
    def _():
        send(core_ref, chip_ref)


def window_sums(own, beside, facing, tokens, grads):
    rows, width = tokens.shape
    seg = own.shape[1]
    shape = jax.ShapeDtypeStruct
    return pl.pallas_call(
        window_kernel,
        out_shape=(
            shape((seg, 2 * width), WIRE),
            shape((seg, 2 * width), WIRE),
            shape((seg, width), F32),
            shape((seg, width), F32),
            shape((1, width), F32),
        ),
        in_specs=[VMEM] * 3 + [HBM] * 2,
        out_specs=(VMEM,) * 5,
        scratch_shapes=[
            pltpu.VMEM((rows, width), tokens.dtype),
            pltpu.VMEM((rows, width), grads.dtype),
            pltpu.SemaphoreType.DMA((2,)),
        ],
        compiler_params=room(16),
    )(own, beside, facing, tokens, grads)


def norm_kernel(core_ref, chip_ref, mid_token, mid_grad, count_ref, gain_ref, *refs):
    mine_ref, theirs_ref = refs[:2]
    normin_ref, normed_ref, rms_ref, dout_ref, pair_ref = refs[-5:]
    width = mid_token.shape[1]
    rows = mine_ref.shape[0]
    pair_ref[:rows, :] = mine_ref[...]
    pair_ref[rows:, :] = theirs_ref[...]
    got = core_ref[...].astype(F32) + chip_ref[...].astype(F32)
    pooled = (mid_token[...] + got[:, :width]) / count_ref[...]
    rms = jnp.sqrt(jnp.mean(pooled * pooled, axis=1, keepdims=True) + 1e-06)
    normed = pooled / rms
    normed_ref[...] = normed
    rms_ref[...] = rms
    normin_ref[...] = (normed * gain_ref[...]).astype(jnp.bfloat16)
    dout_ref[...] = mid_grad[...] + got[:, width:]


def norm(from_core, from_chip, mid_token, mid_grad, count, gain, mine, theirs, ready):
    seg, width = mid_token.shape
    shape = jax.ShapeDtypeStruct
    return pl.pallas_call(
        norm_kernel,
        out_shape=(
            shape((seg, width), jnp.bfloat16),
            shape((seg, width), F32),
            shape((seg, 1), F32),
            shape((seg, width), F32),
            shape((2 * mine.shape[0], mine.shape[1]), mine.dtype),
        ),
        in_specs=[VMEM] * 8 + [ANY],
        out_specs=(VMEM,) * 5,
        compiler_params=room(8),
    )(from_core, from_chip, mid_token, mid_grad, count, gain, mine, theirs, ready)


def dout_kernel(dout_ref, second_ref, full_ref, half_ref):
    seg = dout_ref.shape[0]
    last = lax.broadcasted_iota(jnp.int32, (seg, 1), 0) == seg - 1
    dout = dout_ref[...] + jnp.where(last, second_ref[...], 0.0)
    full_ref[...] = dout
    half_ref[...] = dout.astype(jnp.bfloat16)


def whole_dout(dout, second):
    shape = jax.ShapeDtypeStruct
    return pl.pallas_call(
        dout_kernel,
        out_shape=(shape(dout.shape, F32), shape(dout.shape, jnp.bfloat16)),
        in_specs=[VMEM, VMEM],
        out_specs=(VMEM, VMEM),
        compiler_params=room(4),
    )(dout, second)


def dattended_kernel(own_ref, other_ref, weight_ref, ready_ref, *refs):
    outs, rows, weight, sems = refs[:TURNS], *refs[TURNS:]
    heads, half = weight_ref.shape[:2]
    copies = stacked([own_ref, other_ref], rows)
    copies += [(weight_ref.at[i], weight.at[i * half : (i + 1) * half, :]) for i in range(heads)]
    fetched(copies, sems)
    turn = here()[1]
    for step, out in enumerate(outs):
        at = pl.multiple_of((turn + step) % TURNS * CORES * half, CORES * half)
        part = weight[pl.ds(at, CORES * half), :]
        out[...] = contract_last(rows[...], part).astype(jnp.bfloat16)


def dattended(own, other, halves, ready):
    heads, half, width = halves.shape
    rows = 2 * own.shape[0]
    return pl.pallas_call(
        dattended_kernel,
        out_shape=(jax.ShapeDtypeStruct((rows, CORES * half), jnp.bfloat16),) * TURNS,
        in_specs=[ANY] * 4,
        out_specs=(VMEM,) * TURNS,
        scratch_shapes=[
            pltpu.VMEM((rows, width), jnp.bfloat16),
            pltpu.VMEM((heads * half, width), jnp.bfloat16),
            pltpu.SemaphoreType.DMA((2 + heads,)),
        ],
        compiler_params=room(12),
    )(own, other, halves, ready)


def project_kernel(*refs):
    pieces, weights = refs[:8], refs[8:12]
    q_ref, kv_ref, w_ref, rows, sems = refs[12:]
    copies = stacked(pieces, rows)
    dp = lax.axis_index("dp")
    x, y = dp // ROWS_Y, dp % ROWS_Y
    depth = weights[0].shape[0] // ROWS_X
    for weight, step in zip(weights, (0, 1, -1, 2)):
        its_y = (y - step + ROWS_Y) % ROWS_Y
        for i in range(ROWS_X):
            its_x = x if i == 0 else 1 - x
            at = pl.multiple_of((its_x * ROWS_Y + its_y) * depth, depth)
            copies.append((weight.at[i * depth : (i + 1) * depth, :], w_ref.at[pl.ds(at, depth), :]))
    fetched(copies, sems)
    out = jnp.dot(rows[...], w_ref[...], preferred_element_type=F32).astype(jnp.bfloat16)
    q_ref[...] = out[:, :HEAD]
    kv_ref[...] = out[:, HEAD:]


def project(pieces, weights):
    seg, width = pieces[0].shape
    rows = seg * len(pieces)
    bf16 = lambda *shape: jax.ShapeDtypeStruct(shape, jnp.bfloat16)
    return pl.pallas_call(
        project_kernel,
        out_shape=(bf16(rows, HEAD), bf16(rows, 2 * HEAD), bf16(width, 3 * HEAD)),
        in_specs=[ANY] * 12,
        out_specs=(VMEM,) * 3,
        scratch_shapes=[
            pltpu.VMEM((rows, width), jnp.bfloat16),
            pltpu.SemaphoreType.DMA((16,)),
        ],
        compiler_params=room(12),
    )(*pieces, *weights)


def place_dattended(core, seg, here_refs, there_refs, out_ref):
    half = out_ref.shape[1] // CORES
    mine = slice(core * half, (core + 1) * half)
    other = slice((1 - core) * half, (2 - core) * half)
    slots = ((0, 1), (2, 3), (6, 7), (5, 4)) if core == 0 else ((0, 1), (5, 4), (6, 7), (2, 3))
    for refs in zip(here_refs, there_refs, slots):
        for i, slot in enumerate(refs[2]):
            rows = slice(slot * seg, (slot + 1) * seg)
            out_ref[rows, mine] = refs[0][i * seg : (i + 1) * seg, mine]
            out_ref[rows, other] = refs[1][(1 - i) * seg : (2 - i) * seg, mine]


def attention_kernel(tile, seg, *refs):
    q_ref, here_refs, there_refs, blocks = refs[0], refs[1:5], refs[5:9], refs[9:13]
    dq_ref, outs, (kv, da_ref, dkt, dvt, sems) = refs[13], refs[14:18], refs[18:]
    half, turn, pair, core = here()
    queries, keys = q_ref.shape[0], kv.shape[0]
    fetched(stacked(blocks, kv), sems)

    for which in range(CORES):

        @pl.when(core == which)
        def _(which=which):
            place_dattended(which, seg, here_refs, there_refs, da_ref)

    spot = lax.broadcasted_iota(jnp.int32, (1, keys), 1)
    block = spot // queries
    key_half = jnp.where(block < 2, half, 1 - half)
    key_pair = jnp.where(block % 2 == 0, pair, 1 - pair)
    key_at = rows_at(spot % queries, key_half, turn, key_pair, core, seg)
    turn_up = math.log2(math.e) / math.sqrt(HEAD)
    scale = 1.0 / math.sqrt(HEAD)
    k = kv[:, :HEAD]
    v = kv[:, HEAD:]
    for step in range(queries // tile):
        rows = slice(step * tile, (step + 1) * tile)
        query = lax.broadcasted_iota(jnp.int32, (tile, 1), 0) + step * tile
        query_at = rows_at(query, half, turn, pair, core, seg)
        q = q_ref[rows, :]
        da = da_ref[rows, :]
        score = jnp.where(key_at <= query_at, contract_last(q, k), NEG)
        peak = jnp.max(score, axis=1, keepdims=True)
        expo = jnp.exp2((score - peak) * turn_up)
        probs = expo * (1.0 / jnp.sum(expo, axis=1, keepdims=True))
        probs_b = probs.astype(jnp.bfloat16)
        attended = jnp.dot(probs_b, v, preferred_element_type=F32).astype(jnp.bfloat16)
        delta = jnp.sum(da.astype(F32) * attended.astype(F32), axis=1, keepdims=True)
        dscore = (probs * (contract_last(da, v) - delta)).astype(jnp.bfloat16)
        dq = jnp.dot(dscore, k, preferred_element_type=F32) * scale
        dq_ref[rows, :] = dq.astype(jnp.bfloat16)
        dk_part = contract_first(q, dscore)
        dv_part = contract_first(da, probs_b)
        if step == 0:
            dkt[...] = dk_part
            dvt[...] = dv_part
        else:
            dkt[...] += dk_part
            dvt[...] += dv_part
    part = keys // len(outs)
    for i, out in enumerate(outs):
        lanes = slice(i * part, (i + 1) * part)
        out[:, :HEAD] = (dkt[:, lanes] * scale).T.astype(jnp.bfloat16)
        out[:, HEAD:] = dvt[:, lanes].T.astype(jnp.bfloat16)


def attention(q, da_here, da_there, blocks, seg):
    queries = q.shape[0]
    keys = sum(block.shape[0] for block in blocks)
    part = jax.ShapeDtypeStruct(blocks[0].shape, jnp.bfloat16)
    return pl.pallas_call(
        functools.partial(attention_kernel, 256, seg),
        out_shape=(jax.ShapeDtypeStruct((queries, HEAD), jnp.bfloat16),) + (part,) * 4,
        in_specs=[VMEM] * 9 + [ANY] * 4,
        out_specs=(VMEM,) * 5,
        scratch_shapes=[
            pltpu.VMEM((keys, 2 * HEAD), jnp.bfloat16),
            pltpu.VMEM((queries, HEAD), jnp.bfloat16),
            pltpu.VMEM((HEAD, keys), F32),
            pltpu.VMEM((HEAD, keys), F32),
            pltpu.SemaphoreType.DMA((4,)),
        ],
        compiler_params=room(36),
        cost_estimate=pl.CostEstimate(
            flops=12 * queries * keys * HEAD,
            bytes_accessed=2 * HEAD * (3 * queries + 4 * keys),
            transcendentals=queries * keys,
        ),
    )(q, *da_here, *da_there, *blocks)


def unproject_kernel(seg, dq_ref, *refs):
    parts, w_ref, swap_ref, outs = refs[:4], refs[4], refs[5], refs[6:]
    dkv = sum(ref[...].astype(F32) for ref in parts).astype(jnp.bfloat16)
    left = jnp.concatenate([dq_ref[...], dkv], axis=1)
    out = contract_last(left, w_ref[...])
    for i, slot in enumerate((1, 4, 5, 7)):
        swap_ref[i * seg : (i + 1) * seg, :] = out[slot * seg : (slot + 1) * seg].astype(WIRE)
    for ref, slot in zip(outs, (0, 2, 3, 6)):
        ref[...] = out[slot * seg : (slot + 1) * seg]


def unproject(dq, parts, w_full, seg):
    width = w_full.shape[0]
    return pl.pallas_call(
        functools.partial(unproject_kernel, seg),
        out_shape=(jax.ShapeDtypeStruct((4 * seg, width), WIRE),)
        + (jax.ShapeDtypeStruct((seg, width), F32),) * 4,
        in_specs=[VMEM] * 6,
        out_specs=(VMEM,) * 5,
        compiler_params=room(16),
    )(dq, *parts, w_full)


def join_kernel(swapped, own, near, next_to, far, own_out, near_out, next_out, far_out):
    seg = own.shape[0]
    own_out[...] = own[...] + swapped[:seg, :].astype(F32)
    near_out[...] = near[...] + swapped[seg : 2 * seg, :].astype(F32)
    next_out[...] = (next_to[...] + swapped[2 * seg : 3 * seg, :].astype(F32)).astype(WIRE)
    far_out[...] = (far[...] + swapped[3 * seg :, :].astype(F32)).astype(WIRE)


def joined(swapped, own, near, next_to, far):
    wide = jax.ShapeDtypeStruct(own.shape, F32)
    thin = jax.ShapeDtypeStruct(own.shape, WIRE)
    return pl.pallas_call(
        join_kernel,
        out_shape=(wide, wide, thin, thin),
        in_specs=[VMEM] * 5,
        out_specs=(VMEM,) * 4,
        compiler_params=room(6),
    )(swapped, own, near, next_to, far)


def summed_rows(swap, own, near, next_to, far):
    own, near, next_to, far = joined(other_core(swap), own, near, next_to, far)
    far = turned(far, -1).astype(F32)
    next_to = turned_over(next_to).astype(F32)
    near = turned((near + far).astype(WIRE), -1).astype(F32)
    return own + next_to + near


def per_device(tokens, starts, gain, w_query, w_key, w_value, w_out, cotangent):
    token_rows = tokens[0]
    grad_out = cotangent[0]
    rows, width = token_rows.shape
    seg = starts.shape[1]
    length = rows * CTX
    ctx, core = lax.axis_index("ctx"), here()[3]

    mine, half, own_starts = cut_weights(w_query, w_key, w_value, w_out, starts)
    halves = gathered_halves(half)
    theirs = other_x(mine)
    beside, facing = other_core(own_starts), other_chip(own_starts)
    to_core, to_chip, mid_token, mid_grad, first = window_sums(
        own_starts, beside, facing, token_rows, grad_out
    )
    before = jnp.where(core == 0, facing, beside)[0]
    after = jnp.where(core == 0, beside, facing)[0]
    before = jnp.where(ctx == 0, -1, before)
    after = jnp.where(ctx == CTX - 1, length, after)
    stop = jnp.full((1,), length, jnp.int32)
    window = jnp.concatenate([before, own_starts[0], after, stop])
    opens, ends = window[:-1], window[1:]
    count = (ends - opens)[seg : 2 * seg, None].astype(F32)
    second = two_back(first)
    normin, normed, rms, dout, both = norm(
        other_core(to_core),
        other_chip(to_chip),
        mid_token,
        mid_grad,
        count,
        gain[None],
        mine,
        theirs,
        second,
    )
    weights = [both, shifted_y(both, 1), shifted_y(both, -1), shifted_y(both, 2)]
    dout, dout_b = whole_dout(dout, second)
    dout_there = other_core(dout_b)
    pieces = gathered_rows(normin, weights[1:3] + [dout_there], weights[3:])
    q, own, w_full = project(pieces, weights)
    cross, far, beside = across(own, 0, True), across(own, 0, False), other_pair(own)
    da = dattended(dout_b, dout_there, halves, q)
    da_here = [da[0]] + [
        moved(da[i], lambda h, t, p, k, i=i: (h, t + i, p, k)) for i in range(1, TURNS)
    ]
    da_there = [other_core(piece) for piece in da_here]
    blocks = (own, beside, far, cross)
    dq, own, beside, far, cross = attention(q, da_here, da_there, blocks, seg)
    parts = (own, other_pair(beside), across(far, 1, False), across(cross, 1, True))
    dnormin = summed_rows(*unproject(dq, parts, w_full, seg))

    scaled = dnormin * gain
    dpooled = dout + (scaled - normed * jnp.mean(scaled * normed, axis=-1, keepdims=True)) / rms
    per_seg = (dpooled / count).astype(WIRE)
    beside, facing = other_core(per_seg), other_chip(per_seg)
    before = jnp.where(core == 0, facing, beside)
    after = jnp.where(core == 0, beside, facing)
    per_window = jnp.concatenate([before, per_seg, after], axis=0)
    positions = (ctx * rows + lax.iota(jnp.int32, rows))[:, None]
    member = (opens[None] <= positions) & (positions < ends[None])
    spread = jnp.dot(member.astype(WIRE), per_window, preferred_element_type=F32)
    return (grad_out.astype(F32) + spread).astype(jnp.bfloat16)[None]


def solution(mesh):
    return jax.shard_map(
        per_device,
        mesh=mesh,
        in_specs=(
            P("dp", "ctx", None),
            P("dp", "ctx"),
            P(),
            P("dp", None),
            P("dp", None),
            P("dp", None),
            P("dp", None),
            P("dp", "ctx", None),
        ),
        out_specs=P("dp", "ctx", None),
        check_vma=False,
    )
```

```python
import functools
import math

import jax
import jax.numpy as jnp
from jax import lax
from jax.experimental import pallas as pl
from jax.experimental.pallas import tpu as pltpu
from jax.sharding import PartitionSpec as P

HEAD = 128
HALVES, TURNS, PAIR, CORES = 2, 4, 2, 2
CTX = HALVES * TURNS * PAIR * CORES
ROWS_X, ROWS_Y = 2, 4
NEG = -1e30
WIRE = jnp.bfloat16
F32 = jnp.float32
VMEM = pl.BlockSpec(memory_space=pltpu.VMEM)
ANY = pl.BlockSpec(memory_space=pl.ANY)
HBM = pl.BlockSpec(memory_space=pltpu.HBM)


def room(mib):
    return pltpu.CompilerParams(vmem_limit_bytes=mib * 1024 * 1024)


def place(half, turn, pair, core):
    return ((half * TURNS + turn % TURNS) * PAIR + pair) * CORES + core


def here():
    ctx = lax.axis_index("ctx")
    core, pair = ctx % CORES, ctx // CORES % PAIR
    return ctx // (CORES * PAIR * TURNS), ctx // (CORES * PAIR) % TURNS, pair, core


def moved(value, to):
    spots = [
        (h, t, p, k)
        for h in range(HALVES)
        for t in range(TURNS)
        for p in range(PAIR)
        for k in range(CORES)
    ]
    pairs = [(place(*s), place(*to(*s))) for s in spots if to(*s) is not None]
    return lax.ppermute(value, "ctx", pairs)


def other_chip(value):
    pairs = [(i, i + 1 if i % CORES else i - 1) for i in range(1, CTX - 1)]
    return lax.ppermute(value, "ctx", pairs)


def two_back(value):
    return lax.ppermute(value, "ctx", [(i, i - CORES) for i in range(CORES, CTX)])


def other_core(value):
    return moved(value, lambda h, t, p, k: (h, t, p, 1 - k))


def other_pair(value):
    return moved(value, lambda h, t, p, k: (h, t, 1 - p, k))


def later_pair(value):
    return moved(value, lambda h, t, p, k: (h, t, 1 - p, k) if h == 1 else None)


def across(value, source, cross):
    return moved(
        value,
        lambda h, t, p, k: (1 - h, t, 1 - p if cross else p, k) if h == source else None,
    )


def turned(value, way):
    return moved(value, lambda h, t, p, k: (h, t + way * (1 - 2 * k), p, k))


def turned_over(value):
    return moved(value, lambda h, t, p, k: (h, t - (1 - 2 * k), p, 1 - k))


def contract_last(left, right):
    return lax.dot_general(left, right, (((1,), (1,)), ((), ())), preferred_element_type=F32)


def contract_first(left, right):
    return lax.dot_general(left, right, (((0,), (0,)), ((), ())), preferred_element_type=F32)


def cut_kernel(q_ref, k_ref, v_ref, o_ref, start_ref, out_ref, half_ref, start_out, sems):
    _, turn, _, core = here()
    lane = pl.multiple_of((turn * CORES + core) * HEAD, HEAD)
    copies = [
        (w.at[:, pl.ds(lane, HEAD)], out_ref.at[:, i * HEAD : (i + 1) * HEAD])
        for i, w in enumerate((q_ref, k_ref, v_ref))
    ]
    half = half_ref.shape[0]
    copies.append((o_ref.at[pl.ds(pl.multiple_of(core * half, half), half), :], half_ref))
    copies.append((start_ref, start_out))
    fetched(copies, sems)


def cut_weights(w_query, w_key, w_value, w_out, starts):
    rows, width = w_out.shape
    return pl.pallas_call(
        cut_kernel,
        out_shape=(
            jax.ShapeDtypeStruct((rows, 3 * HEAD), w_query.dtype),
            jax.ShapeDtypeStruct((rows // CORES, width), w_out.dtype),
            jax.ShapeDtypeStruct(starts.shape, starts.dtype),
        ),
        in_specs=[HBM] * 4 + [ANY],
        out_specs=(VMEM, VMEM, VMEM),
        scratch_shapes=[pltpu.SemaphoreType.DMA((5,))],
        compiler_params=room(60),
    )(w_query, w_key, w_value, w_out, starts)


def other_x(value):
    count = ROWS_X * ROWS_Y
    return lax.ppermute(value, "dp", [(d, (d + ROWS_Y) % count) for d in range(count)])


def shifted_y(value, step):
    pairs = [(d, d // ROWS_Y * ROWS_Y + (d + step) % ROWS_Y) for d in range(ROWS_X * ROWS_Y)]
    return lax.ppermute(value, "dp", pairs)


def gathered_halves(half):
    return lax.all_gather(half, "dp", axis=0, tiled=False)


def pass_kernel(value_ref, *refs):
    refs[-1][...] = value_ref[...]


def passed_on(value, *ready):
    return pl.pallas_call(
        pass_kernel,
        out_shape=jax.ShapeDtypeStruct(value.shape, value.dtype),
        in_specs=[VMEM] + [ANY] * len(ready),
        out_specs=VMEM,
        compiler_params=room(4),
    )(value, *ready)


def gathered_rows(shard, first_ready, last_ready):
    near = turned(shard, 1)
    next_to = turned_over(passed_on(shard, near))
    far = passed_on(turned(passed_on(near, *first_ready), 1), *last_ready)
    return [
        shard,
        other_core(shard),
        near,
        next_to,
        other_core(near),
        other_core(next_to),
        far,
        other_core(far),
    ]


def rows_at(row, half, turn, pair, core, seg):
    slot = row // seg
    two = slot // 2
    way = 1 - 2 * core
    step = jnp.where(two == 0, 0, jnp.where(two == 1, way, jnp.where(two == 2, -way, 2)))
    flip = jnp.where(two == 2, 1 - slot % 2, slot % 2)
    its_core = jnp.where(flip == 1, 1 - core, core)
    its_turn = (turn - step + TURNS) % TURNS
    return place(half, its_turn, pair, its_core) * seg + row % seg


def fetched(copies, sems):
    started = []
    for i, (source, target) in enumerate(copies):
        started.append(pltpu.make_async_copy(source, target, sems.at[i]))
        started[-1].start()
    for copy in started:
        copy.wait()


def fill(out_ref, pieces):
    at = 0
    for piece in pieces:
        out_ref[at : at + piece.shape[0], :] = piece[...]
        at += piece.shape[0]


def window_kernel(own_ref, beside_ref, facing_ref, token_hbm, grad_hbm, *refs):
    core_ref, chip_ref, mid_token, mid_grad, first_ref = refs[:5]
    token_ref, grad_ref, sems = refs[5:]
    rows, width = token_ref.shape
    seg = mid_token.shape[0]
    token_copy = pltpu.make_async_copy(token_hbm, token_ref, sems.at[0])
    grad_copy = pltpu.make_async_copy(grad_hbm, grad_ref, sems.at[1])
    token_copy.start()
    grad_copy.start()
    ctx, core = lax.axis_index("ctx"), here()[3]
    at = lax.broadcasted_iota(jnp.int32, (rows, 1), 0) + ctx * rows
    before = jnp.where(core == 0, facing_ref[...], beside_ref[...])
    after = jnp.where(core == 0, beside_ref[...], facing_ref[...])
    before = jnp.where(ctx == 0, -1, before)
    after = jnp.where(ctx == CTX - 1, rows * CTX, after)
    begun = [(part <= at).astype(jnp.int32) for part in (before, own_ref[...], after)]
    slot = sum(jnp.sum(part, axis=1, keepdims=True) for part in begun) - 1
    slots = lax.broadcasted_iota(jnp.int32, (1, 3 * seg), 1)
    member = (slots == slot).astype(jnp.bfloat16)
    earlier = (slots == slot - 1).astype(jnp.bfloat16)
    token_copy.wait()
    token = contract_first(member, token_ref[...])
    grad_copy.wait()
    grad = contract_first(earlier, grad_ref[...])
    outside = jnp.broadcast_to((slot == 0).astype(jnp.bfloat16), (rows, HEAD))
    first_ref[...] = contract_first(outside, grad_ref[...])[:1]
    mid_token[...] = token[seg : 2 * seg]
    mid_grad[...] = grad[seg : 2 * seg]

    def send(lower_ref, upper_ref):
        lower_ref[:, :width] = token[:seg].astype(WIRE)
        lower_ref[:, width:] = grad[:seg].astype(WIRE)
        upper_ref[:, :width] = token[2 * seg :].astype(WIRE)
        upper_ref[:, width:] = grad[2 * seg :].astype(WIRE)

    @pl.when(core == 0)
    def _():
        send(chip_ref, core_ref)

    @pl.when(core == 1)
    def _():
        send(core_ref, chip_ref)


def window_sums(own, beside, facing, tokens, grads):
    rows, width = tokens.shape
    seg = own.shape[1]
    shape = jax.ShapeDtypeStruct
    return pl.pallas_call(
        window_kernel,
        out_shape=(
            shape((seg, 2 * width), WIRE),
            shape((seg, 2 * width), WIRE),
            shape((seg, width), F32),
            shape((seg, width), F32),
            shape((1, width), F32),
        ),
        in_specs=[VMEM] * 3 + [HBM] * 2,
        out_specs=(VMEM,) * 5,
        scratch_shapes=[
            pltpu.VMEM((rows, width), tokens.dtype),
            pltpu.VMEM((rows, width), grads.dtype),
            pltpu.SemaphoreType.DMA((2,)),
        ],
        compiler_params=room(16),
    )(own, beside, facing, tokens, grads)


def norm_kernel(core_ref, chip_ref, mid_token, mid_grad, count_ref, gain_ref, *refs):
    mine_ref, theirs_ref = refs[:2]
    normin_ref, normed_ref, rms_ref, dout_ref, pair_ref = refs[-5:]
    width = mid_token.shape[1]
    rows = mine_ref.shape[0]
    pair_ref[:rows, :] = mine_ref[...]
    pair_ref[rows:, :] = theirs_ref[...]
    got = core_ref[...].astype(F32) + chip_ref[...].astype(F32)
    pooled = (mid_token[...] + got[:, :width]) / count_ref[...]
    rms = jnp.sqrt(jnp.mean(pooled * pooled, axis=1, keepdims=True) + 1e-06)
    normed = pooled / rms
    normed_ref[...] = normed
    rms_ref[...] = rms
    normin_ref[...] = (normed * gain_ref[...]).astype(jnp.bfloat16)
    dout_ref[...] = mid_grad[...] + got[:, width:]


def norm(from_core, from_chip, mid_token, mid_grad, count, gain, mine, theirs, ready):
    seg, width = mid_token.shape
    shape = jax.ShapeDtypeStruct
    return pl.pallas_call(
        norm_kernel,
        out_shape=(
            shape((seg, width), jnp.bfloat16),
            shape((seg, width), F32),
            shape((seg, 1), F32),
            shape((seg, width), F32),
            shape((2 * mine.shape[0], mine.shape[1]), mine.dtype),
        ),
        in_specs=[VMEM] * 8 + [ANY],
        out_specs=(VMEM,) * 5,
        compiler_params=room(8),
    )(from_core, from_chip, mid_token, mid_grad, count, gain, mine, theirs, ready)


def dout_kernel(dout_ref, second_ref, full_ref, half_ref):
    seg = dout_ref.shape[0]
    last = lax.broadcasted_iota(jnp.int32, (seg, 1), 0) == seg - 1
    dout = dout_ref[...] + jnp.where(last, second_ref[...], 0.0)
    full_ref[...] = dout
    half_ref[...] = dout.astype(jnp.bfloat16)


def whole_dout(dout, second):
    shape = jax.ShapeDtypeStruct
    return pl.pallas_call(
        dout_kernel,
        out_shape=(shape(dout.shape, F32), shape(dout.shape, jnp.bfloat16)),
        in_specs=[VMEM, VMEM],
        out_specs=(VMEM, VMEM),
        compiler_params=room(4),
    )(dout, second)


def dattended_kernel(own_ref, other_ref, weight_ref, ready_ref, *refs):
    outs, rows, weight, sems = refs[:TURNS], *refs[TURNS:]
    heads, half = weight_ref.shape[:2]
    fill(rows, [own_ref, other_ref])
    fetched(
        [(weight_ref.at[i], weight.at[i * half : (i + 1) * half, :]) for i in range(heads)], sems
    )
    turn = here()[1]
    for step, out in enumerate(outs):
        at = pl.multiple_of((turn + step) % TURNS * CORES * half, CORES * half)
        part = weight[pl.ds(at, CORES * half), :]
        out[...] = contract_last(rows[...], part).astype(jnp.bfloat16)


def dattended(own, other, halves, ready):
    heads, half, width = halves.shape
    rows = 2 * own.shape[0]
    return pl.pallas_call(
        dattended_kernel,
        out_shape=(jax.ShapeDtypeStruct((rows, CORES * half), jnp.bfloat16),) * TURNS,
        in_specs=[VMEM, VMEM, ANY, ANY],
        out_specs=(VMEM,) * TURNS,
        scratch_shapes=[
            pltpu.VMEM((rows, width), jnp.bfloat16),
            pltpu.VMEM((heads * half, width), jnp.bfloat16),
            pltpu.SemaphoreType.DMA((heads,)),
        ],
        compiler_params=room(12),
    )(own, other, halves, ready)


def project_kernel(*refs):
    pieces, weights = refs[:8], refs[8:12]
    q_ref, kv_ref, top_ref, bottom_ref, w_ref, rows = refs[12:]
    fill(rows, pieces)
    dp = lax.axis_index("dp")
    x, y = dp // ROWS_Y, dp % ROWS_Y
    depth = weights[0].shape[0] // ROWS_X
    for weight, step in zip(weights, (0, 1, -1, 2)):
        its_y = (y - step + ROWS_Y) % ROWS_Y
        for i in range(ROWS_X):
            its_x = x if i == 0 else 1 - x
            at = pl.multiple_of((its_x * ROWS_Y + its_y) * depth, depth)
            w_ref[pl.ds(at, depth), :] = weight[i * depth : (i + 1) * depth, :]
    out = jnp.dot(rows[...], w_ref[...], preferred_element_type=F32).astype(jnp.bfloat16)
    cut = out.shape[0] // 2
    q_ref[...] = out[:, :HEAD]
    kv_ref[...] = out[:, HEAD:]
    top_ref[...] = out[:cut, HEAD:]
    bottom_ref[...] = out[cut:, HEAD:]


def project(pieces, weights):
    seg, width = pieces[0].shape
    rows = seg * len(pieces)
    bf16 = lambda *shape: jax.ShapeDtypeStruct(shape, jnp.bfloat16)
    return pl.pallas_call(
        project_kernel,
        out_shape=(
            bf16(rows, HEAD),
            bf16(rows, 2 * HEAD),
            bf16(rows // 2, 2 * HEAD),
            bf16(rows // 2, 2 * HEAD),
            bf16(width, 3 * HEAD),
        ),
        in_specs=[VMEM] * 12,
        out_specs=(VMEM,) * 5,
        scratch_shapes=[pltpu.VMEM((rows, width), jnp.bfloat16)],
        compiler_params=room(12),
    )(*pieces, *weights)


def place_dattended(core, seg, here_refs, there_refs, out_ref):
    half = out_ref.shape[1] // CORES
    mine = slice(core * half, (core + 1) * half)
    other = slice((1 - core) * half, (2 - core) * half)
    slots = ((0, 1), (2, 3), (6, 7), (5, 4)) if core == 0 else ((0, 1), (5, 4), (6, 7), (2, 3))
    for refs in zip(here_refs, there_refs, slots):
        for i, slot in enumerate(refs[2]):
            rows = slice(slot * seg, (slot + 1) * seg)
            out_ref[rows, mine] = refs[0][i * seg : (i + 1) * seg, mine]
            out_ref[rows, other] = refs[1][(1 - i) * seg : (2 - i) * seg, mine]


def attention_kernel(tile, seg, *refs):
    q_ref, here_refs, there_refs, blocks = refs[0], refs[1:5], refs[5:9], refs[9:15]
    dq_ref, outs, (kv, da_ref, dkt, dvt) = refs[15], refs[16:22], refs[22:]
    half, turn, pair, core = here()
    queries, keys = q_ref.shape[0], kv.shape[0]
    fill(kv, blocks)

    for which in range(CORES):

        @pl.when(core == which)
        def _(which=which):
            place_dattended(which, seg, here_refs, there_refs, da_ref)

    spot = lax.broadcasted_iota(jnp.int32, (1, keys), 1)
    block = spot // queries
    key_half = jnp.where(block < 2, half, 1 - half)
    key_pair = jnp.where(block % 2 == 0, pair, 1 - pair)
    key_at = rows_at(spot % queries, key_half, turn, key_pair, core, seg)
    turn_up = math.log2(math.e) / math.sqrt(HEAD)
    scale = 1.0 / math.sqrt(HEAD)
    k = kv[:, :HEAD]
    v = kv[:, HEAD:]
    for step in range(queries // tile):
        rows = slice(step * tile, (step + 1) * tile)
        query = lax.broadcasted_iota(jnp.int32, (tile, 1), 0) + step * tile
        query_at = rows_at(query, half, turn, pair, core, seg)
        q = q_ref[rows, :]
        da = da_ref[rows, :]
        score = jnp.where(key_at <= query_at, contract_last(q, k), NEG)
        peak = jnp.max(score, axis=1, keepdims=True)
        expo = jnp.exp2((score - peak) * turn_up)
        probs = expo * (1.0 / jnp.sum(expo, axis=1, keepdims=True))
        probs_b = probs.astype(jnp.bfloat16)
        attended = jnp.dot(probs_b, v, preferred_element_type=F32).astype(jnp.bfloat16)
        delta = jnp.sum(da.astype(F32) * attended.astype(F32), axis=1, keepdims=True)
        dscore = (probs * (contract_last(da, v) - delta)).astype(jnp.bfloat16)
        dq = jnp.dot(dscore, k, preferred_element_type=F32) * scale
        dq_ref[rows, :] = dq.astype(jnp.bfloat16)
        dk_part = contract_first(q, dscore)
        dv_part = contract_first(da, probs_b)
        if step == 0:
            dkt[...] = dk_part
            dvt[...] = dv_part
        else:
            dkt[...] += dk_part
            dvt[...] += dv_part
    at = 0
    for out in outs:
        lanes = slice(at, at + out.shape[0])
        at += out.shape[0]
        out[:, :HEAD] = (dkt[:, lanes] * scale).T.astype(jnp.bfloat16)
        out[:, HEAD:] = dvt[:, lanes].T.astype(jnp.bfloat16)


def attention(q, da_here, da_there, blocks, seg):
    queries = q.shape[0]
    keys = sum(block.shape[0] for block in blocks)
    parts = tuple(jax.ShapeDtypeStruct(block.shape, jnp.bfloat16) for block in blocks)
    return pl.pallas_call(
        functools.partial(attention_kernel, 256, seg),
        out_shape=(jax.ShapeDtypeStruct((queries, HEAD), jnp.bfloat16),) + parts,
        in_specs=[VMEM] * 15,
        out_specs=(VMEM,) * 7,
        scratch_shapes=[
            pltpu.VMEM((keys, 2 * HEAD), jnp.bfloat16),
            pltpu.VMEM((queries, HEAD), jnp.bfloat16),
            pltpu.VMEM((HEAD, keys), F32),
            pltpu.VMEM((HEAD, keys), F32),
        ],
        compiler_params=room(36),
        cost_estimate=pl.CostEstimate(
            flops=12 * queries * keys * HEAD,
            bytes_accessed=2 * HEAD * (3 * queries + 4 * keys),
            transcendentals=queries * keys,
        ),
    )(q, *da_here, *da_there, *blocks)


def unproject_kernel(seg, dq_ref, *refs):
    parts, w_ref, swap_ref, outs = refs[:5], refs[5], refs[6], refs[7:]
    own, beside, far_top, cross_top, far_bottom = (ref[...].astype(F32) for ref in parts)
    far = jnp.concatenate([far_top + cross_top, far_bottom], axis=0)
    dkv = (own + beside + far).astype(jnp.bfloat16)
    left = jnp.concatenate([dq_ref[...], dkv], axis=1)
    out = contract_last(left, w_ref[...])
    for i, slot in enumerate((1, 4, 5, 7)):
        swap_ref[i * seg : (i + 1) * seg, :] = out[slot * seg : (slot + 1) * seg].astype(WIRE)
    for ref, slot in zip(outs, (0, 2, 3, 6)):
        ref[...] = out[slot * seg : (slot + 1) * seg]


def unproject(dq, parts, w_full, seg):
    width = w_full.shape[0]
    return pl.pallas_call(
        functools.partial(unproject_kernel, seg),
        out_shape=(jax.ShapeDtypeStruct((4 * seg, width), WIRE),)
        + (jax.ShapeDtypeStruct((seg, width), F32),) * 4,
        in_specs=[VMEM] * 7,
        out_specs=(VMEM,) * 5,
        compiler_params=room(16),
    )(dq, *parts, w_full)


def join_kernel(swapped, own, near, next_to, far, own_out, near_out, next_out, far_out):
    seg = own.shape[0]
    own_out[...] = own[...] + swapped[:seg, :].astype(F32)
    near_out[...] = near[...] + swapped[seg : 2 * seg, :].astype(F32)
    next_out[...] = (next_to[...] + swapped[2 * seg : 3 * seg, :].astype(F32)).astype(WIRE)
    far_out[...] = (far[...] + swapped[3 * seg :, :].astype(F32)).astype(WIRE)


def joined(swapped, own, near, next_to, far):
    wide = jax.ShapeDtypeStruct(own.shape, F32)
    thin = jax.ShapeDtypeStruct(own.shape, WIRE)
    return pl.pallas_call(
        join_kernel,
        out_shape=(wide, wide, thin, thin),
        in_specs=[VMEM] * 5,
        out_specs=(VMEM,) * 4,
        compiler_params=room(6),
    )(swapped, own, near, next_to, far)


def summed_rows(swap, own, near, next_to, far):
    own, near, next_to, far = joined(other_core(swap), own, near, next_to, far)
    far = turned(far, -1).astype(F32)
    next_to = turned_over(next_to).astype(F32)
    near = turned((near + far).astype(WIRE), -1).astype(F32)
    return own + next_to + near


def per_device(tokens, starts, gain, w_query, w_key, w_value, w_out, cotangent):
    token_rows = tokens[0]
    grad_out = cotangent[0]
    rows, width = token_rows.shape
    seg = starts.shape[1]
    length = rows * CTX
    ctx, core = lax.axis_index("ctx"), here()[3]

    mine, half, own_starts = cut_weights(w_query, w_key, w_value, w_out, starts)
    halves = gathered_halves(half)
    theirs = other_x(mine)
    beside, facing = other_core(own_starts), other_chip(own_starts)
    own_starts = starts
    to_core, to_chip, mid_token, mid_grad, first = window_sums(
        own_starts, beside, facing, token_rows, grad_out
    )
    before = jnp.where(core == 0, facing, beside)[0]
    after = jnp.where(core == 0, beside, facing)[0]
    before = jnp.where(ctx == 0, -1, before)
    after = jnp.where(ctx == CTX - 1, length, after)
    stop = jnp.full((1,), length, jnp.int32)
    window = jnp.concatenate([before, own_starts[0], after, stop])
    opens, ends = window[:-1], window[1:]
    count = (ends - opens)[seg : 2 * seg, None].astype(F32)
    second = two_back(first)
    normin, normed, rms, dout, both = norm(
        other_core(to_core),
        other_chip(to_chip),
        mid_token,
        mid_grad,
        count,
        gain[None],
        mine,
        theirs,
        second,
    )
    weights = [both, shifted_y(both, 1), shifted_y(both, -1), shifted_y(both, 2)]
    dout, dout_b = whole_dout(dout, second)
    dout_there = other_core(dout_b)
    pieces = gathered_rows(normin, weights[1:3] + [dout_there], weights[3:])
    q, own, top, bottom, w_full = project(pieces, weights)
    far_bottom, beside = across(bottom, 0, False), other_pair(own)
    far_top, cross_top = across(top, 0, False), across(top, 0, True)
    cross_bottom = later_pair(far_bottom)
    da = dattended(dout_b, dout_there, halves, q)
    da_here = [da[0]] + [
        moved(da[i], lambda h, t, p, k, i=i: (h, t + i, p, k)) for i in range(1, TURNS)
    ]
    da_there = [other_core(piece) for piece in da_here]
    blocks = (own, beside, far_top, far_bottom, cross_top, cross_bottom)
    dq, *grads = attention(q, da_here, da_there, blocks, seg)
    own, beside, far_top, far_bottom, cross_top, cross_bottom = grads
    passed = later_pair(cross_bottom)
    beside, far_top, cross_top = other_pair(beside), across(far_top, 1, False), across(cross_top, 1, True)
    far_bottom = (far_bottom.astype(F32) + passed.astype(F32)).astype(WIRE)
    far_bottom = across(far_bottom, 1, False)
    parts = (own, beside, far_top, cross_top, far_bottom)
    dnormin = summed_rows(*unproject(dq, parts, w_full, seg))

    scaled = dnormin * gain
    dpooled = dout + (scaled - normed * jnp.mean(scaled * normed, axis=-1, keepdims=True)) / rms
    per_seg = (dpooled / count).astype(WIRE)
    beside, facing = other_core(per_seg), other_chip(per_seg)
    before = jnp.where(core == 0, facing, beside)
    after = jnp.where(core == 0, beside, facing)
    per_window = jnp.concatenate([before, per_seg, after], axis=0)
    positions = (ctx * rows + lax.iota(jnp.int32, rows))[:, None]
    member = (opens[None] <= positions) & (positions < ends[None])
    spread = jnp.dot(member.astype(WIRE), per_window, preferred_element_type=F32)
    return (grad_out.astype(F32) + spread).astype(jnp.bfloat16)[None]


def solution(mesh):
    return jax.shard_map(
        per_device,
        mesh=mesh,
        in_specs=(
            P("dp", "ctx", None),
            P("dp", "ctx"),
            P(),
            P("dp", None),
            P("dp", None),
            P("dp", None),
            P("dp", None),
            P("dp", "ctx", None),
        ),
        out_specs=P("dp", "ctx", None),
        check_vma=False,
    )
```

```python
import functools
import math

import jax
import jax.numpy as jnp
from jax import lax
from jax.experimental import pallas as pl
from jax.experimental.pallas import tpu as pltpu
from jax.sharding import PartitionSpec as P

HEAD = 128
HALVES, TURNS, PAIR, CORES = 2, 4, 2, 2
CTX = HALVES * TURNS * PAIR * CORES
ROWS_X, ROWS_Y = 2, 4
NEG = -1e30
WIRE = jnp.bfloat16
F32 = jnp.float32
VMEM = pl.BlockSpec(memory_space=pltpu.VMEM)
ANY = pl.BlockSpec(memory_space=pl.ANY)
HBM = pl.BlockSpec(memory_space=pltpu.HBM)


def room(mib):
    return pltpu.CompilerParams(vmem_limit_bytes=mib * 1024 * 1024)


def place(half, turn, pair, core):
    return ((half * TURNS + turn % TURNS) * PAIR + pair) * CORES + core


def here():
    ctx = lax.axis_index("ctx")
    core, pair = ctx % CORES, ctx // CORES % PAIR
    return ctx // (CORES * PAIR * TURNS), ctx // (CORES * PAIR) % TURNS, pair, core


def moved(value, to):
    spots = [
        (h, t, p, k)
        for h in range(HALVES)
        for t in range(TURNS)
        for p in range(PAIR)
        for k in range(CORES)
    ]
    pairs = [(place(*s), place(*to(*s))) for s in spots if to(*s) is not None]
    return lax.ppermute(value, "ctx", pairs)


def other_chip(value):
    pairs = [(i, i + 1 if i % CORES else i - 1) for i in range(1, CTX - 1)]
    return lax.ppermute(value, "ctx", pairs)


def two_back(value):
    return lax.ppermute(value, "ctx", [(i, i - CORES) for i in range(CORES, CTX)])


def other_core(value):
    return moved(value, lambda h, t, p, k: (h, t, p, 1 - k))


def other_pair(value):
    return moved(value, lambda h, t, p, k: (h, t, 1 - p, k))


def across(value, source, cross):
    return moved(
        value,
        lambda h, t, p, k: (1 - h, t, 1 - p if cross else p, k) if h == source else None,
    )


def turned(value, way):
    return moved(value, lambda h, t, p, k: (h, t + way * (1 - 2 * k), p, k))


def turned_over(value):
    return moved(value, lambda h, t, p, k: (h, t - (1 - 2 * k), p, 1 - k))


def contract_last(left, right):
    return lax.dot_general(left, right, (((1,), (1,)), ((), ())), preferred_element_type=F32)


def contract_first(left, right):
    return lax.dot_general(left, right, (((0,), (0,)), ((), ())), preferred_element_type=F32)


def cut_kernel(q_ref, k_ref, v_ref, o_ref, start_ref, out_ref, half_ref, start_out, sems):
    _, turn, _, core = here()
    lane = pl.multiple_of((turn * CORES + core) * HEAD, HEAD)
    copies = [
        (w.at[:, pl.ds(lane, HEAD)], out_ref.at[:, i * HEAD : (i + 1) * HEAD])
        for i, w in enumerate((q_ref, k_ref, v_ref))
    ]
    half = half_ref.shape[0]
    copies.append((o_ref.at[pl.ds(pl.multiple_of(core * half, half), half), :], half_ref))
    copies.append((start_ref, start_out))
    fetched(copies, sems)


def cut_weights(w_query, w_key, w_value, w_out, starts):
    rows, width = w_out.shape
    return pl.pallas_call(
        cut_kernel,
        out_shape=(
            jax.ShapeDtypeStruct((rows, 3 * HEAD), w_query.dtype),
            jax.ShapeDtypeStruct((rows // CORES, width), w_out.dtype),
            jax.ShapeDtypeStruct(starts.shape, starts.dtype),
        ),
        in_specs=[HBM] * 4 + [ANY],
        out_specs=(VMEM, VMEM, VMEM),
        scratch_shapes=[pltpu.SemaphoreType.DMA((5,))],
        compiler_params=room(60),
    )(w_query, w_key, w_value, w_out, starts)


def other_x(value):
    count = ROWS_X * ROWS_Y
    return lax.ppermute(value, "dp", [(d, (d + ROWS_Y) % count) for d in range(count)])


def shifted_y(value, step):
    pairs = [(d, d // ROWS_Y * ROWS_Y + (d + step) % ROWS_Y) for d in range(ROWS_X * ROWS_Y)]
    return lax.ppermute(value, "dp", pairs)


def gathered_halves(half):
    return lax.all_gather(half, "dp", axis=0, tiled=False)


def pass_kernel(value_ref, *refs):
    refs[-1][...] = value_ref[...]


def passed_on(value, *ready):
    return pl.pallas_call(
        pass_kernel,
        out_shape=jax.ShapeDtypeStruct(value.shape, value.dtype),
        in_specs=[VMEM] + [ANY] * len(ready),
        out_specs=VMEM,
        compiler_params=room(4),
    )(value, *ready)


def gathered_rows(shard, first_ready, last_ready):
    near = turned(shard, 1)
    next_to = turned_over(passed_on(shard, near))
    far = passed_on(turned(passed_on(near, *first_ready), 1), *last_ready)
    return [
        shard,
        other_core(shard),
        near,
        next_to,
        other_core(near),
        other_core(next_to),
        far,
        other_core(far),
    ]


def rows_at(row, half, turn, pair, core, seg):
    slot = row // seg
    two = slot // 2
    way = 1 - 2 * core
    step = jnp.where(two == 0, 0, jnp.where(two == 1, way, jnp.where(two == 2, -way, 2)))
    flip = jnp.where(two == 2, 1 - slot % 2, slot % 2)
    its_core = jnp.where(flip == 1, 1 - core, core)
    its_turn = (turn - step + TURNS) % TURNS
    return place(half, its_turn, pair, its_core) * seg + row % seg


def fetched(copies, sems):
    started = []
    for i, (source, target) in enumerate(copies):
        started.append(pltpu.make_async_copy(source, target, sems.at[i]))
        started[-1].start()
    for copy in started:
        copy.wait()


def fill(out_ref, pieces):
    at = 0
    for piece in pieces:
        out_ref[at : at + piece.shape[0], :] = piece[...]
        at += piece.shape[0]


def window_kernel(own_ref, beside_ref, facing_ref, token_hbm, grad_hbm, *refs):
    core_ref, chip_ref, mid_token, mid_grad, first_ref = refs[:5]
    token_ref, grad_ref, sems = refs[5:]
    rows, width = token_ref.shape
    seg = mid_token.shape[0]
    token_copy = pltpu.make_async_copy(token_hbm, token_ref, sems.at[0])
    grad_copy = pltpu.make_async_copy(grad_hbm, grad_ref, sems.at[1])
    token_copy.start()
    grad_copy.start()
    ctx, core = lax.axis_index("ctx"), here()[3]
    at = lax.broadcasted_iota(jnp.int32, (rows, 1), 0) + ctx * rows
    before = jnp.where(core == 0, facing_ref[...], beside_ref[...])
    after = jnp.where(core == 0, beside_ref[...], facing_ref[...])
    before = jnp.where(ctx == 0, -1, before)
    after = jnp.where(ctx == CTX - 1, rows * CTX, after)
    begun = [(part <= at).astype(jnp.int32) for part in (before, own_ref[...], after)]
    slot = sum(jnp.sum(part, axis=1, keepdims=True) for part in begun) - 1
    slots = lax.broadcasted_iota(jnp.int32, (1, 3 * seg), 1)
    member = (slots == slot).astype(jnp.bfloat16)
    earlier = (slots == slot - 1).astype(jnp.bfloat16)
    token_copy.wait()
    token = contract_first(member, token_ref[...])
    grad_copy.wait()
    grad = contract_first(earlier, grad_ref[...])
    outside = jnp.broadcast_to((slot == 0).astype(jnp.bfloat16), (rows, HEAD))
    first_ref[...] = contract_first(outside, grad_ref[...])[:1]
    mid_token[...] = token[seg : 2 * seg]
    mid_grad[...] = grad[seg : 2 * seg]

    def send(lower_ref, upper_ref):
        lower_ref[:, :width] = token[:seg].astype(WIRE)
        lower_ref[:, width:] = grad[:seg].astype(WIRE)
        upper_ref[:, :width] = token[2 * seg :].astype(WIRE)
        upper_ref[:, width:] = grad[2 * seg :].astype(WIRE)

    @pl.when(core == 0)
    def _():
        send(chip_ref, core_ref)

    @pl.when(core == 1)
    def _():
        send(core_ref, chip_ref)


def window_sums(own, beside, facing, tokens, grads):
    rows, width = tokens.shape
    seg = own.shape[1]
    shape = jax.ShapeDtypeStruct
    return pl.pallas_call(
        window_kernel,
        out_shape=(
            shape((seg, 2 * width), WIRE),
            shape((seg, 2 * width), WIRE),
            shape((seg, width), F32),
            shape((seg, width), F32),
            shape((1, width), F32),
        ),
        in_specs=[VMEM] * 3 + [HBM] * 2,
        out_specs=(VMEM,) * 5,
        scratch_shapes=[
            pltpu.VMEM((rows, width), tokens.dtype),
            pltpu.VMEM((rows, width), grads.dtype),
            pltpu.SemaphoreType.DMA((2,)),
        ],
        compiler_params=room(16),
    )(own, beside, facing, tokens, grads)


def norm_kernel(core_ref, chip_ref, mid_token, mid_grad, count_ref, gain_ref, *refs):
    mine_ref, theirs_ref, normin_ref, normed_ref, rms_ref, dout_ref, pair_ref = refs
    width = mid_token.shape[1]
    rows = mine_ref.shape[0]
    pair_ref[:rows, :] = mine_ref[...]
    pair_ref[rows:, :] = theirs_ref[...]
    got = core_ref[...].astype(F32) + chip_ref[...].astype(F32)
    pooled = (mid_token[...] + got[:, :width]) / count_ref[...]
    rms = jnp.sqrt(jnp.mean(pooled * pooled, axis=1, keepdims=True) + 1e-06)
    normed = pooled / rms
    normed_ref[...] = normed
    rms_ref[...] = rms
    normin_ref[...] = (normed * gain_ref[...]).astype(jnp.bfloat16)
    dout_ref[...] = mid_grad[...] + got[:, width:]


def norm(from_core, from_chip, mid_token, mid_grad, count, gain, mine, theirs):
    seg, width = mid_token.shape
    shape = jax.ShapeDtypeStruct
    return pl.pallas_call(
        norm_kernel,
        out_shape=(
            shape((seg, width), jnp.bfloat16),
            shape((seg, width), F32),
            shape((seg, 1), F32),
            shape((seg, width), F32),
            shape((2 * mine.shape[0], mine.shape[1]), mine.dtype),
        ),
        in_specs=[VMEM] * 8,
        out_specs=(VMEM,) * 5,
        compiler_params=room(8),
    )(from_core, from_chip, mid_token, mid_grad, count, gain, mine, theirs)


def dout_kernel(dout_ref, second_ref, full_ref, half_ref):
    seg = dout_ref.shape[0]
    last = lax.broadcasted_iota(jnp.int32, (seg, 1), 0) == seg - 1
    dout = dout_ref[...] + jnp.where(last, second_ref[...], 0.0)
    full_ref[...] = dout
    half_ref[...] = dout.astype(jnp.bfloat16)


def whole_dout(dout, second):
    shape = jax.ShapeDtypeStruct
    return pl.pallas_call(
        dout_kernel,
        out_shape=(shape(dout.shape, F32), shape(dout.shape, jnp.bfloat16)),
        in_specs=[VMEM, VMEM],
        out_specs=(VMEM, VMEM),
        compiler_params=room(4),
    )(dout, second)


def project_kernel(*refs):
    pieces, weights, douts, halves = refs[:8], refs[8:12], refs[12:14], refs[14]
    q_ref, kv_ref, w_ref, outs = *refs[15:18], refs[18:22]
    rows, chip_rows, w_back, sems = refs[22:]
    heads, half = halves.shape[:2]
    started = []
    for i in range(heads):
        target = w_back.at[i * half : (i + 1) * half, :]
        started.append(pltpu.make_async_copy(halves.at[i], target, sems.at[i]))
        started[-1].start()
    fill(rows, pieces)
    fill(chip_rows, douts)
    dp = lax.axis_index("dp")
    x, y = dp // ROWS_Y, dp % ROWS_Y
    depth = weights[0].shape[0] // ROWS_X
    for weight, step in zip(weights, (0, 1, -1, 2)):
        its_y = (y - step + ROWS_Y) % ROWS_Y
        for i in range(ROWS_X):
            its_x = x if i == 0 else 1 - x
            at = pl.multiple_of((its_x * ROWS_Y + its_y) * depth, depth)
            w_ref[pl.ds(at, depth), :] = weight[i * depth : (i + 1) * depth, :]
    out = jnp.dot(rows[...], w_ref[...], preferred_element_type=F32).astype(jnp.bfloat16)
    q_ref[...] = out[:, :HEAD]
    kv_ref[...] = out[:, HEAD:]
    for copy in started:
        copy.wait()
    turn = here()[1]
    for step, ref in enumerate(outs):
        at = pl.multiple_of((turn + step) % TURNS * CORES * half, CORES * half)
        part = w_back[pl.ds(at, CORES * half), :]
        ref[...] = contract_last(chip_rows[...], part).astype(jnp.bfloat16)


def project(pieces, weights, douts, halves):
    seg, width = pieces[0].shape
    rows = seg * len(pieces)
    heads, half = halves.shape[:2]
    bf16 = lambda *shape: jax.ShapeDtypeStruct(shape, jnp.bfloat16)
    return pl.pallas_call(
        project_kernel,
        out_shape=(bf16(rows, HEAD), bf16(rows, 2 * HEAD), bf16(width, 3 * HEAD))
        + (bf16(2 * seg, CORES * half),) * TURNS,
        in_specs=[VMEM] * 14 + [ANY],
        out_specs=(VMEM,) * (3 + TURNS),
        scratch_shapes=[
            pltpu.VMEM((rows, width), jnp.bfloat16),
            pltpu.VMEM((2 * seg, width), jnp.bfloat16),
            pltpu.VMEM((heads * half, width), jnp.bfloat16),
            pltpu.SemaphoreType.DMA((heads,)),
        ],
        compiler_params=room(50),
    )(*pieces, *weights, *douts, halves)


def place_dattended(core, seg, here_refs, there_refs, out_ref):
    half = out_ref.shape[1] // CORES
    mine = slice(core * half, (core + 1) * half)
    other = slice((1 - core) * half, (2 - core) * half)
    slots = ((0, 1), (2, 3), (6, 7), (5, 4)) if core == 0 else ((0, 1), (5, 4), (6, 7), (2, 3))
    for refs in zip(here_refs, there_refs, slots):
        for i, slot in enumerate(refs[2]):
            rows = slice(slot * seg, (slot + 1) * seg)
            out_ref[rows, mine] = refs[0][i * seg : (i + 1) * seg, mine]
            out_ref[rows, other] = refs[1][(1 - i) * seg : (2 - i) * seg, mine]


def attention_kernel(tile, seg, *refs):
    q_ref, here_refs, there_refs, blocks = refs[0], refs[1:5], refs[5:9], refs[9:13]
    dq_ref, outs, (kv, da_ref, dkt, dvt) = refs[13], refs[14:18], refs[18:]
    half, turn, pair, core = here()
    queries, keys = q_ref.shape[0], kv.shape[0]
    fill(kv, blocks)

    for which in range(CORES):

        @pl.when(core == which)
        def _(which=which):
            place_dattended(which, seg, here_refs, there_refs, da_ref)

    spot = lax.broadcasted_iota(jnp.int32, (1, keys), 1)
    block = spot // queries
    key_half = jnp.where(block < 2, half, 1 - half)
    key_pair = jnp.where(block % 2 == 0, pair, 1 - pair)
    key_at = rows_at(spot % queries, key_half, turn, key_pair, core, seg)
    turn_up = math.log2(math.e) / math.sqrt(HEAD)
    scale = 1.0 / math.sqrt(HEAD)
    k = kv[:, :HEAD]
    v = kv[:, HEAD:]
    for step in range(queries // tile):
        rows = slice(step * tile, (step + 1) * tile)
        query = lax.broadcasted_iota(jnp.int32, (tile, 1), 0) + step * tile
        query_at = rows_at(query, half, turn, pair, core, seg)
        q = q_ref[rows, :]
        da = da_ref[rows, :]
        score = jnp.where(key_at <= query_at, contract_last(q, k), NEG)
        peak = jnp.max(score, axis=1, keepdims=True)
        expo = jnp.exp2((score - peak) * turn_up)
        probs = expo * (1.0 / jnp.sum(expo, axis=1, keepdims=True))
        probs_b = probs.astype(jnp.bfloat16)
        attended = jnp.dot(probs_b, v, preferred_element_type=F32).astype(jnp.bfloat16)
        delta = jnp.sum(da.astype(F32) * attended.astype(F32), axis=1, keepdims=True)
        dscore = (probs * (contract_last(da, v) - delta)).astype(jnp.bfloat16)
        dq = jnp.dot(dscore, k, preferred_element_type=F32) * scale
        dq_ref[rows, :] = dq.astype(jnp.bfloat16)
        dk_part = contract_first(q, dscore)
        dv_part = contract_first(da, probs_b)
        if step == 0:
            dkt[...] = dk_part
            dvt[...] = dv_part
        else:
            dkt[...] += dk_part
            dvt[...] += dv_part
    at = 0
    for out in outs:
        lanes = slice(at, at + out.shape[0])
        at += out.shape[0]
        out[:, :HEAD] = (dkt[:, lanes] * scale).T.astype(jnp.bfloat16)
        out[:, HEAD:] = dvt[:, lanes].T.astype(jnp.bfloat16)


def attention(q, da_here, da_there, blocks, seg):
    queries = q.shape[0]
    keys = sum(block.shape[0] for block in blocks)
    parts = tuple(jax.ShapeDtypeStruct(block.shape, jnp.bfloat16) for block in blocks)
    return pl.pallas_call(
        functools.partial(attention_kernel, 256, seg),
        out_shape=(jax.ShapeDtypeStruct((queries, HEAD), jnp.bfloat16),) + parts,
        in_specs=[VMEM] * 13,
        out_specs=(VMEM,) * 5,
        scratch_shapes=[
            pltpu.VMEM((keys, 2 * HEAD), jnp.bfloat16),
            pltpu.VMEM((queries, HEAD), jnp.bfloat16),
            pltpu.VMEM((HEAD, keys), F32),
            pltpu.VMEM((HEAD, keys), F32),
        ],
        compiler_params=room(36),
        cost_estimate=pl.CostEstimate(
            flops=12 * queries * keys * HEAD,
            bytes_accessed=2 * HEAD * (3 * queries + 4 * keys),
            transcendentals=queries * keys,
        ),
    )(q, *da_here, *da_there, *blocks)


def unproject_kernel(seg, dq_ref, *refs):
    parts, w_ref, swap_ref, outs = refs[:4], refs[4], refs[5], refs[6:]
    dkv = sum(ref[...].astype(F32) for ref in parts).astype(jnp.bfloat16)
    left = jnp.concatenate([dq_ref[...], dkv], axis=1)
    out = contract_last(left, w_ref[...])
    for i, slot in enumerate((1, 4, 5, 7)):
        swap_ref[i * seg : (i + 1) * seg, :] = out[slot * seg : (slot + 1) * seg].astype(WIRE)
    for ref, slot in zip(outs, (0, 2, 3, 6)):
        ref[...] = out[slot * seg : (slot + 1) * seg]


def unproject(dq, parts, w_full, seg):
    width = w_full.shape[0]
    return pl.pallas_call(
        functools.partial(unproject_kernel, seg),
        out_shape=(jax.ShapeDtypeStruct((4 * seg, width), WIRE),)
        + (jax.ShapeDtypeStruct((seg, width), F32),) * 4,
        in_specs=[VMEM] * 6,
        out_specs=(VMEM,) * 5,
        compiler_params=room(16),
    )(dq, *parts, w_full)


def join_kernel(swapped, own, near, next_to, far, own_out, near_out, next_out, far_out):
    seg = own.shape[0]
    own_out[...] = own[...] + swapped[:seg, :].astype(F32)
    near_out[...] = near[...] + swapped[seg : 2 * seg, :].astype(F32)
    next_out[...] = (next_to[...] + swapped[2 * seg : 3 * seg, :].astype(F32)).astype(WIRE)
    far_out[...] = (far[...] + swapped[3 * seg :, :].astype(F32)).astype(WIRE)


def joined(swapped, own, near, next_to, far):
    wide = jax.ShapeDtypeStruct(own.shape, F32)
    thin = jax.ShapeDtypeStruct(own.shape, WIRE)
    return pl.pallas_call(
        join_kernel,
        out_shape=(wide, wide, thin, thin),
        in_specs=[VMEM] * 5,
        out_specs=(VMEM,) * 4,
        compiler_params=room(6),
    )(swapped, own, near, next_to, far)


def summed_rows(swap, own, near, next_to, far):
    own, near, next_to, far = joined(other_core(swap), own, near, next_to, far)
    far = turned(far, -1).astype(F32)
    next_to = turned_over(next_to).astype(F32)
    near = turned((near + far).astype(WIRE), -1).astype(F32)
    return own + next_to + near


def per_device(tokens, starts, gain, w_query, w_key, w_value, w_out, cotangent):
    token_rows = tokens[0]
    grad_out = cotangent[0]
    rows, width = token_rows.shape
    seg = starts.shape[1]
    length = rows * CTX
    ctx, core = lax.axis_index("ctx"), here()[3]

    mine, half, own_starts = cut_weights(w_query, w_key, w_value, w_out, starts)
    halves = gathered_halves(half)
    theirs = other_x(mine)
    beside, facing = other_core(own_starts), other_chip(own_starts)
    own_starts = starts
    to_core, to_chip, mid_token, mid_grad, first = window_sums(
        own_starts, beside, facing, token_rows, grad_out
    )
    before = jnp.where(core == 0, facing, beside)[0]
    after = jnp.where(core == 0, beside, facing)[0]
    before = jnp.where(ctx == 0, -1, before)
    after = jnp.where(ctx == CTX - 1, length, after)
    stop = jnp.full((1,), length, jnp.int32)
    window = jnp.concatenate([before, own_starts[0], after, stop])
    opens, ends = window[:-1], window[1:]
    count = (ends - opens)[seg : 2 * seg, None].astype(F32)
    second = two_back(first)
    normin, normed, rms, dout, both = norm(
        other_core(to_core),
        other_chip(to_chip),
        mid_token,
        mid_grad,
        count,
        gain[None],
        mine,
        theirs,
    )
    weights = [both, shifted_y(both, 1), shifted_y(both, -1), shifted_y(both, 2)]
    dout, dout_b = whole_dout(dout, second)
    dout_there = other_core(dout_b)
    pieces = gathered_rows(normin, [dout_there], weights[1:])
    q, own, w_full, *da = project(pieces, weights, (dout_b, dout_there), halves)
    cross, far, beside = across(own, 0, True), across(own, 0, False), other_pair(own)
    da_here = [da[0]] + [
        moved(da[i], lambda h, t, p, k, i=i: (h, t + i, p, k)) for i in range(1, TURNS)
    ]
    da_there = [other_core(piece) for piece in da_here]
    blocks = (own, beside, far, cross)
    dq, own, beside, far, cross = attention(q, da_here, da_there, blocks, seg)
    parts = (own, other_pair(beside), across(far, 1, False), across(cross, 1, True))
    dnormin = summed_rows(*unproject(dq, parts, w_full, seg))

    scaled = dnormin * gain
    dpooled = dout + (scaled - normed * jnp.mean(scaled * normed, axis=-1, keepdims=True)) / rms
    per_seg = (dpooled / count).astype(WIRE)
    beside, facing = other_core(per_seg), other_chip(per_seg)
    before = jnp.where(core == 0, facing, beside)
    after = jnp.where(core == 0, beside, facing)
    per_window = jnp.concatenate([before, per_seg, after], axis=0)
    positions = (ctx * rows + lax.iota(jnp.int32, rows))[:, None]
    member = (opens[None] <= positions) & (positions < ends[None])
    spread = jnp.dot(member.astype(WIRE), per_window, preferred_element_type=F32)
    return (grad_out.astype(F32) + spread).astype(jnp.bfloat16)[None]


def solution(mesh):
    return jax.shard_map(
        per_device,
        mesh=mesh,
        in_specs=(
            P("dp", "ctx", None),
            P("dp", "ctx"),
            P(),
            P("dp", None),
            P("dp", None),
            P("dp", None),
            P("dp", None),
            P("dp", "ctx", None),
        ),
        out_specs=P("dp", "ctx", None),
        check_vma=False,
    )
```

```python
import functools
import math

import jax
import jax.numpy as jnp
from jax import lax
from jax.experimental import pallas as pl
from jax.experimental.pallas import tpu as pltpu
from jax.sharding import PartitionSpec as P

HEAD = 128
HALVES, TURNS, PAIR, CORES = 2, 4, 2, 2
CTX = HALVES * TURNS * PAIR * CORES
ROWS_X, ROWS_Y = 2, 4
NEG = -1e30
WIRE = jnp.bfloat16
F32 = jnp.float32
VMEM = pl.BlockSpec(memory_space=pltpu.VMEM)
ANY = pl.BlockSpec(memory_space=pl.ANY)
HBM = pl.BlockSpec(memory_space=pltpu.HBM)


def room(mib):
    return pltpu.CompilerParams(vmem_limit_bytes=mib * 1024 * 1024)


def place(half, turn, pair, core):
    return ((half * TURNS + turn % TURNS) * PAIR + pair) * CORES + core


def here():
    ctx = lax.axis_index("ctx")
    core, pair = ctx % CORES, ctx // CORES % PAIR
    return ctx // (CORES * PAIR * TURNS), ctx // (CORES * PAIR) % TURNS, pair, core


def moved(value, to):
    spots = [
        (h, t, p, k)
        for h in range(HALVES)
        for t in range(TURNS)
        for p in range(PAIR)
        for k in range(CORES)
    ]
    pairs = [(place(*s), place(*to(*s))) for s in spots if to(*s) is not None]
    return lax.ppermute(value, "ctx", pairs)


def other_chip(value):
    pairs = [(i, i + 1 if i % CORES else i - 1) for i in range(1, CTX - 1)]
    return lax.ppermute(value, "ctx", pairs)


def two_back(value):
    return lax.ppermute(value, "ctx", [(i, i - CORES) for i in range(CORES, CTX)])


def other_core(value):
    return moved(value, lambda h, t, p, k: (h, t, p, 1 - k))


def other_pair(value):
    return moved(value, lambda h, t, p, k: (h, t, 1 - p, k))


def across(value, source, cross):
    return moved(
        value,
        lambda h, t, p, k: (1 - h, t, 1 - p if cross else p, k) if h == source else None,
    )


def turned(value, way):
    return moved(value, lambda h, t, p, k: (h, t + way * (1 - 2 * k), p, k))


def turned_over(value):
    return moved(value, lambda h, t, p, k: (h, t - (1 - 2 * k), p, 1 - k))


def contract_last(left, right):
    return lax.dot_general(left, right, (((1,), (1,)), ((), ())), preferred_element_type=F32)


def contract_first(left, right):
    return lax.dot_general(left, right, (((0,), (0,)), ((), ())), preferred_element_type=F32)


def cut_kernel(q_ref, k_ref, v_ref, o_ref, start_ref, out_ref, half_ref, start_out, sems):
    _, turn, _, core = here()
    lane = pl.multiple_of((turn * CORES + core) * HEAD, HEAD)
    copies = [
        (w.at[:, pl.ds(lane, HEAD)], out_ref.at[:, i * HEAD : (i + 1) * HEAD])
        for i, w in enumerate((q_ref, k_ref, v_ref))
    ]
    half = half_ref.shape[0]
    copies.append((o_ref.at[pl.ds(pl.multiple_of(core * half, half), half), :], half_ref))
    copies.append((start_ref, start_out))
    fetched(copies, sems)


def cut_weights(w_query, w_key, w_value, w_out, starts):
    rows, width = w_out.shape
    return pl.pallas_call(
        cut_kernel,
        out_shape=(
            jax.ShapeDtypeStruct((rows, 3 * HEAD), w_query.dtype),
            jax.ShapeDtypeStruct((rows // CORES, width), w_out.dtype),
            jax.ShapeDtypeStruct(starts.shape, starts.dtype),
        ),
        in_specs=[HBM] * 4 + [ANY],
        out_specs=(VMEM, VMEM, VMEM),
        scratch_shapes=[pltpu.SemaphoreType.DMA((5,))],
        compiler_params=room(60),
    )(w_query, w_key, w_value, w_out, starts)


def other_x(value):
    count = ROWS_X * ROWS_Y
    return lax.ppermute(value, "dp", [(d, (d + ROWS_Y) % count) for d in range(count)])


def shifted_y(value, step):
    pairs = [(d, d // ROWS_Y * ROWS_Y + (d + step) % ROWS_Y) for d in range(ROWS_X * ROWS_Y)]
    return lax.ppermute(value, "dp", pairs)


def gathered_halves(half):
    return lax.all_gather(half, "dp", axis=0, tiled=False)


def pass_kernel(value_ref, *refs):
    refs[-1][...] = value_ref[...]


def passed_on(value, *ready):
    return pl.pallas_call(
        pass_kernel,
        out_shape=jax.ShapeDtypeStruct(value.shape, value.dtype),
        in_specs=[VMEM] + [ANY] * len(ready),
        out_specs=VMEM,
        compiler_params=room(4),
    )(value, *ready)


def gathered_rows(shard, first_ready, last_ready):
    near = turned(shard, 1)
    next_to = turned_over(passed_on(shard, near))
    far = passed_on(turned(passed_on(near, *first_ready), 1), *last_ready)
    return [
        shard,
        other_core(shard),
        near,
        next_to,
        other_core(near),
        other_core(next_to),
        far,
        other_core(far),
    ]


def rows_at(row, half, turn, pair, core, seg):
    slot = row // seg
    two = slot // 2
    way = 1 - 2 * core
    step = jnp.where(two == 0, 0, jnp.where(two == 1, way, jnp.where(two == 2, -way, 2)))
    flip = jnp.where(two == 2, 1 - slot % 2, slot % 2)
    its_core = jnp.where(flip == 1, 1 - core, core)
    its_turn = (turn - step + TURNS) % TURNS
    return place(half, its_turn, pair, its_core) * seg + row % seg


def fetched(copies, sems):
    started = []
    for i, (source, target) in enumerate(copies):
        started.append(pltpu.make_async_copy(source, target, sems.at[i]))
        started[-1].start()
    for copy in started:
        copy.wait()


def fill(out_ref, pieces):
    at = 0
    for piece in pieces:
        out_ref[at : at + piece.shape[0], :] = piece[...]
        at += piece.shape[0]


def window_kernel(own_ref, beside_ref, facing_ref, token_hbm, grad_hbm, *refs):
    core_ref, chip_ref, mid_token, mid_grad, first_ref = refs[:5]
    token_ref, grad_ref, sems = refs[5:]
    rows, width = token_ref.shape
    seg = mid_token.shape[0]
    token_copy = pltpu.make_async_copy(token_hbm, token_ref, sems.at[0])
    grad_copy = pltpu.make_async_copy(grad_hbm, grad_ref, sems.at[1])
    token_copy.start()
    grad_copy.start()
    ctx, core = lax.axis_index("ctx"), here()[3]
    at = lax.broadcasted_iota(jnp.int32, (rows, 1), 0) + ctx * rows
    before = jnp.where(core == 0, facing_ref[...], beside_ref[...])
    after = jnp.where(core == 0, beside_ref[...], facing_ref[...])
    before = jnp.where(ctx == 0, -1, before)
    after = jnp.where(ctx == CTX - 1, rows * CTX, after)
    begun = [(part <= at).astype(jnp.int32) for part in (before, own_ref[...], after)]
    slot = sum(jnp.sum(part, axis=1, keepdims=True) for part in begun) - 1
    slots = lax.broadcasted_iota(jnp.int32, (1, 3 * seg), 1)
    member = (slots == slot).astype(jnp.bfloat16)
    earlier = (slots == slot - 1).astype(jnp.bfloat16)
    token_copy.wait()
    token = contract_first(member, token_ref[...])
    grad_copy.wait()
    grad = contract_first(earlier, grad_ref[...])
    outside = jnp.broadcast_to((slot == 0).astype(jnp.bfloat16), (rows, HEAD))
    first_ref[...] = contract_first(outside, grad_ref[...])[:1]
    mid_token[...] = token[seg : 2 * seg]
    mid_grad[...] = grad[seg : 2 * seg]

    def send(lower_ref, upper_ref):
        lower_ref[:, :width] = token[:seg].astype(WIRE)
        lower_ref[:, width:] = grad[:seg].astype(WIRE)
        upper_ref[:, :width] = token[2 * seg :].astype(WIRE)
        upper_ref[:, width:] = grad[2 * seg :].astype(WIRE)

    @pl.when(core == 0)
    def _():
        send(chip_ref, core_ref)

    @pl.when(core == 1)
    def _():
        send(core_ref, chip_ref)


def window_sums(own, beside, facing, tokens, grads):
    rows, width = tokens.shape
    seg = own.shape[1]
    shape = jax.ShapeDtypeStruct
    return pl.pallas_call(
        window_kernel,
        out_shape=(
            shape((seg, 2 * width), WIRE),
            shape((seg, 2 * width), WIRE),
            shape((seg, width), F32),
            shape((seg, width), F32),
            shape((1, width), F32),
        ),
        in_specs=[VMEM] * 3 + [HBM] * 2,
        out_specs=(VMEM,) * 5,
        scratch_shapes=[
            pltpu.VMEM((rows, width), tokens.dtype),
            pltpu.VMEM((rows, width), grads.dtype),
            pltpu.SemaphoreType.DMA((2,)),
        ],
        compiler_params=room(16),
    )(own, beside, facing, tokens, grads)


def norm_kernel(core_ref, chip_ref, mid_token, mid_grad, count_ref, gain_ref, *refs):
    mine_ref, theirs_ref, normin_ref, normed_ref, rms_ref, dout_ref, pair_ref = refs
    width = mid_token.shape[1]
    rows = mine_ref.shape[0]
    pair_ref[:rows, :] = mine_ref[...]
    pair_ref[rows:, :] = theirs_ref[...]
    got = core_ref[...].astype(F32) + chip_ref[...].astype(F32)
    pooled = (mid_token[...] + got[:, :width]) / count_ref[...]
    rms = jnp.sqrt(jnp.mean(pooled * pooled, axis=1, keepdims=True) + 1e-06)
    normed = pooled / rms
    normed_ref[...] = normed
    rms_ref[...] = rms
    normin_ref[...] = (normed * gain_ref[...]).astype(jnp.bfloat16)
    dout_ref[...] = mid_grad[...] + got[:, width:]


def norm(from_core, from_chip, mid_token, mid_grad, count, gain, mine, theirs):
    seg, width = mid_token.shape
    shape = jax.ShapeDtypeStruct
    return pl.pallas_call(
        norm_kernel,
        out_shape=(
            shape((seg, width), jnp.bfloat16),
            shape((seg, width), F32),
            shape((seg, 1), F32),
            shape((seg, width), F32),
            shape((2 * mine.shape[0], mine.shape[1]), mine.dtype),
        ),
        in_specs=[VMEM] * 8,
        out_specs=(VMEM,) * 5,
        compiler_params=room(8),
    )(from_core, from_chip, mid_token, mid_grad, count, gain, mine, theirs)


def dout_kernel(dout_ref, second_ref, full_ref, half_ref):
    seg = dout_ref.shape[0]
    last = lax.broadcasted_iota(jnp.int32, (seg, 1), 0) == seg - 1
    dout = dout_ref[...] + jnp.where(last, second_ref[...], 0.0)
    full_ref[...] = dout
    half_ref[...] = dout.astype(jnp.bfloat16)


def whole_dout(dout, second):
    shape = jax.ShapeDtypeStruct
    return pl.pallas_call(
        dout_kernel,
        out_shape=(shape(dout.shape, F32), shape(dout.shape, jnp.bfloat16)),
        in_specs=[VMEM, VMEM],
        out_specs=(VMEM, VMEM),
        compiler_params=room(4),
    )(dout, second)


def project_kernel(*refs):
    pieces, weights, douts, halves = refs[:8], refs[8:12], refs[12:14], refs[14]
    q_ref, kv_ref, w_ref, outs = *refs[15:18], refs[18:22]
    rows, chip_rows, w_back, sems = refs[22:]
    heads, half = halves.shape[:2]
    started = []
    for i in range(heads):
        target = w_back.at[i * half : (i + 1) * half, :]
        started.append(pltpu.make_async_copy(halves.at[i], target, sems.at[i]))
        started[-1].start()
    fill(rows, pieces)
    fill(chip_rows, douts)
    dp = lax.axis_index("dp")
    x, y = dp // ROWS_Y, dp % ROWS_Y
    depth = weights[0].shape[0] // ROWS_X
    for weight, step in zip(weights, (0, 1, -1, 2)):
        its_y = (y - step + ROWS_Y) % ROWS_Y
        for i in range(ROWS_X):
            its_x = x if i == 0 else 1 - x
            at = pl.multiple_of((its_x * ROWS_Y + its_y) * depth, depth)
            w_ref[pl.ds(at, depth), :] = weight[i * depth : (i + 1) * depth, :]
    out = jnp.dot(rows[...], w_ref[...], preferred_element_type=F32).astype(jnp.bfloat16)
    q_ref[...] = out[:, :HEAD]
    kv_ref[...] = out[:, HEAD:]
    for copy in started:
        copy.wait()
    turn = here()[1]
    for step, ref in enumerate(outs):
        at = pl.multiple_of((turn + step) % TURNS * CORES * half, CORES * half)
        part = w_back[pl.ds(at, CORES * half), :]
        ref[...] = contract_last(chip_rows[...], part).astype(jnp.bfloat16)


def project(pieces, weights, douts, halves):
    seg, width = pieces[0].shape
    rows = seg * len(pieces)
    heads, half = halves.shape[:2]
    bf16 = lambda *shape: jax.ShapeDtypeStruct(shape, jnp.bfloat16)
    return pl.pallas_call(
        project_kernel,
        out_shape=(bf16(rows, HEAD), bf16(rows, 2 * HEAD), bf16(width, 3 * HEAD))
        + (bf16(2 * seg, CORES * half),) * TURNS,
        in_specs=[VMEM] * 14 + [ANY],
        out_specs=(VMEM,) * (3 + TURNS),
        scratch_shapes=[
            pltpu.VMEM((rows, width), jnp.bfloat16),
            pltpu.VMEM((2 * seg, width), jnp.bfloat16),
            pltpu.VMEM((heads * half, width), jnp.bfloat16),
            pltpu.SemaphoreType.DMA((heads,)),
        ],
        compiler_params=room(50),
    )(*pieces, *weights, *douts, halves)


def place_dattended(core, seg, here_refs, there_refs, out_ref):
    half = out_ref.shape[1] // CORES
    mine = slice(core * half, (core + 1) * half)
    other = slice((1 - core) * half, (2 - core) * half)
    slots = ((0, 1), (2, 3), (6, 7), (5, 4)) if core == 0 else ((0, 1), (5, 4), (6, 7), (2, 3))
    for refs in zip(here_refs, there_refs, slots):
        for i, slot in enumerate(refs[2]):
            rows = slice(slot * seg, (slot + 1) * seg)
            out_ref[rows, mine] = refs[0][i * seg : (i + 1) * seg, mine]
            out_ref[rows, other] = refs[1][(1 - i) * seg : (2 - i) * seg, mine]


def attention_kernel(tile, seg, *refs):
    q_ref, here_refs, there_refs, blocks = refs[0], refs[1:5], refs[5:9], refs[9:13]
    dq_ref, outs, (kv, da_ref, dkt, dvt) = refs[13], refs[14:18], refs[18:]
    half, turn, pair, core = here()
    queries = q_ref.shape[0]
    for which in range(CORES):

        @pl.when(core == which)
        def _(which=which):
            place_dattended(which, seg, here_refs, there_refs, da_ref)

    turn_up = math.log2(math.e) / math.sqrt(HEAD)
    scale = 1.0 / math.sqrt(HEAD)

    def run(used):
        keys = used * queries
        fill(kv, blocks[:used])
        near = 2 * queries
        spot = lax.broadcasted_iota(jnp.int32, (1, near), 1)
        key_pair = jnp.where(spot < queries, pair, 1 - pair)
        key_at = rows_at(spot % queries, half, turn, key_pair, core, seg)
        k = kv[:keys, :HEAD]
        v = kv[:keys, HEAD:]
        for step in range(queries // tile):
            rows = slice(step * tile, (step + 1) * tile)
            query = lax.broadcasted_iota(jnp.int32, (tile, 1), 0) + step * tile
            query_at = rows_at(query, half, turn, pair, core, seg)
            q = q_ref[rows, :]
            da = da_ref[rows, :]
            score = contract_last(q, k)
            masked = jnp.where(key_at <= query_at, score[:, :near], NEG)
            score = masked if used == 2 else jnp.concatenate([masked, score[:, near:]], axis=1)
            peak = jnp.max(score, axis=1, keepdims=True)
            expo = jnp.exp2((score - peak) * turn_up)
            probs = expo * (1.0 / jnp.sum(expo, axis=1, keepdims=True))
            probs_b = probs.astype(jnp.bfloat16)
            attended = jnp.dot(probs_b, v, preferred_element_type=F32).astype(jnp.bfloat16)
            delta = jnp.sum(da.astype(F32) * attended.astype(F32), axis=1, keepdims=True)
            dscore = (probs * (contract_last(da, v) - delta)).astype(jnp.bfloat16)
            dq = jnp.dot(dscore, k, preferred_element_type=F32) * scale
            dq_ref[rows, :] = dq.astype(jnp.bfloat16)
            dk_part = contract_first(q, dscore)
            dv_part = contract_first(da, probs_b)
            if step == 0:
                dkt[:, :keys] = dk_part
                dvt[:, :keys] = dv_part
            else:
                dkt[:, :keys] += dk_part
                dvt[:, :keys] += dv_part
        for i, out in enumerate(outs[:used]):
            lanes = slice(i * queries, (i + 1) * queries)
            out[:, :HEAD] = (dkt[:, lanes] * scale).T.astype(jnp.bfloat16)
            out[:, HEAD:] = dvt[:, lanes].T.astype(jnp.bfloat16)

    @pl.when(half == 0)
    def _():
        run(2)
        for out in outs[2:]:
            out[...] = jnp.zeros_like(out)

    @pl.when(half == 1)
    def _():
        run(4)


def attention(q, da_here, da_there, blocks, seg):
    queries = q.shape[0]
    keys = sum(block.shape[0] for block in blocks)
    parts = tuple(jax.ShapeDtypeStruct(block.shape, jnp.bfloat16) for block in blocks)
    return pl.pallas_call(
        functools.partial(attention_kernel, 256, seg),
        out_shape=(jax.ShapeDtypeStruct((queries, HEAD), jnp.bfloat16),) + parts,
        in_specs=[VMEM] * 13,
        out_specs=(VMEM,) * 5,
        scratch_shapes=[
            pltpu.VMEM((keys, 2 * HEAD), jnp.bfloat16),
            pltpu.VMEM((queries, HEAD), jnp.bfloat16),
            pltpu.VMEM((HEAD, keys), F32),
            pltpu.VMEM((HEAD, keys), F32),
        ],
        compiler_params=room(36),
        cost_estimate=pl.CostEstimate(
            flops=12 * queries * keys * HEAD,
            bytes_accessed=2 * HEAD * (3 * queries + 4 * keys),
            transcendentals=queries * keys,
        ),
    )(q, *da_here, *da_there, *blocks)


def unproject_kernel(seg, dq_ref, *refs):
    parts, w_ref, swap_ref, outs = refs[:4], refs[4], refs[5], refs[6:]
    dkv = sum(ref[...].astype(F32) for ref in parts).astype(jnp.bfloat16)
    left = jnp.concatenate([dq_ref[...], dkv], axis=1)
    out = contract_last(left, w_ref[...])
    for i, slot in enumerate((1, 4, 5, 7)):
        swap_ref[i * seg : (i + 1) * seg, :] = out[slot * seg : (slot + 1) * seg].astype(WIRE)
    for ref, slot in zip(outs, (0, 2, 3, 6)):
        ref[...] = out[slot * seg : (slot + 1) * seg]


def unproject(dq, parts, w_full, seg):
    width = w_full.shape[0]
    return pl.pallas_call(
        functools.partial(unproject_kernel, seg),
        out_shape=(jax.ShapeDtypeStruct((4 * seg, width), WIRE),)
        + (jax.ShapeDtypeStruct((seg, width), F32),) * 4,
        in_specs=[VMEM] * 6,
        out_specs=(VMEM,) * 5,
        compiler_params=room(16),
    )(dq, *parts, w_full)


def join_kernel(swapped, own, near, next_to, far, own_out, near_out, next_out, far_out):
    seg = own.shape[0]
    own_out[...] = own[...] + swapped[:seg, :].astype(F32)
    near_out[...] = near[...] + swapped[seg : 2 * seg, :].astype(F32)
    next_out[...] = (next_to[...] + swapped[2 * seg : 3 * seg, :].astype(F32)).astype(WIRE)
    far_out[...] = (far[...] + swapped[3 * seg :, :].astype(F32)).astype(WIRE)


def joined(swapped, own, near, next_to, far):
    wide = jax.ShapeDtypeStruct(own.shape, F32)
    thin = jax.ShapeDtypeStruct(own.shape, WIRE)
    return pl.pallas_call(
        join_kernel,
        out_shape=(wide, wide, thin, thin),
        in_specs=[VMEM] * 5,
        out_specs=(VMEM,) * 4,
        compiler_params=room(6),
    )(swapped, own, near, next_to, far)


def summed_rows(swap, own, near, next_to, far):
    own, near, next_to, far = joined(other_core(swap), own, near, next_to, far)
    far = turned(far, -1).astype(F32)
    next_to = turned_over(next_to).astype(F32)
    near = turned((near + far).astype(WIRE), -1).astype(F32)
    return own + next_to + near


def per_device(tokens, starts, gain, w_query, w_key, w_value, w_out, cotangent):
    token_rows = tokens[0]
    grad_out = cotangent[0]
    rows, width = token_rows.shape
    seg = starts.shape[1]
    length = rows * CTX
    ctx, core = lax.axis_index("ctx"), here()[3]

    mine, half, own_starts = cut_weights(w_query, w_key, w_value, w_out, starts)
    halves = gathered_halves(half)
    theirs = other_x(mine)
    beside, facing = other_core(own_starts), other_chip(own_starts)
    own_starts = starts
    to_core, to_chip, mid_token, mid_grad, first = window_sums(
        own_starts, beside, facing, token_rows, grad_out
    )
    before = jnp.where(core == 0, facing, beside)[0]
    after = jnp.where(core == 0, beside, facing)[0]
    before = jnp.where(ctx == 0, -1, before)
    after = jnp.where(ctx == CTX - 1, length, after)
    stop = jnp.full((1,), length, jnp.int32)
    window = jnp.concatenate([before, own_starts[0], after, stop])
    opens, ends = window[:-1], window[1:]
    count = (ends - opens)[seg : 2 * seg, None].astype(F32)
    second = two_back(first)
    normin, normed, rms, dout, both = norm(
        other_core(to_core),
        other_chip(to_chip),
        mid_token,
        mid_grad,
        count,
        gain[None],
        mine,
        theirs,
    )
    weights = [both, shifted_y(both, 1), shifted_y(both, -1), shifted_y(both, 2)]
    dout, dout_b = whole_dout(dout, second)
    dout_there = other_core(dout_b)
    pieces = gathered_rows(normin, [dout_there], weights[1:])
    q, own, w_full, *da = project(pieces, weights, (dout_b, dout_there), halves)
    far, beside = across(own, 0, False), other_pair(own)
    da_here = [da[0]] + [
        moved(da[i], lambda h, t, p, k, i=i: (h, t + i, p, k)) for i in range(1, TURNS)
    ]
    cross = across(passed_on(own, *da_here[1:]), 0, True)
    da_there = [other_core(piece) for piece in da_here]
    blocks = (own, beside, far, cross)
    dq, own, beside, far, cross = attention(q, da_here, da_there, blocks, seg)
    parts = (own, other_pair(beside), across(far, 1, False), across(cross, 1, True))
    dnormin = summed_rows(*unproject(dq, parts, w_full, seg))

    scaled = dnormin * gain
    dpooled = dout + (scaled - normed * jnp.mean(scaled * normed, axis=-1, keepdims=True)) / rms
    per_seg = (dpooled / count).astype(WIRE)
    beside, facing = other_core(per_seg), other_chip(per_seg)
    before = jnp.where(core == 0, facing, beside)
    after = jnp.where(core == 0, beside, facing)
    per_window = jnp.concatenate([before, per_seg, after], axis=0)
    positions = (ctx * rows + lax.iota(jnp.int32, rows))[:, None]
    member = (opens[None] <= positions) & (positions < ends[None])
    spread = jnp.dot(member.astype(WIRE), per_window, preferred_element_type=F32)
    return (grad_out.astype(F32) + spread).astype(jnp.bfloat16)[None]


def solution(mesh):
    return jax.shard_map(
        per_device,
        mesh=mesh,
        in_specs=(
            P("dp", "ctx", None),
            P("dp", "ctx"),
            P(),
            P("dp", None),
            P("dp", None),
            P("dp", None),
            P("dp", None),
            P("dp", "ctx", None),
        ),
        out_specs=P("dp", "ctx", None),
        check_vma=False,
    )
```

```python
import functools
import math

import jax
import jax.numpy as jnp
from jax import lax
from jax.experimental import pallas as pl
from jax.experimental.pallas import tpu as pltpu
from jax.sharding import PartitionSpec as P

HEAD = 128
HALVES, TURNS, PAIR, CORES = 2, 4, 2, 2
CTX = HALVES * TURNS * PAIR * CORES
ROWS_X, ROWS_Y = 2, 4
NEG = -1e30
WIRE = jnp.bfloat16
F32 = jnp.float32
VMEM = pl.BlockSpec(memory_space=pltpu.VMEM)
ANY = pl.BlockSpec(memory_space=pl.ANY)
HBM = pl.BlockSpec(memory_space=pltpu.HBM)


def room(mib):
    return pltpu.CompilerParams(vmem_limit_bytes=mib * 1024 * 1024)


def place(half, turn, pair, core):
    return ((half * TURNS + turn % TURNS) * PAIR + pair) * CORES + core


def here():
    ctx = lax.axis_index("ctx")
    core, pair = ctx % CORES, ctx // CORES % PAIR
    return ctx // (CORES * PAIR * TURNS), ctx // (CORES * PAIR) % TURNS, pair, core


def moved(value, to):
    spots = [
        (h, t, p, k)
        for h in range(HALVES)
        for t in range(TURNS)
        for p in range(PAIR)
        for k in range(CORES)
    ]
    pairs = [(place(*s), place(*to(*s))) for s in spots if to(*s) is not None]
    return lax.ppermute(value, "ctx", pairs)


def other_chip(value):
    pairs = [(i, i + 1 if i % CORES else i - 1) for i in range(1, CTX - 1)]
    return lax.ppermute(value, "ctx", pairs)


def two_back(value):
    return lax.ppermute(value, "ctx", [(i, i - CORES) for i in range(CORES, CTX)])


def other_core(value):
    return moved(value, lambda h, t, p, k: (h, t, p, 1 - k))


def other_pair(value):
    return moved(value, lambda h, t, p, k: (h, t, 1 - p, k))


def across(value, source, cross):
    return moved(
        value,
        lambda h, t, p, k: (1 - h, t, 1 - p if cross else p, k) if h == source else None,
    )


def turned(value, way):
    return moved(value, lambda h, t, p, k: (h, t + way * (1 - 2 * k), p, k))


def turned_over(value):
    return moved(value, lambda h, t, p, k: (h, t - (1 - 2 * k), p, 1 - k))


def contract_last(left, right):
    return lax.dot_general(left, right, (((1,), (1,)), ((), ())), preferred_element_type=F32)


def contract_first(left, right):
    return lax.dot_general(left, right, (((0,), (0,)), ((), ())), preferred_element_type=F32)


def half_kernel(o_ref, start_ref, half_ref, start_out, sems):
    half = half_ref.shape[0]
    at = pl.multiple_of(here()[3] * half, half)
    fetched([(o_ref.at[pl.ds(at, half), :], half_ref), (start_ref, start_out)], sems)


def cut_rows(w_out, starts):
    rows, width = w_out.shape
    return pl.pallas_call(
        half_kernel,
        out_shape=(
            jax.ShapeDtypeStruct((rows // CORES, width), w_out.dtype),
            jax.ShapeDtypeStruct(starts.shape, starts.dtype),
        ),
        in_specs=[HBM, ANY],
        out_specs=(VMEM, VMEM),
        scratch_shapes=[pltpu.SemaphoreType.DMA((2,))],
        compiler_params=room(60),
    )(w_out, starts)


def cut_kernel(q_ref, k_ref, v_ref, ready_ref, out_ref, sems):
    _, turn, _, core = here()
    lane = pl.multiple_of((turn * CORES + core) * HEAD, HEAD)
    copies = [
        (w.at[:, pl.ds(lane, HEAD)], out_ref.at[:, i * HEAD : (i + 1) * HEAD])
        for i, w in enumerate((q_ref, k_ref, v_ref))
    ]
    fetched(copies, sems)


def cut_columns(w_query, w_key, w_value, ready):
    return pl.pallas_call(
        cut_kernel,
        out_shape=jax.ShapeDtypeStruct((w_query.shape[0], 3 * HEAD), w_query.dtype),
        in_specs=[HBM] * 3 + [ANY],
        out_specs=VMEM,
        scratch_shapes=[pltpu.SemaphoreType.DMA((3,))],
        compiler_params=room(60),
    )(w_query, w_key, w_value, ready)


def other_x(value):
    count = ROWS_X * ROWS_Y
    return lax.ppermute(value, "dp", [(d, (d + ROWS_Y) % count) for d in range(count)])


def shifted_y(value, step):
    pairs = [(d, d // ROWS_Y * ROWS_Y + (d + step) % ROWS_Y) for d in range(ROWS_X * ROWS_Y)]
    return lax.ppermute(value, "dp", pairs)


def gathered_halves(half):
    return lax.all_gather(half, "dp", axis=0, tiled=False)


def pass_kernel(value_ref, *refs):
    refs[-1][...] = value_ref[...]


def passed_on(value, *ready):
    return pl.pallas_call(
        pass_kernel,
        out_shape=jax.ShapeDtypeStruct(value.shape, value.dtype),
        in_specs=[VMEM] + [ANY] * len(ready),
        out_specs=VMEM,
        compiler_params=room(4),
    )(value, *ready)


def gathered_rows(shard, first_ready, last_ready):
    near = turned(shard, 1)
    near_there = other_core(near)
    next_to = turned_over(passed_on(shard, near, *first_ready))
    far = passed_on(turned(near, 1), *last_ready)
    return [
        shard,
        other_core(shard),
        near,
        next_to,
        near_there,
        other_core(next_to),
        far,
        other_core(far),
    ]


def rows_at(row, half, turn, pair, core, seg):
    slot = row // seg
    two = slot // 2
    way = 1 - 2 * core
    step = jnp.where(two == 0, 0, jnp.where(two == 1, way, jnp.where(two == 2, -way, 2)))
    flip = jnp.where(two == 2, 1 - slot % 2, slot % 2)
    its_core = jnp.where(flip == 1, 1 - core, core)
    its_turn = (turn - step + TURNS) % TURNS
    return place(half, its_turn, pair, its_core) * seg + row % seg


def fetched(copies, sems):
    started = []
    for i, (source, target) in enumerate(copies):
        started.append(pltpu.make_async_copy(source, target, sems.at[i]))
        started[-1].start()
    for copy in started:
        copy.wait()


def fill(out_ref, pieces):
    at = 0
    for piece in pieces:
        out_ref[at : at + piece.shape[0], :] = piece[...]
        at += piece.shape[0]


def window_kernel(own_ref, beside_ref, facing_ref, token_hbm, grad_hbm, *refs):
    core_ref, chip_ref, mid_token, mid_grad, first_ref = refs[:5]
    token_ref, grad_ref, sems = refs[5:]
    rows, width = token_ref.shape
    seg = mid_token.shape[0]
    token_copy = pltpu.make_async_copy(token_hbm, token_ref, sems.at[0])
    grad_copy = pltpu.make_async_copy(grad_hbm, grad_ref, sems.at[1])
    token_copy.start()
    grad_copy.start()
    ctx, core = lax.axis_index("ctx"), here()[3]
    at = lax.broadcasted_iota(jnp.int32, (rows, 1), 0) + ctx * rows
    before = jnp.where(core == 0, facing_ref[...], beside_ref[...])
    after = jnp.where(core == 0, beside_ref[...], facing_ref[...])
    before = jnp.where(ctx == 0, -1, before)
    after = jnp.where(ctx == CTX - 1, rows * CTX, after)
    begun = [(part <= at).astype(jnp.int32) for part in (before, own_ref[...], after)]
    slot = sum(jnp.sum(part, axis=1, keepdims=True) for part in begun) - 1
    slots = lax.broadcasted_iota(jnp.int32, (1, 3 * seg), 1)
    member = (slots == slot).astype(jnp.bfloat16)
    earlier = (slots == slot - 1).astype(jnp.bfloat16)
    token_copy.wait()
    token = contract_first(member, token_ref[...])
    grad_copy.wait()
    grad = contract_first(earlier, grad_ref[...])
    outside = jnp.broadcast_to((slot == 0).astype(jnp.bfloat16), (rows, HEAD))
    first_ref[...] = contract_first(outside, grad_ref[...])[:1]
    mid_token[...] = token[seg : 2 * seg]
    mid_grad[...] = grad[seg : 2 * seg]

    def send(lower_ref, upper_ref):
        lower_ref[:, :width] = token[:seg].astype(WIRE)
        lower_ref[:, width:] = grad[:seg].astype(WIRE)
        upper_ref[:, :width] = token[2 * seg :].astype(WIRE)
        upper_ref[:, width:] = grad[2 * seg :].astype(WIRE)

    @pl.when(core == 0)
    def _():
        send(chip_ref, core_ref)

    @pl.when(core == 1)
    def _():
        send(core_ref, chip_ref)


def window_sums(own, beside, facing, tokens, grads):
    rows, width = tokens.shape
    seg = own.shape[1]
    shape = jax.ShapeDtypeStruct
    return pl.pallas_call(
        window_kernel,
        out_shape=(
            shape((seg, 2 * width), WIRE),
            shape((seg, 2 * width), WIRE),
            shape((seg, width), F32),
            shape((seg, width), F32),
            shape((1, width), F32),
        ),
        in_specs=[VMEM] * 3 + [HBM] * 2,
        out_specs=(VMEM,) * 5,
        scratch_shapes=[
            pltpu.VMEM((rows, width), tokens.dtype),
            pltpu.VMEM((rows, width), grads.dtype),
            pltpu.SemaphoreType.DMA((2,)),
        ],
        compiler_params=room(16),
    )(own, beside, facing, tokens, grads)


def norm_kernel(core_ref, chip_ref, mid_token, mid_grad, count_ref, gain_ref, *refs):
    mine_ref, theirs_ref, normin_ref, normed_ref, rms_ref, dout_ref, pair_ref = refs
    width = mid_token.shape[1]
    rows = mine_ref.shape[0]
    pair_ref[:rows, :] = mine_ref[...]
    pair_ref[rows:, :] = theirs_ref[...]
    got = core_ref[...].astype(F32) + chip_ref[...].astype(F32)
    pooled = (mid_token[...] + got[:, :width]) / count_ref[...]
    rms = jnp.sqrt(jnp.mean(pooled * pooled, axis=1, keepdims=True) + 1e-06)
    normed = pooled / rms
    normed_ref[...] = normed
    rms_ref[...] = rms
    normin_ref[...] = (normed * gain_ref[...]).astype(jnp.bfloat16)
    dout_ref[...] = mid_grad[...] + got[:, width:]


def norm(from_core, from_chip, mid_token, mid_grad, count, gain, mine, theirs):
    seg, width = mid_token.shape
    shape = jax.ShapeDtypeStruct
    return pl.pallas_call(
        norm_kernel,
        out_shape=(
            shape((seg, width), jnp.bfloat16),
            shape((seg, width), F32),
            shape((seg, 1), F32),
            shape((seg, width), F32),
            shape((2 * mine.shape[0], mine.shape[1]), mine.dtype),
        ),
        in_specs=[VMEM] * 8,
        out_specs=(VMEM,) * 5,
        compiler_params=room(8),
    )(from_core, from_chip, mid_token, mid_grad, count, gain, mine, theirs)


def dout_kernel(dout_ref, second_ref, full_ref, half_ref):
    seg = dout_ref.shape[0]
    last = lax.broadcasted_iota(jnp.int32, (seg, 1), 0) == seg - 1
    dout = dout_ref[...] + jnp.where(last, second_ref[...], 0.0)
    full_ref[...] = dout
    half_ref[...] = dout.astype(jnp.bfloat16)


def whole_dout(dout, second):
    shape = jax.ShapeDtypeStruct
    return pl.pallas_call(
        dout_kernel,
        out_shape=(shape(dout.shape, F32), shape(dout.shape, jnp.bfloat16)),
        in_specs=[VMEM, VMEM],
        out_specs=(VMEM, VMEM),
        compiler_params=room(4),
    )(dout, second)


def project_kernel(*refs):
    pieces, weights, douts, halves = refs[:8], refs[8:12], refs[12:14], refs[14]
    q_ref, kv_ref, w_ref, outs = *refs[15:18], refs[18:22]
    rows, chip_rows, w_back, sems = refs[22:]
    heads, half = halves.shape[:2]
    started = []
    for i in range(heads):
        target = w_back.at[i * half : (i + 1) * half, :]
        started.append(pltpu.make_async_copy(halves.at[i], target, sems.at[i]))
        started[-1].start()
    fill(rows, pieces)
    fill(chip_rows, douts)
    dp = lax.axis_index("dp")
    x, y = dp // ROWS_Y, dp % ROWS_Y
    depth = weights[0].shape[0] // ROWS_X
    for weight, step in zip(weights, (0, 1, -1, 2)):
        its_y = (y - step + ROWS_Y) % ROWS_Y
        for i in range(ROWS_X):
            its_x = x if i == 0 else 1 - x
            at = pl.multiple_of((its_x * ROWS_Y + its_y) * depth, depth)
            w_ref[pl.ds(at, depth), :] = weight[i * depth : (i + 1) * depth, :]
    out = jnp.dot(rows[...], w_ref[...], preferred_element_type=F32).astype(jnp.bfloat16)
    q_ref[...] = out[:, :HEAD]
    kv_ref[...] = out[:, HEAD:]
    for copy in started:
        copy.wait()
    turn = here()[1]
    for step, ref in enumerate(outs):
        at = pl.multiple_of((turn + step) % TURNS * CORES * half, CORES * half)
        part = w_back[pl.ds(at, CORES * half), :]
        ref[...] = contract_last(chip_rows[...], part).astype(jnp.bfloat16)


def project(pieces, weights, douts, halves):
    seg, width = pieces[0].shape
    rows = seg * len(pieces)
    heads, half = halves.shape[:2]
    bf16 = lambda *shape: jax.ShapeDtypeStruct(shape, jnp.bfloat16)
    return pl.pallas_call(
        project_kernel,
        out_shape=(bf16(rows, HEAD), bf16(rows, 2 * HEAD), bf16(width, 3 * HEAD))
        + (bf16(2 * seg, CORES * half),) * TURNS,
        in_specs=[VMEM] * 14 + [ANY],
        out_specs=(VMEM,) * (3 + TURNS),
        scratch_shapes=[
            pltpu.VMEM((rows, width), jnp.bfloat16),
            pltpu.VMEM((2 * seg, width), jnp.bfloat16),
            pltpu.VMEM((heads * half, width), jnp.bfloat16),
            pltpu.SemaphoreType.DMA((heads,)),
        ],
        compiler_params=room(50),
    )(*pieces, *weights, *douts, halves)


def place_dattended(core, seg, here_refs, there_refs, out_ref):
    half = out_ref.shape[1] // CORES
    mine = slice(core * half, (core + 1) * half)
    other = slice((1 - core) * half, (2 - core) * half)
    slots = ((0, 1), (2, 3), (6, 7), (5, 4)) if core == 0 else ((0, 1), (5, 4), (6, 7), (2, 3))
    for refs in zip(here_refs, there_refs, slots):
        for i, slot in enumerate(refs[2]):
            rows = slice(slot * seg, (slot + 1) * seg)
            out_ref[rows, mine] = refs[0][i * seg : (i + 1) * seg, mine]
            out_ref[rows, other] = refs[1][(1 - i) * seg : (2 - i) * seg, mine]


def attention_kernel(tile, seg, *refs):
    q_ref, here_refs, there_refs, blocks = refs[0], refs[1:5], refs[5:9], refs[9:13]
    dq_ref, outs, (kv, da_ref, dkt, dvt) = refs[13], refs[14:18], refs[18:]
    half, turn, pair, core = here()
    queries = q_ref.shape[0]
    for which in range(CORES):

        @pl.when(core == which)
        def _(which=which):
            place_dattended(which, seg, here_refs, there_refs, da_ref)

    turn_up = math.log2(math.e) / math.sqrt(HEAD)
    scale = 1.0 / math.sqrt(HEAD)

    def run(used):
        keys = used * queries
        fill(kv, blocks[:used])
        near = 2 * queries
        spot = lax.broadcasted_iota(jnp.int32, (1, near), 1)
        key_pair = jnp.where(spot < queries, pair, 1 - pair)
        key_at = rows_at(spot % queries, half, turn, key_pair, core, seg)
        k = kv[:keys, :HEAD]
        v = kv[:keys, HEAD:]
        for step in range(queries // tile):
            rows = slice(step * tile, (step + 1) * tile)
            query = lax.broadcasted_iota(jnp.int32, (tile, 1), 0) + step * tile
            query_at = rows_at(query, half, turn, pair, core, seg)
            q = q_ref[rows, :]
            da = da_ref[rows, :]
            score = contract_last(q, k)
            masked = jnp.where(key_at <= query_at, score[:, :near], NEG)
            score = masked if used == 2 else jnp.concatenate([masked, score[:, near:]], axis=1)
            peak = jnp.max(score, axis=1, keepdims=True)
            expo = jnp.exp2((score - peak) * turn_up)
            probs = expo * (1.0 / jnp.sum(expo, axis=1, keepdims=True))
            probs_b = probs.astype(jnp.bfloat16)
            attended = jnp.dot(probs_b, v, preferred_element_type=F32).astype(jnp.bfloat16)
            delta = jnp.sum(da.astype(F32) * attended.astype(F32), axis=1, keepdims=True)
            dscore = (probs * (contract_last(da, v) - delta)).astype(jnp.bfloat16)
            dq = jnp.dot(dscore, k, preferred_element_type=F32) * scale
            dq_ref[rows, :] = dq.astype(jnp.bfloat16)
            dk_part = contract_first(q, dscore)
            dv_part = contract_first(da, probs_b)
            if step == 0:
                dkt[:, :keys] = dk_part
                dvt[:, :keys] = dv_part
            else:
                dkt[:, :keys] += dk_part
                dvt[:, :keys] += dv_part
        for i, out in enumerate(outs[:used]):
            lanes = slice(i * queries, (i + 1) * queries)
            out[:, :HEAD] = (dkt[:, lanes] * scale).T.astype(jnp.bfloat16)
            out[:, HEAD:] = dvt[:, lanes].T.astype(jnp.bfloat16)

    @pl.when(half == 0)
    def _():
        run(2)
        for out in outs[2:]:
            out[...] = jnp.zeros_like(out)

    @pl.when(half == 1)
    def _():
        run(4)


def attention(q, da_here, da_there, blocks, seg):
    queries = q.shape[0]
    keys = sum(block.shape[0] for block in blocks)
    parts = tuple(jax.ShapeDtypeStruct(block.shape, jnp.bfloat16) for block in blocks)
    return pl.pallas_call(
        functools.partial(attention_kernel, 256, seg),
        out_shape=(jax.ShapeDtypeStruct((queries, HEAD), jnp.bfloat16),) + parts,
        in_specs=[VMEM] * 13,
        out_specs=(VMEM,) * 5,
        scratch_shapes=[
            pltpu.VMEM((keys, 2 * HEAD), jnp.bfloat16),
            pltpu.VMEM((queries, HEAD), jnp.bfloat16),
            pltpu.VMEM((HEAD, keys), F32),
            pltpu.VMEM((HEAD, keys), F32),
        ],
        compiler_params=room(36),
        cost_estimate=pl.CostEstimate(
            flops=12 * queries * keys * HEAD,
            bytes_accessed=2 * HEAD * (3 * queries + 4 * keys),
            transcendentals=queries * keys,
        ),
    )(q, *da_here, *da_there, *blocks)


def unproject_kernel(seg, dq_ref, *refs):
    parts, w_ref, swap_ref, outs = refs[:4], refs[4], refs[5], refs[6:]
    dkv = sum(ref[...].astype(F32) for ref in parts).astype(jnp.bfloat16)
    left = jnp.concatenate([dq_ref[...], dkv], axis=1)
    out = contract_last(left, w_ref[...])
    for i, slot in enumerate((1, 4, 5, 7)):
        swap_ref[i * seg : (i + 1) * seg, :] = out[slot * seg : (slot + 1) * seg].astype(WIRE)
    for ref, slot in zip(outs, (0, 2, 3, 6)):
        ref[...] = out[slot * seg : (slot + 1) * seg]


def unproject(dq, parts, w_full, seg):
    width = w_full.shape[0]
    return pl.pallas_call(
        functools.partial(unproject_kernel, seg),
        out_shape=(jax.ShapeDtypeStruct((4 * seg, width), WIRE),)
        + (jax.ShapeDtypeStruct((seg, width), F32),) * 4,
        in_specs=[VMEM] * 6,
        out_specs=(VMEM,) * 5,
        compiler_params=room(16),
    )(dq, *parts, w_full)


def join_kernel(swapped, own, near, next_to, far, own_out, near_out, next_out, far_out):
    seg = own.shape[0]
    own_out[...] = own[...] + swapped[:seg, :].astype(F32)
    near_out[...] = near[...] + swapped[seg : 2 * seg, :].astype(F32)
    next_out[...] = (next_to[...] + swapped[2 * seg : 3 * seg, :].astype(F32)).astype(WIRE)
    far_out[...] = (far[...] + swapped[3 * seg :, :].astype(F32)).astype(WIRE)


def joined(swapped, own, near, next_to, far):
    wide = jax.ShapeDtypeStruct(own.shape, F32)
    thin = jax.ShapeDtypeStruct(own.shape, WIRE)
    return pl.pallas_call(
        join_kernel,
        out_shape=(wide, wide, thin, thin),
        in_specs=[VMEM] * 5,
        out_specs=(VMEM,) * 4,
        compiler_params=room(6),
    )(swapped, own, near, next_to, far)


def summed_rows(swap, own, near, next_to, far):
    own, near, next_to, far = joined(other_core(swap), own, near, next_to, far)
    far = turned(far, -1).astype(F32)
    next_to = turned_over(next_to).astype(F32)
    near = turned((near + far).astype(WIRE), -1).astype(F32)
    return own + next_to + near


def per_device(tokens, starts, gain, w_query, w_key, w_value, w_out, cotangent):
    token_rows = tokens[0]
    grad_out = cotangent[0]
    rows, width = token_rows.shape
    seg = starts.shape[1]
    length = rows * CTX
    ctx, core = lax.axis_index("ctx"), here()[3]

    half, own_starts = cut_rows(w_out, starts)
    mine = cut_columns(w_query, w_key, w_value, own_starts)
    halves = gathered_halves(half)
    theirs = other_x(mine)
    beside, facing = other_core(own_starts), other_chip(own_starts)
    own_starts = starts
    to_core, to_chip, mid_token, mid_grad, first = window_sums(
        own_starts, beside, facing, token_rows, grad_out
    )
    before = jnp.where(core == 0, facing, beside)[0]
    after = jnp.where(core == 0, beside, facing)[0]
    before = jnp.where(ctx == 0, -1, before)
    after = jnp.where(ctx == CTX - 1, length, after)
    stop = jnp.full((1,), length, jnp.int32)
    window = jnp.concatenate([before, own_starts[0], after, stop])
    opens, ends = window[:-1], window[1:]
    count = (ends - opens)[seg : 2 * seg, None].astype(F32)
    second = two_back(first)
    normin, normed, rms, dout, both = norm(
        other_core(to_core),
        other_chip(to_chip),
        mid_token,
        mid_grad,
        count,
        gain[None],
        mine,
        theirs,
    )
    weights = [both, shifted_y(both, 1), shifted_y(both, -1), shifted_y(both, 2)]
    dout, dout_b = whole_dout(dout, second)
    dout_there = other_core(dout_b)
    pieces = gathered_rows(normin, [dout_there], weights[1:])
    q, own, w_full, *da = project(pieces, weights, (dout_b, dout_there), halves)
    far, beside = across(own, 0, False), other_pair(own)
    da_here = [da[0]] + [
        moved(da[i], lambda h, t, p, k, i=i: (h, t + i, p, k)) for i in range(1, TURNS)
    ]
    cross = across(passed_on(own, *da_here[1:]), 0, True)
    da_there = [other_core(piece) for piece in da_here]
    blocks = (own, beside, far, cross)
    dq, own, beside, far, cross = attention(q, da_here, da_there, blocks, seg)
    parts = (own, other_pair(beside), across(far, 1, False), across(cross, 1, True))
    dnormin = summed_rows(*unproject(dq, parts, w_full, seg))

    scaled = dnormin * gain
    dpooled = dout + (scaled - normed * jnp.mean(scaled * normed, axis=-1, keepdims=True)) / rms
    per_seg = (dpooled / count).astype(WIRE)
    beside, facing = other_core(per_seg), other_chip(per_seg)
    before = jnp.where(core == 0, facing, beside)
    after = jnp.where(core == 0, beside, facing)
    per_window = jnp.concatenate([before, per_seg, after], axis=0)
    positions = (ctx * rows + lax.iota(jnp.int32, rows))[:, None]
    member = (opens[None] <= positions) & (positions < ends[None])
    spread = jnp.dot(member.astype(WIRE), per_window, preferred_element_type=F32)
    return (grad_out.astype(F32) + spread).astype(jnp.bfloat16)[None]


def solution(mesh):
    return jax.shard_map(
        per_device,
        mesh=mesh,
        in_specs=(
            P("dp", "ctx", None),
            P("dp", "ctx"),
            P(),
            P("dp", None),
            P("dp", None),
            P("dp", None),
            P("dp", None),
            P("dp", "ctx", None),
        ),
        out_specs=P("dp", "ctx", None),
        check_vma=False,
    )
```

```python
import functools
import math

import jax
import jax.numpy as jnp
from jax import lax
from jax.experimental import pallas as pl
from jax.experimental.pallas import tpu as pltpu
from jax.sharding import PartitionSpec as P

HEAD = 128
HALVES, TURNS, PAIR, CORES = 2, 4, 2, 2
CTX = HALVES * TURNS * PAIR * CORES
ROWS_X, ROWS_Y = 2, 4
NEG = -1e30
WIRE = jnp.bfloat16
F32 = jnp.float32
VMEM = pl.BlockSpec(memory_space=pltpu.VMEM)
ANY = pl.BlockSpec(memory_space=pl.ANY)
HBM = pl.BlockSpec(memory_space=pltpu.HBM)


def room(mib):
    return pltpu.CompilerParams(vmem_limit_bytes=mib * 1024 * 1024)


def place(half, turn, pair, core):
    return ((half * TURNS + turn % TURNS) * PAIR + pair) * CORES + core


def here():
    ctx = lax.axis_index("ctx")
    core, pair = ctx % CORES, ctx // CORES % PAIR
    return ctx // (CORES * PAIR * TURNS), ctx // (CORES * PAIR) % TURNS, pair, core


def moved(value, to):
    spots = [
        (h, t, p, k)
        for h in range(HALVES)
        for t in range(TURNS)
        for p in range(PAIR)
        for k in range(CORES)
    ]
    pairs = [(place(*s), place(*to(*s))) for s in spots if to(*s) is not None]
    return lax.ppermute(value, "ctx", pairs)


def other_chip(value):
    pairs = [(i, i + 1 if i % CORES else i - 1) for i in range(1, CTX - 1)]
    return lax.ppermute(value, "ctx", pairs)


def two_back(value):
    return lax.ppermute(value, "ctx", [(i, i - CORES) for i in range(CORES, CTX)])


def other_core(value):
    return moved(value, lambda h, t, p, k: (h, t, p, 1 - k))


def other_pair(value):
    return moved(value, lambda h, t, p, k: (h, t, 1 - p, k))


def across(value, source, cross):
    return moved(
        value,
        lambda h, t, p, k: (1 - h, t, 1 - p if cross else p, k) if h == source else None,
    )


def turned(value, way):
    return moved(value, lambda h, t, p, k: (h, t + way * (1 - 2 * k), p, k))


def turned_over(value):
    return moved(value, lambda h, t, p, k: (h, t - (1 - 2 * k), p, 1 - k))


def contract_last(left, right):
    return lax.dot_general(left, right, (((1,), (1,)), ((), ())), preferred_element_type=F32)


def contract_first(left, right):
    return lax.dot_general(left, right, (((0,), (0,)), ((), ())), preferred_element_type=F32)


def cut_kernel(q_ref, k_ref, v_ref, o_ref, start_ref, out_ref, half_ref, start_out, sems):
    _, turn, _, core = here()
    lane = pl.multiple_of((turn * CORES + core) * HEAD, HEAD)
    copies = [
        (w.at[:, pl.ds(lane, HEAD)], out_ref.at[:, i * HEAD : (i + 1) * HEAD])
        for i, w in enumerate((q_ref, k_ref, v_ref))
    ]
    half = half_ref.shape[0]
    copies.append((o_ref.at[pl.ds(pl.multiple_of(core * half, half), half), :], half_ref))
    copies.append((start_ref, start_out))
    fetched(copies, sems)


def cut_weights(w_query, w_key, w_value, w_out, starts):
    rows, width = w_out.shape
    return pl.pallas_call(
        cut_kernel,
        out_shape=(
            jax.ShapeDtypeStruct((rows, 3 * HEAD), w_query.dtype),
            jax.ShapeDtypeStruct((rows // CORES, width), w_out.dtype),
            jax.ShapeDtypeStruct(starts.shape, starts.dtype),
        ),
        in_specs=[HBM] * 4 + [ANY],
        out_specs=(VMEM, VMEM, VMEM),
        scratch_shapes=[pltpu.SemaphoreType.DMA((5,))],
        compiler_params=room(60),
    )(w_query, w_key, w_value, w_out, starts)


def other_x(value):
    count = ROWS_X * ROWS_Y
    return lax.ppermute(value, "dp", [(d, (d + ROWS_Y) % count) for d in range(count)])


def shifted_y(value, step):
    pairs = [(d, d // ROWS_Y * ROWS_Y + (d + step) % ROWS_Y) for d in range(ROWS_X * ROWS_Y)]
    return lax.ppermute(value, "dp", pairs)


def gathered_halves(half):
    return lax.all_gather(half, "dp", axis=0, tiled=False)


def pass_kernel(value_ref, *refs):
    refs[-1][...] = value_ref[...]


def passed_on(value, *ready):
    return pl.pallas_call(
        pass_kernel,
        out_shape=jax.ShapeDtypeStruct(value.shape, value.dtype),
        in_specs=[VMEM] + [ANY] * len(ready),
        out_specs=VMEM,
        compiler_params=room(4),
    )(value, *ready)


def gathered_rows(shard, first_ready, last_ready):
    near = turned(shard, 1)
    next_to = turned_over(passed_on(shard, near))
    far = passed_on(turned(passed_on(near, *first_ready), 1), *last_ready)
    return [
        shard,
        other_core(shard),
        near,
        next_to,
        other_core(near),
        other_core(next_to),
        far,
        other_core(far),
    ]


def rows_at(row, half, turn, pair, core, seg):
    slot = row // seg
    two = slot // 2
    way = 1 - 2 * core
    step = jnp.where(two == 0, 0, jnp.where(two == 1, way, jnp.where(two == 2, -way, 2)))
    flip = jnp.where(two == 2, 1 - slot % 2, slot % 2)
    its_core = jnp.where(flip == 1, 1 - core, core)
    its_turn = (turn - step + TURNS) % TURNS
    return place(half, its_turn, pair, its_core) * seg + row % seg


def fetched(copies, sems):
    started = []
    for i, (source, target) in enumerate(copies):
        started.append(pltpu.make_async_copy(source, target, sems.at[i]))
        started[-1].start()
    for copy in started:
        copy.wait()


def fill(out_ref, pieces):
    at = 0
    for piece in pieces:
        out_ref[at : at + piece.shape[0], :] = piece[...]
        at += piece.shape[0]


def window_kernel(own_ref, beside_ref, facing_ref, token_hbm, grad_hbm, *refs):
    core_ref, chip_ref, mid_token, mid_grad, first_ref = refs[:5]
    token_ref, grad_ref, sems = refs[5:]
    rows, width = token_ref.shape
    seg = mid_token.shape[0]
    token_copy = pltpu.make_async_copy(token_hbm, token_ref, sems.at[0])
    grad_copy = pltpu.make_async_copy(grad_hbm, grad_ref, sems.at[1])
    token_copy.start()
    grad_copy.start()
    ctx, core = lax.axis_index("ctx"), here()[3]
    at = lax.broadcasted_iota(jnp.int32, (rows, 1), 0) + ctx * rows
    before = jnp.where(core == 0, facing_ref[...], beside_ref[...])
    after = jnp.where(core == 0, beside_ref[...], facing_ref[...])
    before = jnp.where(ctx == 0, -1, before)
    after = jnp.where(ctx == CTX - 1, rows * CTX, after)
    begun = [(part <= at).astype(jnp.int32) for part in (before, own_ref[...], after)]
    slot = sum(jnp.sum(part, axis=1, keepdims=True) for part in begun) - 1
    slots = lax.broadcasted_iota(jnp.int32, (1, 3 * seg), 1)
    member = (slots == slot).astype(jnp.bfloat16)
    earlier = (slots == slot - 1).astype(jnp.bfloat16)
    token_copy.wait()
    token = contract_first(member, token_ref[...])
    grad_copy.wait()
    grad = contract_first(earlier, grad_ref[...])
    outside = jnp.broadcast_to((slot == 0).astype(jnp.bfloat16), (rows, HEAD))
    first_ref[...] = contract_first(outside, grad_ref[...])[:1]
    mid_token[...] = token[seg : 2 * seg]
    mid_grad[...] = grad[seg : 2 * seg]

    def send(lower_ref, upper_ref):
        lower_ref[:, :width] = token[:seg].astype(WIRE)
        lower_ref[:, width:] = grad[:seg].astype(WIRE)
        upper_ref[:, :width] = token[2 * seg :].astype(WIRE)
        upper_ref[:, width:] = grad[2 * seg :].astype(WIRE)

    @pl.when(core == 0)
    def _():
        send(chip_ref, core_ref)

    @pl.when(core == 1)
    def _():
        send(core_ref, chip_ref)


def window_sums(own, beside, facing, tokens, grads):
    rows, width = tokens.shape
    seg = own.shape[1]
    shape = jax.ShapeDtypeStruct
    return pl.pallas_call(
        window_kernel,
        out_shape=(
            shape((seg, 2 * width), WIRE),
            shape((seg, 2 * width), WIRE),
            shape((seg, width), F32),
            shape((seg, width), F32),
            shape((1, width), F32),
        ),
        in_specs=[VMEM] * 3 + [HBM] * 2,
        out_specs=(VMEM,) * 5,
        scratch_shapes=[
            pltpu.VMEM((rows, width), tokens.dtype),
            pltpu.VMEM((rows, width), grads.dtype),
            pltpu.SemaphoreType.DMA((2,)),
        ],
        compiler_params=room(16),
    )(own, beside, facing, tokens, grads)


def norm_kernel(core_ref, chip_ref, mid_token, mid_grad, count_ref, gain_ref, *refs):
    mine_ref, theirs_ref, normin_ref, normed_ref, rms_ref, dout_ref, pair_ref = refs
    width = mid_token.shape[1]
    rows = mine_ref.shape[0]
    pair_ref[:rows, :] = mine_ref[...]
    pair_ref[rows:, :] = theirs_ref[...]
    got = core_ref[...].astype(F32) + chip_ref[...].astype(F32)
    pooled = (mid_token[...] + got[:, :width]) / count_ref[...]
    rms = jnp.sqrt(jnp.mean(pooled * pooled, axis=1, keepdims=True) + 1e-06)
    normed = pooled / rms
    normed_ref[...] = normed
    rms_ref[...] = rms
    normin_ref[...] = (normed * gain_ref[...]).astype(jnp.bfloat16)
    dout_ref[...] = mid_grad[...] + got[:, width:]


def norm(from_core, from_chip, mid_token, mid_grad, count, gain, mine, theirs):
    seg, width = mid_token.shape
    shape = jax.ShapeDtypeStruct
    return pl.pallas_call(
        norm_kernel,
        out_shape=(
            shape((seg, width), jnp.bfloat16),
            shape((seg, width), F32),
            shape((seg, 1), F32),
            shape((seg, width), F32),
            shape((2 * mine.shape[0], mine.shape[1]), mine.dtype),
        ),
        in_specs=[VMEM] * 8,
        out_specs=(VMEM,) * 5,
        compiler_params=room(8),
    )(from_core, from_chip, mid_token, mid_grad, count, gain, mine, theirs)


def dout_kernel(dout_ref, second_ref, full_ref, half_ref):
    seg = dout_ref.shape[0]
    last = lax.broadcasted_iota(jnp.int32, (seg, 1), 0) == seg - 1
    dout = dout_ref[...] + jnp.where(last, second_ref[...], 0.0)
    full_ref[...] = dout
    half_ref[...] = dout.astype(jnp.bfloat16)


def whole_dout(dout, second):
    shape = jax.ShapeDtypeStruct
    return pl.pallas_call(
        dout_kernel,
        out_shape=(shape(dout.shape, F32), shape(dout.shape, jnp.bfloat16)),
        in_specs=[VMEM, VMEM],
        out_specs=(VMEM, VMEM),
        compiler_params=room(4),
    )(dout, second)


def dattended_kernel(own_ref, other_ref, weight, ready_ref, *refs):
    outs, rows = refs[:TURNS], refs[TURNS]
    fill(rows, [own_ref, other_ref])
    two = outs[0].shape[1]
    turn = here()[1]
    for step, ref in enumerate(outs):
        at = pl.multiple_of((turn + step) % TURNS * two, two)
        ref[...] = contract_last(rows[...], weight[pl.ds(at, two), :]).astype(jnp.bfloat16)


def dattended(own, other, halves, ready):
    heads, half, width = halves.shape
    rows = 2 * own.shape[0]
    return pl.pallas_call(
        dattended_kernel,
        out_shape=(jax.ShapeDtypeStruct((rows, CORES * half), jnp.bfloat16),) * TURNS,
        in_specs=[VMEM] * 3 + [ANY],
        out_specs=(VMEM,) * TURNS,
        scratch_shapes=[pltpu.VMEM((rows, width), jnp.bfloat16)],
        compiler_params=room(8),
    )(own, other, halves.reshape(heads * half, width), ready)


def project_kernel(*refs):
    pieces, weights = refs[:8], refs[8:12]
    q_ref, kv_ref, w_ref, rows = refs[12:]
    fill(rows, pieces)
    dp = lax.axis_index("dp")
    x, y = dp // ROWS_Y, dp % ROWS_Y
    depth = weights[0].shape[0] // ROWS_X
    for weight, step in zip(weights, (0, 1, -1, 2)):
        its_y = (y - step + ROWS_Y) % ROWS_Y
        for i in range(ROWS_X):
            its_x = x if i == 0 else 1 - x
            at = pl.multiple_of((its_x * ROWS_Y + its_y) * depth, depth)
            w_ref[pl.ds(at, depth), :] = weight[i * depth : (i + 1) * depth, :]
    out = jnp.dot(rows[...], w_ref[...], preferred_element_type=F32).astype(jnp.bfloat16)
    q_ref[...] = out[:, :HEAD]
    kv_ref[...] = out[:, HEAD:]


def project(pieces, weights):
    seg, width = pieces[0].shape
    rows = seg * len(pieces)
    bf16 = lambda *shape: jax.ShapeDtypeStruct(shape, jnp.bfloat16)
    return pl.pallas_call(
        project_kernel,
        out_shape=(bf16(rows, HEAD), bf16(rows, 2 * HEAD), bf16(width, 3 * HEAD)),
        in_specs=[VMEM] * 12,
        out_specs=(VMEM,) * 3,
        scratch_shapes=[pltpu.VMEM((rows, width), jnp.bfloat16)],
        compiler_params=room(12),
    )(*pieces, *weights)


def place_dattended(core, seg, here_refs, there_refs, out_ref):
    half = out_ref.shape[1] // CORES
    mine = slice(core * half, (core + 1) * half)
    other = slice((1 - core) * half, (2 - core) * half)
    slots = ((0, 1), (2, 3), (6, 7), (5, 4)) if core == 0 else ((0, 1), (5, 4), (6, 7), (2, 3))
    for refs in zip(here_refs, there_refs, slots):
        for i, slot in enumerate(refs[2]):
            rows = slice(slot * seg, (slot + 1) * seg)
            out_ref[rows, mine] = refs[0][i * seg : (i + 1) * seg, mine]
            out_ref[rows, other] = refs[1][(1 - i) * seg : (2 - i) * seg, mine]


def attention_kernel(tile, seg, *refs):
    q_ref, here_refs, there_refs, blocks = refs[0], refs[1:5], refs[5:9], refs[9:13]
    dq_ref, outs, (kv, da_ref, dkt, dvt) = refs[13], refs[14:18], refs[18:]
    half, turn, pair, core = here()
    queries = q_ref.shape[0]
    for which in range(CORES):

        @pl.when(core == which)
        def _(which=which):
            place_dattended(which, seg, here_refs, there_refs, da_ref)

    turn_up = math.log2(math.e) / math.sqrt(HEAD)
    scale = 1.0 / math.sqrt(HEAD)

    def run(used):
        keys = used * queries
        fill(kv, blocks[:used])
        near = 2 * queries
        spot = lax.broadcasted_iota(jnp.int32, (1, near), 1)
        key_pair = jnp.where(spot < queries, pair, 1 - pair)
        key_at = rows_at(spot % queries, half, turn, key_pair, core, seg)
        k = kv[:keys, :HEAD]
        v = kv[:keys, HEAD:]
        for step in range(queries // tile):
            rows = slice(step * tile, (step + 1) * tile)
            query = lax.broadcasted_iota(jnp.int32, (tile, 1), 0) + step * tile
            query_at = rows_at(query, half, turn, pair, core, seg)
            q = q_ref[rows, :]
            da = da_ref[rows, :]
            score = contract_last(q, k)
            masked = jnp.where(key_at <= query_at, score[:, :near], NEG)
            score = masked if used == 2 else jnp.concatenate([masked, score[:, near:]], axis=1)
            peak = jnp.max(score, axis=1, keepdims=True)
            expo = jnp.exp2((score - peak) * turn_up)
            probs = expo * (1.0 / jnp.sum(expo, axis=1, keepdims=True))
            probs_b = probs.astype(jnp.bfloat16)
            attended = jnp.dot(probs_b, v, preferred_element_type=F32).astype(jnp.bfloat16)
            delta = jnp.sum(da.astype(F32) * attended.astype(F32), axis=1, keepdims=True)
            dscore = (probs * (contract_last(da, v) - delta)).astype(jnp.bfloat16)
            dq = jnp.dot(dscore, k, preferred_element_type=F32) * scale
            dq_ref[rows, :] = dq.astype(jnp.bfloat16)
            dk_part = contract_first(q, dscore)
            dv_part = contract_first(da, probs_b)
            if step == 0:
                dkt[:, :keys] = dk_part
                dvt[:, :keys] = dv_part
            else:
                dkt[:, :keys] += dk_part
                dvt[:, :keys] += dv_part
        for i, out in enumerate(outs[:used]):
            lanes = slice(i * queries, (i + 1) * queries)
            out[:, :HEAD] = (dkt[:, lanes] * scale).T.astype(jnp.bfloat16)
            out[:, HEAD:] = dvt[:, lanes].T.astype(jnp.bfloat16)

    @pl.when(half == 0)
    def _():
        run(2)
        for out in outs[2:]:
            out[...] = jnp.zeros_like(out)

    @pl.when(half == 1)
    def _():
        run(4)


def attention(q, da_here, da_there, blocks, seg):
    queries = q.shape[0]
    keys = sum(block.shape[0] for block in blocks)
    parts = tuple(jax.ShapeDtypeStruct(block.shape, jnp.bfloat16) for block in blocks)
    return pl.pallas_call(
        functools.partial(attention_kernel, 256, seg),
        out_shape=(jax.ShapeDtypeStruct((queries, HEAD), jnp.bfloat16),) + parts,
        in_specs=[VMEM] * 13,
        out_specs=(VMEM,) * 5,
        scratch_shapes=[
            pltpu.VMEM((keys, 2 * HEAD), jnp.bfloat16),
            pltpu.VMEM((queries, HEAD), jnp.bfloat16),
            pltpu.VMEM((HEAD, keys), F32),
            pltpu.VMEM((HEAD, keys), F32),
        ],
        compiler_params=room(36),
        cost_estimate=pl.CostEstimate(
            flops=12 * queries * keys * HEAD,
            bytes_accessed=2 * HEAD * (3 * queries + 4 * keys),
            transcendentals=queries * keys,
        ),
    )(q, *da_here, *da_there, *blocks)


def unproject_kernel(seg, dq_ref, *refs):
    parts, w_ref, swap_ref, outs = refs[:4], refs[4], refs[5], refs[6:]
    dkv = sum(ref[...].astype(F32) for ref in parts).astype(jnp.bfloat16)
    left = jnp.concatenate([dq_ref[...], dkv], axis=1)
    out = contract_last(left, w_ref[...])
    for i, slot in enumerate((1, 4, 5, 7)):
        swap_ref[i * seg : (i + 1) * seg, :] = out[slot * seg : (slot + 1) * seg].astype(WIRE)
    for ref, slot in zip(outs, (0, 2, 3, 6)):
        ref[...] = out[slot * seg : (slot + 1) * seg]


def unproject(dq, parts, w_full, seg):
    width = w_full.shape[0]
    return pl.pallas_call(
        functools.partial(unproject_kernel, seg),
        out_shape=(jax.ShapeDtypeStruct((4 * seg, width), WIRE),)
        + (jax.ShapeDtypeStruct((seg, width), F32),) * 4,
        in_specs=[VMEM] * 6,
        out_specs=(VMEM,) * 5,
        compiler_params=room(16),
    )(dq, *parts, w_full)


def join_kernel(swapped, own, near, next_to, far, own_out, near_out, next_out, far_out):
    seg = own.shape[0]
    own_out[...] = own[...] + swapped[:seg, :].astype(F32)
    near_out[...] = near[...] + swapped[seg : 2 * seg, :].astype(F32)
    next_out[...] = (next_to[...] + swapped[2 * seg : 3 * seg, :].astype(F32)).astype(WIRE)
    far_out[...] = (far[...] + swapped[3 * seg :, :].astype(F32)).astype(WIRE)


def joined(swapped, own, near, next_to, far):
    wide = jax.ShapeDtypeStruct(own.shape, F32)
    thin = jax.ShapeDtypeStruct(own.shape, WIRE)
    return pl.pallas_call(
        join_kernel,
        out_shape=(wide, wide, thin, thin),
        in_specs=[VMEM] * 5,
        out_specs=(VMEM,) * 4,
        compiler_params=room(6),
    )(swapped, own, near, next_to, far)


def summed_rows(swap, own, near, next_to, far):
    own, near, next_to, far = joined(other_core(swap), own, near, next_to, far)
    far = turned(far, -1).astype(F32)
    next_to = turned_over(next_to).astype(F32)
    near = turned((near + far).astype(WIRE), -1).astype(F32)
    return own + next_to + near


def per_device(tokens, starts, gain, w_query, w_key, w_value, w_out, cotangent):
    token_rows = tokens[0]
    grad_out = cotangent[0]
    rows, width = token_rows.shape
    seg = starts.shape[1]
    length = rows * CTX
    ctx, core = lax.axis_index("ctx"), here()[3]

    mine, half, own_starts = cut_weights(w_query, w_key, w_value, w_out, starts)
    halves = gathered_halves(half)
    theirs = other_x(mine)
    beside, facing = other_core(own_starts), other_chip(own_starts)
    own_starts = starts
    to_core, to_chip, mid_token, mid_grad, first = window_sums(
        own_starts, beside, facing, token_rows, grad_out
    )
    before = jnp.where(core == 0, facing, beside)[0]
    after = jnp.where(core == 0, beside, facing)[0]
    before = jnp.where(ctx == 0, -1, before)
    after = jnp.where(ctx == CTX - 1, length, after)
    stop = jnp.full((1,), length, jnp.int32)
    window = jnp.concatenate([before, own_starts[0], after, stop])
    opens, ends = window[:-1], window[1:]
    count = (ends - opens)[seg : 2 * seg, None].astype(F32)
    second = two_back(first)
    normin, normed, rms, dout, both = norm(
        other_core(to_core),
        other_chip(to_chip),
        mid_token,
        mid_grad,
        count,
        gain[None],
        mine,
        theirs,
    )
    weights = [both, shifted_y(both, 1), shifted_y(both, -1), shifted_y(both, 2)]
    dout, dout_b = whole_dout(dout, second)
    dout_there = other_core(dout_b)
    pieces = gathered_rows(normin, [dout_there], weights[1:])
    q, own, w_full = project(pieces, weights)
    da = dattended(dout_b, dout_there, halves, w_full)
    far, beside = across(own, 0, False), other_pair(own)
    da_here = [da[0]] + [
        moved(da[i], lambda h, t, p, k, i=i: (h, t + i, p, k)) for i in range(1, TURNS)
    ]
    cross = across(passed_on(own, *da_here[1:]), 0, True)
    da_there = [other_core(piece) for piece in da_here]
    blocks = (own, beside, far, cross)
    dq, own, beside, far, cross = attention(q, da_here, da_there, blocks, seg)
    parts = (own, other_pair(beside), across(far, 1, False), across(cross, 1, True))
    dnormin = summed_rows(*unproject(dq, parts, w_full, seg))

    scaled = dnormin * gain
    dpooled = dout + (scaled - normed * jnp.mean(scaled * normed, axis=-1, keepdims=True)) / rms
    per_seg = (dpooled / count).astype(WIRE)
    beside, facing = other_core(per_seg), other_chip(per_seg)
    before = jnp.where(core == 0, facing, beside)
    after = jnp.where(core == 0, beside, facing)
    per_window = jnp.concatenate([before, per_seg, after], axis=0)
    positions = (ctx * rows + lax.iota(jnp.int32, rows))[:, None]
    member = (opens[None] <= positions) & (positions < ends[None])
    spread = jnp.dot(member.astype(WIRE), per_window, preferred_element_type=F32)
    return (grad_out.astype(F32) + spread).astype(jnp.bfloat16)[None]


def solution(mesh):
    return jax.shard_map(
        per_device,
        mesh=mesh,
        in_specs=(
            P("dp", "ctx", None),
            P("dp", "ctx"),
            P(),
            P("dp", None),
            P("dp", None),
            P("dp", None),
            P("dp", None),
            P("dp", "ctx", None),
        ),
        out_specs=P("dp", "ctx", None),
        check_vma=False,
    )
```

```python
import functools
import math

import jax
import jax.numpy as jnp
from jax import lax
from jax.experimental import pallas as pl
from jax.experimental.pallas import tpu as pltpu
from jax.sharding import PartitionSpec as P

HEAD = 128
HALVES, TURNS, PAIR, CORES = 2, 4, 2, 2
CTX = HALVES * TURNS * PAIR * CORES
ROWS_X, ROWS_Y = 2, 4
NEG = -1e30
WIRE = jnp.bfloat16
F32 = jnp.float32
VMEM = pl.BlockSpec(memory_space=pltpu.VMEM)
ANY = pl.BlockSpec(memory_space=pl.ANY)
HBM = pl.BlockSpec(memory_space=pltpu.HBM)


def room(mib):
    return pltpu.CompilerParams(vmem_limit_bytes=mib * 1024 * 1024)


def place(half, turn, pair, core):
    return ((half * TURNS + turn % TURNS) * PAIR + pair) * CORES + core


def here():
    ctx = lax.axis_index("ctx")
    core, pair = ctx % CORES, ctx // CORES % PAIR
    return ctx // (CORES * PAIR * TURNS), ctx // (CORES * PAIR) % TURNS, pair, core


def moved(value, to):
    spots = [
        (h, t, p, k)
        for h in range(HALVES)
        for t in range(TURNS)
        for p in range(PAIR)
        for k in range(CORES)
    ]
    pairs = [(place(*s), place(*to(*s))) for s in spots if to(*s) is not None]
    return lax.ppermute(value, "ctx", pairs)


def other_chip(value):
    pairs = [(i, i + 1 if i % CORES else i - 1) for i in range(1, CTX - 1)]
    return lax.ppermute(value, "ctx", pairs)


def two_back(value):
    return lax.ppermute(value, "ctx", [(i, i - CORES) for i in range(CORES, CTX)])


def other_core(value):
    return moved(value, lambda h, t, p, k: (h, t, p, 1 - k))


def other_pair(value):
    return moved(value, lambda h, t, p, k: (h, t, 1 - p, k))


def across(value, source, cross):
    return moved(
        value,
        lambda h, t, p, k: (1 - h, t, 1 - p if cross else p, k) if h == source else None,
    )


def turned(value, way):
    return moved(value, lambda h, t, p, k: (h, t + way * (1 - 2 * k), p, k))


def turned_over(value):
    return moved(value, lambda h, t, p, k: (h, t - (1 - 2 * k), p, 1 - k))


def contract_last(left, right):
    return lax.dot_general(left, right, (((1,), (1,)), ((), ())), preferred_element_type=F32)


def contract_first(left, right):
    return lax.dot_general(left, right, (((0,), (0,)), ((), ())), preferred_element_type=F32)


def cut_kernel(q_ref, k_ref, v_ref, o_ref, start_ref, out_ref, half_ref, start_out, sems):
    _, turn, _, core = here()
    lane = pl.multiple_of((turn * CORES + core) * HEAD, HEAD)
    copies = [
        (w.at[:, pl.ds(lane, HEAD)], out_ref.at[:, i * HEAD : (i + 1) * HEAD])
        for i, w in enumerate((q_ref, k_ref, v_ref))
    ]
    half = half_ref.shape[0]
    copies.append((o_ref.at[pl.ds(pl.multiple_of(core * half, half), half), :], half_ref))
    copies.append((start_ref, start_out))
    fetched(copies, sems)


def cut_weights(w_query, w_key, w_value, w_out, starts):
    rows, width = w_out.shape
    return pl.pallas_call(
        cut_kernel,
        out_shape=(
            jax.ShapeDtypeStruct((rows, 3 * HEAD), w_query.dtype),
            jax.ShapeDtypeStruct((rows // CORES, width), w_out.dtype),
            jax.ShapeDtypeStruct(starts.shape, starts.dtype),
        ),
        in_specs=[HBM] * 4 + [ANY],
        out_specs=(VMEM, VMEM, VMEM),
        scratch_shapes=[pltpu.SemaphoreType.DMA((5,))],
        compiler_params=room(60),
    )(w_query, w_key, w_value, w_out, starts)


def other_x(value):
    count = ROWS_X * ROWS_Y
    return lax.ppermute(value, "dp", [(d, (d + ROWS_Y) % count) for d in range(count)])


def shifted_y(value, step):
    pairs = [(d, d // ROWS_Y * ROWS_Y + (d + step) % ROWS_Y) for d in range(ROWS_X * ROWS_Y)]
    return lax.ppermute(value, "dp", pairs)


def gathered_halves(half):
    return lax.all_gather(half, "dp", axis=0, tiled=False)


def pass_kernel(value_ref, *refs):
    refs[-1][...] = value_ref[...]


def passed_on(value, *ready):
    return pl.pallas_call(
        pass_kernel,
        out_shape=jax.ShapeDtypeStruct(value.shape, value.dtype),
        in_specs=[VMEM] + [ANY] * len(ready),
        out_specs=VMEM,
        compiler_params=room(4),
    )(value, *ready)


def gathered_rows(shard, first_ready, last_ready):
    near = turned(shard, 1)
    next_to = turned_over(passed_on(shard, near))
    far = passed_on(turned(passed_on(near, *first_ready), 1), *last_ready)
    return [
        shard,
        other_core(shard),
        near,
        next_to,
        other_core(near),
        other_core(next_to),
        far,
        other_core(far),
    ]


def rows_at(row, half, turn, pair, core, seg):
    slot = row // seg
    two = slot // 2
    way = 1 - 2 * core
    step = jnp.where(two == 0, 0, jnp.where(two == 1, way, jnp.where(two == 2, -way, 2)))
    flip = jnp.where(two == 2, 1 - slot % 2, slot % 2)
    its_core = jnp.where(flip == 1, 1 - core, core)
    its_turn = (turn - step + TURNS) % TURNS
    return place(half, its_turn, pair, its_core) * seg + row % seg


def fetched(copies, sems):
    started = []
    for i, (source, target) in enumerate(copies):
        started.append(pltpu.make_async_copy(source, target, sems.at[i]))
        started[-1].start()
    for copy in started:
        copy.wait()


def fill(out_ref, pieces):
    at = 0
    for piece in pieces:
        out_ref[at : at + piece.shape[0], :] = piece[...]
        at += piece.shape[0]


def window_kernel(own_ref, beside_ref, facing_ref, token_hbm, grad_hbm, *refs):
    core_ref, chip_ref, mid_token, mid_grad, first_ref = refs[:5]
    token_ref, grad_ref, sems = refs[5:]
    rows, width = token_ref.shape
    seg = mid_token.shape[0]
    token_copy = pltpu.make_async_copy(token_hbm, token_ref, sems.at[0])
    grad_copy = pltpu.make_async_copy(grad_hbm, grad_ref, sems.at[1])
    token_copy.start()
    grad_copy.start()
    ctx, core = lax.axis_index("ctx"), here()[3]
    at = lax.broadcasted_iota(jnp.int32, (rows, 1), 0) + ctx * rows
    before = jnp.where(core == 0, facing_ref[...], beside_ref[...])
    after = jnp.where(core == 0, beside_ref[...], facing_ref[...])
    before = jnp.where(ctx == 0, -1, before)
    after = jnp.where(ctx == CTX - 1, rows * CTX, after)
    begun = [(part <= at).astype(jnp.int32) for part in (before, own_ref[...], after)]
    slot = sum(jnp.sum(part, axis=1, keepdims=True) for part in begun) - 1
    slots = lax.broadcasted_iota(jnp.int32, (1, 3 * seg), 1)
    member = (slots == slot).astype(jnp.bfloat16)
    earlier = (slots == slot - 1).astype(jnp.bfloat16)
    token_copy.wait()
    token = contract_first(member, token_ref[...])
    grad_copy.wait()
    grad = contract_first(earlier, grad_ref[...])
    outside = jnp.broadcast_to((slot == 0).astype(jnp.bfloat16), (rows, HEAD))
    first_ref[...] = contract_first(outside, grad_ref[...])[:1]
    mid_token[...] = token[seg : 2 * seg]
    mid_grad[...] = grad[seg : 2 * seg]

    def send(lower_ref, upper_ref):
        lower_ref[:, :width] = token[:seg].astype(WIRE)
        lower_ref[:, width:] = grad[:seg].astype(WIRE)
        upper_ref[:, :width] = token[2 * seg :].astype(WIRE)
        upper_ref[:, width:] = grad[2 * seg :].astype(WIRE)

    @pl.when(core == 0)
    def _():
        send(chip_ref, core_ref)

    @pl.when(core == 1)
    def _():
        send(core_ref, chip_ref)


def window_sums(own, beside, facing, tokens, grads):
    rows, width = tokens.shape
    seg = own.shape[1]
    shape = jax.ShapeDtypeStruct
    return pl.pallas_call(
        window_kernel,
        out_shape=(
            shape((seg, 2 * width), WIRE),
            shape((seg, 2 * width), WIRE),
            shape((seg, width), F32),
            shape((seg, width), F32),
            shape((1, width), F32),
        ),
        in_specs=[VMEM] * 3 + [HBM] * 2,
        out_specs=(VMEM,) * 5,
        scratch_shapes=[
            pltpu.VMEM((rows, width), tokens.dtype),
            pltpu.VMEM((rows, width), grads.dtype),
            pltpu.SemaphoreType.DMA((2,)),
        ],
        compiler_params=room(16),
    )(own, beside, facing, tokens, grads)


def norm_kernel(core_ref, chip_ref, mid_token, mid_grad, count_ref, gain_ref, *refs):
    mine_ref, theirs_ref, normin_ref, normed_ref, rms_ref, dout_ref, pair_ref = refs
    width = mid_token.shape[1]
    rows = mine_ref.shape[0]
    pair_ref[:rows, :] = mine_ref[...]
    pair_ref[rows:, :] = theirs_ref[...]
    got = core_ref[...].astype(F32) + chip_ref[...].astype(F32)
    pooled = (mid_token[...] + got[:, :width]) / count_ref[...]
    rms = jnp.sqrt(jnp.mean(pooled * pooled, axis=1, keepdims=True) + 1e-06)
    normed = pooled / rms
    normed_ref[...] = normed
    rms_ref[...] = rms
    normin_ref[...] = (normed * gain_ref[...]).astype(jnp.bfloat16)
    dout_ref[...] = mid_grad[...] + got[:, width:]


def norm(from_core, from_chip, mid_token, mid_grad, count, gain, mine, theirs):
    seg, width = mid_token.shape
    shape = jax.ShapeDtypeStruct
    return pl.pallas_call(
        norm_kernel,
        out_shape=(
            shape((seg, width), jnp.bfloat16),
            shape((seg, width), F32),
            shape((seg, 1), F32),
            shape((seg, width), F32),
            shape((2 * mine.shape[0], mine.shape[1]), mine.dtype),
        ),
        in_specs=[VMEM] * 8,
        out_specs=(VMEM,) * 5,
        compiler_params=room(8),
    )(from_core, from_chip, mid_token, mid_grad, count, gain, mine, theirs)


def dout_kernel(dout_ref, second_ref, full_ref, half_ref):
    seg = dout_ref.shape[0]
    last = lax.broadcasted_iota(jnp.int32, (seg, 1), 0) == seg - 1
    dout = dout_ref[...] + jnp.where(last, second_ref[...], 0.0)
    full_ref[...] = dout
    half_ref[...] = dout.astype(jnp.bfloat16)


def whole_dout(dout, second):
    shape = jax.ShapeDtypeStruct
    return pl.pallas_call(
        dout_kernel,
        out_shape=(shape(dout.shape, F32), shape(dout.shape, jnp.bfloat16)),
        in_specs=[VMEM, VMEM],
        out_specs=(VMEM, VMEM),
        compiler_params=room(4),
    )(dout, second)


def dattended_kernel(own_ref, other_ref, weight, ready_ref, *refs):
    outs, rows = refs[:TURNS], refs[TURNS]
    fill(rows, [own_ref, other_ref])
    two = outs[0].shape[1]
    turn = here()[1]
    for step, ref in enumerate(outs):
        at = pl.multiple_of((turn + step) % TURNS * two, two)
        ref[...] = contract_last(rows[...], weight[pl.ds(at, two), :]).astype(jnp.bfloat16)


def dattended(own, other, halves, ready):
    heads, half, width = halves.shape
    rows = 2 * own.shape[0]
    return pl.pallas_call(
        dattended_kernel,
        out_shape=(jax.ShapeDtypeStruct((rows, CORES * half), jnp.bfloat16),) * TURNS,
        in_specs=[VMEM] * 3 + [ANY],
        out_specs=(VMEM,) * TURNS,
        scratch_shapes=[pltpu.VMEM((rows, width), jnp.bfloat16)],
        compiler_params=room(8),
    )(own, other, halves.reshape(heads * half, width), ready)


def project_kernel(*refs):
    pieces, weights = refs[:8], refs[8:12]
    q_ref, kv_ref, w_ref, rows = refs[12:]
    fill(rows, pieces)
    dp = lax.axis_index("dp")
    x, y = dp // ROWS_Y, dp % ROWS_Y
    depth = weights[0].shape[0] // ROWS_X
    for weight, step in zip(weights, (0, 1, -1, 2)):
        its_y = (y - step + ROWS_Y) % ROWS_Y
        for i in range(ROWS_X):
            its_x = x if i == 0 else 1 - x
            at = pl.multiple_of((its_x * ROWS_Y + its_y) * depth, depth)
            w_ref[pl.ds(at, depth), :] = weight[i * depth : (i + 1) * depth, :]
    out = jnp.dot(rows[...], w_ref[...], preferred_element_type=F32).astype(jnp.bfloat16)
    q_ref[...] = out[:, :HEAD]
    kv_ref[...] = out[:, HEAD:]


def project(pieces, weights):
    seg, width = pieces[0].shape
    rows = seg * len(pieces)
    bf16 = lambda *shape: jax.ShapeDtypeStruct(shape, jnp.bfloat16)
    return pl.pallas_call(
        project_kernel,
        out_shape=(bf16(rows, HEAD), bf16(rows, 2 * HEAD), bf16(width, 3 * HEAD)),
        in_specs=[VMEM] * 12,
        out_specs=(VMEM,) * 3,
        scratch_shapes=[pltpu.VMEM((rows, width), jnp.bfloat16)],
        compiler_params=room(12),
    )(*pieces, *weights)


def place_dattended(core, seg, here_refs, there_refs, out_ref):
    half = out_ref.shape[1] // CORES
    mine = slice(core * half, (core + 1) * half)
    other = slice((1 - core) * half, (2 - core) * half)
    slots = ((0, 1), (2, 3), (6, 7), (5, 4)) if core == 0 else ((0, 1), (5, 4), (6, 7), (2, 3))
    for refs in zip(here_refs, there_refs, slots):
        for i, slot in enumerate(refs[2]):
            rows = slice(slot * seg, (slot + 1) * seg)
            out_ref[rows, mine] = refs[0][i * seg : (i + 1) * seg, mine]
            out_ref[rows, other] = refs[1][(1 - i) * seg : (2 - i) * seg, mine]


def attention_kernel(tile, seg, *refs):
    q_ref, here_refs, there_refs, blocks = refs[0], refs[1:5], refs[5:9], refs[9:13]
    dq_ref, outs, (kv, da_ref, dkt, dvt) = refs[13], refs[14:18], refs[18:]
    half, turn, pair, core = here()
    queries = q_ref.shape[0]
    for which in range(CORES):

        @pl.when(core == which)
        def _(which=which):
            place_dattended(which, seg, here_refs, there_refs, da_ref)

    turn_up = math.log2(math.e) / math.sqrt(HEAD)
    scale = 1.0 / math.sqrt(HEAD)

    def run(used):
        keys = used * queries
        fill(kv, blocks[:used])
        near = 2 * queries
        spot = lax.broadcasted_iota(jnp.int32, (1, near), 1)
        key_pair = jnp.where(spot < queries, pair, 1 - pair)
        key_at = rows_at(spot % queries, half, turn, key_pair, core, seg)
        k = kv[:keys, :HEAD]
        v = kv[:keys, HEAD:]
        for step in range(queries // tile):
            rows = slice(step * tile, (step + 1) * tile)
            query = lax.broadcasted_iota(jnp.int32, (tile, 1), 0) + step * tile
            query_at = rows_at(query, half, turn, pair, core, seg)
            q = q_ref[rows, :]
            da = da_ref[rows, :]
            score = contract_last(q, k)
            masked = jnp.where(key_at <= query_at, score[:, :near], NEG)
            score = masked if used == 2 else jnp.concatenate([masked, score[:, near:]], axis=1)
            peak = jnp.max(score, axis=1, keepdims=True)
            expo = jnp.exp2((score - peak) * turn_up)
            probs = expo * (1.0 / jnp.sum(expo, axis=1, keepdims=True))
            probs_b = probs.astype(jnp.bfloat16)
            attended = jnp.dot(probs_b, v, preferred_element_type=F32).astype(jnp.bfloat16)
            delta = jnp.sum(da.astype(F32) * attended.astype(F32), axis=1, keepdims=True)
            dscore = (probs * (contract_last(da, v) - delta)).astype(jnp.bfloat16)
            dq = jnp.dot(dscore, k, preferred_element_type=F32) * scale
            dq_ref[rows, :] = dq.astype(jnp.bfloat16)
            dk_part = contract_first(q, dscore)
            dv_part = contract_first(da, probs_b)
            if step == 0:
                dkt[:, :keys] = dk_part
                dvt[:, :keys] = dv_part
            else:
                dkt[:, :keys] += dk_part
                dvt[:, :keys] += dv_part
        for i, out in enumerate(outs[:used]):
            lanes = slice(i * queries, (i + 1) * queries)
            out[:, :HEAD] = (dkt[:, lanes] * scale).T.astype(jnp.bfloat16)
            out[:, HEAD:] = dvt[:, lanes].T.astype(jnp.bfloat16)

    @pl.when(half == 0)
    def _():
        run(2)
        for out in outs[2:]:
            out[...] = jnp.zeros_like(out)

    @pl.when(half == 1)
    def _():
        run(4)


def attention(q, da_here, da_there, blocks, seg):
    queries = q.shape[0]
    keys = sum(block.shape[0] for block in blocks)
    parts = tuple(jax.ShapeDtypeStruct(block.shape, jnp.bfloat16) for block in blocks)
    return pl.pallas_call(
        functools.partial(attention_kernel, 256, seg),
        out_shape=(jax.ShapeDtypeStruct((queries, HEAD), jnp.bfloat16),) + parts,
        in_specs=[VMEM] * 13,
        out_specs=(VMEM,) * 5,
        scratch_shapes=[
            pltpu.VMEM((keys, 2 * HEAD), jnp.bfloat16),
            pltpu.VMEM((queries, HEAD), jnp.bfloat16),
            pltpu.VMEM((HEAD, keys), F32),
            pltpu.VMEM((HEAD, keys), F32),
        ],
        compiler_params=room(36),
        cost_estimate=pl.CostEstimate(
            flops=12 * queries * keys * HEAD,
            bytes_accessed=2 * HEAD * (3 * queries + 4 * keys),
            transcendentals=queries * keys,
        ),
    )(q, *da_here, *da_there, *blocks)


def unproject_kernel(seg, dq_ref, *refs):
    parts, w_ref, swap_ref, outs = refs[:4], refs[4], refs[5], refs[6:]
    dkv = sum(ref[...].astype(F32) for ref in parts).astype(jnp.bfloat16)
    left = jnp.concatenate([dq_ref[...], dkv], axis=1)
    out = contract_last(left, w_ref[...])
    for i, slot in enumerate((1, 4, 5, 7)):
        swap_ref[i * seg : (i + 1) * seg, :] = out[slot * seg : (slot + 1) * seg].astype(WIRE)
    for ref, slot in zip(outs, (0, 2, 3, 6)):
        ref[...] = out[slot * seg : (slot + 1) * seg]


def unproject(dq, parts, w_full, seg):
    width = w_full.shape[0]
    return pl.pallas_call(
        functools.partial(unproject_kernel, seg),
        out_shape=(jax.ShapeDtypeStruct((4 * seg, width), WIRE),)
        + (jax.ShapeDtypeStruct((seg, width), F32),) * 4,
        in_specs=[VMEM] * 6,
        out_specs=(VMEM,) * 5,
        compiler_params=room(16),
    )(dq, *parts, w_full)


def join_kernel(swapped, own, near, next_to, far, own_out, near_out, next_out, far_out):
    seg = own.shape[0]
    own_out[...] = own[...] + swapped[:seg, :].astype(F32)
    near_out[...] = near[...] + swapped[seg : 2 * seg, :].astype(F32)
    next_out[...] = (next_to[...] + swapped[2 * seg : 3 * seg, :].astype(F32)).astype(WIRE)
    far_out[...] = (far[...] + swapped[3 * seg :, :].astype(F32)).astype(WIRE)


def joined(swapped, own, near, next_to, far):
    wide = jax.ShapeDtypeStruct(own.shape, F32)
    thin = jax.ShapeDtypeStruct(own.shape, WIRE)
    return pl.pallas_call(
        join_kernel,
        out_shape=(wide, wide, thin, thin),
        in_specs=[VMEM] * 5,
        out_specs=(VMEM,) * 4,
        compiler_params=room(6),
    )(swapped, own, near, next_to, far)


def summed_rows(swap, own, near, next_to, far):
    own, near, next_to, far = joined(other_core(swap), own, near, next_to, far)
    far = turned(far, -1).astype(F32)
    next_to = turned_over(next_to).astype(F32)
    near = turned((near + far).astype(WIRE), -1).astype(F32)
    return own + next_to + near


def per_device(tokens, starts, gain, w_query, w_key, w_value, w_out, cotangent):
    token_rows = tokens[0]
    grad_out = cotangent[0]
    rows, width = token_rows.shape
    seg = starts.shape[1]
    length = rows * CTX
    ctx, core = lax.axis_index("ctx"), here()[3]

    mine, half, own_starts = cut_weights(w_query, w_key, w_value, w_out, starts)
    halves = gathered_halves(half)
    theirs = other_x(mine)
    beside, facing = other_core(own_starts), other_chip(own_starts)
    own_starts = starts
    to_core, to_chip, mid_token, mid_grad, first = window_sums(
        own_starts, beside, facing, token_rows, grad_out
    )
    before = jnp.where(core == 0, facing, beside)[0]
    after = jnp.where(core == 0, beside, facing)[0]
    before = jnp.where(ctx == 0, -1, before)
    after = jnp.where(ctx == CTX - 1, length, after)
    stop = jnp.full((1,), length, jnp.int32)
    window = jnp.concatenate([before, own_starts[0], after, stop])
    opens, ends = window[:-1], window[1:]
    count = (ends - opens)[seg : 2 * seg, None].astype(F32)
    second = two_back(first)
    normin, normed, rms, dout, both = norm(
        other_core(to_core),
        other_chip(to_chip),
        mid_token,
        mid_grad,
        count,
        gain[None],
        mine,
        theirs,
    )
    weights = [both, shifted_y(both, 1), shifted_y(both, -1), shifted_y(both, 2)]
    dout, dout_b = whole_dout(dout, second)
    dout_there = other_core(dout_b)
    pieces = gathered_rows(normin, [dout_there], weights[1:])
    q, own, w_full = project(pieces, weights)
    da = dattended(dout_b, dout_there, halves, w_full)
    far, beside = across(own, 0, False), other_pair(own)
    da_here = [da[0]] + [
        moved(da[i], lambda h, t, p, k, i=i: (h, t + i, p, k)) for i in range(1, TURNS)
    ]
    cross = across(passed_on(own, da_here[1], da_here[3]), 0, True)
    da_there = [other_core(piece) for piece in da_here]
    blocks = (own, beside, far, cross)
    dq, own, beside, far, cross = attention(q, da_here, da_there, blocks, seg)
    parts = (own, other_pair(beside), across(far, 1, False), across(cross, 1, True))
    dnormin = summed_rows(*unproject(dq, parts, w_full, seg))

    scaled = dnormin * gain
    dpooled = dout + (scaled - normed * jnp.mean(scaled * normed, axis=-1, keepdims=True)) / rms
    per_seg = (dpooled / count).astype(WIRE)
    beside, facing = other_core(per_seg), other_chip(per_seg)
    before = jnp.where(core == 0, facing, beside)
    after = jnp.where(core == 0, beside, facing)
    per_window = jnp.concatenate([before, per_seg, after], axis=0)
    positions = (ctx * rows + lax.iota(jnp.int32, rows))[:, None]
    member = (opens[None] <= positions) & (positions < ends[None])
    spread = jnp.dot(member.astype(WIRE), per_window, preferred_element_type=F32)
    return (grad_out.astype(F32) + spread).astype(jnp.bfloat16)[None]


def solution(mesh):
    return jax.shard_map(
        per_device,
        mesh=mesh,
        in_specs=(
            P("dp", "ctx", None),
            P("dp", "ctx"),
            P(),
            P("dp", None),
            P("dp", None),
            P("dp", None),
            P("dp", None),
            P("dp", "ctx", None),
        ),
        out_specs=P("dp", "ctx", None),
        check_vma=False,
    )
```

```python
import functools
import math

import jax
import jax.numpy as jnp
from jax import lax
from jax.experimental import pallas as pl
from jax.experimental.pallas import tpu as pltpu
from jax.sharding import PartitionSpec as P

HEAD = 128
HALVES, TURNS, PAIR, CORES = 2, 4, 2, 2
CTX = HALVES * TURNS * PAIR * CORES
ROWS_X, ROWS_Y = 2, 4
NEG = -1e30
WIRE = jnp.bfloat16
F32 = jnp.float32
VMEM = pl.BlockSpec(memory_space=pltpu.VMEM)
ANY = pl.BlockSpec(memory_space=pl.ANY)
HBM = pl.BlockSpec(memory_space=pltpu.HBM)


def room(mib):
    return pltpu.CompilerParams(vmem_limit_bytes=mib * 1024 * 1024)


def place(half, turn, pair, core):
    return ((half * TURNS + turn % TURNS) * PAIR + pair) * CORES + core


def here():
    ctx = lax.axis_index("ctx")
    core, pair = ctx % CORES, ctx // CORES % PAIR
    return ctx // (CORES * PAIR * TURNS), ctx // (CORES * PAIR) % TURNS, pair, core


def moved(value, to):
    spots = [
        (h, t, p, k)
        for h in range(HALVES)
        for t in range(TURNS)
        for p in range(PAIR)
        for k in range(CORES)
    ]
    pairs = [(place(*s), place(*to(*s))) for s in spots if to(*s) is not None]
    return lax.ppermute(value, "ctx", pairs)


def other_chip(value):
    pairs = [(i, i + 1 if i % CORES else i - 1) for i in range(1, CTX - 1)]
    return lax.ppermute(value, "ctx", pairs)


def two_back(value):
    return lax.ppermute(value, "ctx", [(i, i - CORES) for i in range(CORES, CTX)])


def other_core(value):
    return moved(value, lambda h, t, p, k: (h, t, p, 1 - k))


def other_pair(value):
    return moved(value, lambda h, t, p, k: (h, t, 1 - p, k))


def across(value, source, cross):
    return moved(
        value,
        lambda h, t, p, k: (1 - h, t, 1 - p if cross else p, k) if h == source else None,
    )


def turned(value, way):
    return moved(value, lambda h, t, p, k: (h, t + way * (1 - 2 * k), p, k))


def turned_over(value):
    return moved(value, lambda h, t, p, k: (h, t - (1 - 2 * k), p, 1 - k))


def contract_last(left, right):
    return lax.dot_general(left, right, (((1,), (1,)), ((), ())), preferred_element_type=F32)


def contract_first(left, right):
    return lax.dot_general(left, right, (((0,), (0,)), ((), ())), preferred_element_type=F32)


def cut_kernel(q_ref, k_ref, v_ref, o_ref, start_ref, out_ref, half_ref, start_out, sems):
    _, turn, _, core = here()
    lane = pl.multiple_of((turn * CORES + core) * HEAD, HEAD)
    copies = [
        (w.at[:, pl.ds(lane, HEAD)], out_ref.at[:, i * HEAD : (i + 1) * HEAD])
        for i, w in enumerate((q_ref, k_ref, v_ref))
    ]
    half = half_ref.shape[0]
    copies.append((o_ref.at[pl.ds(pl.multiple_of(core * half, half), half), :], half_ref))
    copies.append((start_ref, start_out))
    fetched(copies, sems)


def cut_weights(w_query, w_key, w_value, w_out, starts):
    rows, width = w_out.shape
    return pl.pallas_call(
        cut_kernel,
        out_shape=(
            jax.ShapeDtypeStruct((rows, 3 * HEAD), w_query.dtype),
            jax.ShapeDtypeStruct((rows // CORES, width), w_out.dtype),
            jax.ShapeDtypeStruct(starts.shape, starts.dtype),
        ),
        in_specs=[HBM] * 4 + [ANY],
        out_specs=(VMEM, VMEM, VMEM),
        scratch_shapes=[pltpu.SemaphoreType.DMA((5,))],
        compiler_params=room(60),
    )(w_query, w_key, w_value, w_out, starts)


def other_x(value):
    count = ROWS_X * ROWS_Y
    return lax.ppermute(value, "dp", [(d, (d + ROWS_Y) % count) for d in range(count)])


def shifted_y(value, step):
    pairs = [(d, d // ROWS_Y * ROWS_Y + (d + step) % ROWS_Y) for d in range(ROWS_X * ROWS_Y)]
    return lax.ppermute(value, "dp", pairs)


def gathered_halves(half):
    return lax.all_gather(half, "dp", axis=0, tiled=False)


def pass_kernel(value_ref, *refs):
    refs[-1][...] = value_ref[...]


def passed_on(value, *ready):
    return pl.pallas_call(
        pass_kernel,
        out_shape=jax.ShapeDtypeStruct(value.shape, value.dtype),
        in_specs=[VMEM] + [ANY] * len(ready),
        out_specs=VMEM,
        compiler_params=room(4),
    )(value, *ready)


def gathered_rows(shard, first_ready, last_ready):
    near = turned(shard, 1)
    next_to = turned_over(passed_on(shard, near))
    far = passed_on(turned(passed_on(near, *first_ready), 1), *last_ready)
    return [
        shard,
        other_core(shard),
        near,
        next_to,
        other_core(near),
        other_core(next_to),
        far,
        other_core(far),
    ]


def rows_at(row, half, turn, pair, core, seg):
    slot = row // seg
    two = slot // 2
    way = 1 - 2 * core
    step = jnp.where(two == 0, 0, jnp.where(two == 1, way, jnp.where(two == 2, -way, 2)))
    flip = jnp.where(two == 2, 1 - slot % 2, slot % 2)
    its_core = jnp.where(flip == 1, 1 - core, core)
    its_turn = (turn - step + TURNS) % TURNS
    return place(half, its_turn, pair, its_core) * seg + row % seg


def fetched(copies, sems):
    started = []
    for i, (source, target) in enumerate(copies):
        started.append(pltpu.make_async_copy(source, target, sems.at[i]))
        started[-1].start()
    for copy in started:
        copy.wait()


def fill(out_ref, pieces):
    at = 0
    for piece in pieces:
        out_ref[at : at + piece.shape[0], :] = piece[...]
        at += piece.shape[0]


def window_kernel(own_ref, beside_ref, facing_ref, token_hbm, grad_hbm, *refs):
    core_ref, chip_ref, mid_token, mid_grad, first_ref = refs[:5]
    token_ref, grad_ref, sems = refs[5:]
    rows, width = token_ref.shape
    seg = mid_token.shape[0]
    token_copy = pltpu.make_async_copy(token_hbm, token_ref, sems.at[0])
    grad_copy = pltpu.make_async_copy(grad_hbm, grad_ref, sems.at[1])
    token_copy.start()
    grad_copy.start()
    ctx, core = lax.axis_index("ctx"), here()[3]
    at = lax.broadcasted_iota(jnp.int32, (rows, 1), 0) + ctx * rows
    before = jnp.where(core == 0, facing_ref[...], beside_ref[...])
    after = jnp.where(core == 0, beside_ref[...], facing_ref[...])
    before = jnp.where(ctx == 0, -1, before)
    after = jnp.where(ctx == CTX - 1, rows * CTX, after)
    begun = [(part <= at).astype(jnp.int32) for part in (before, own_ref[...], after)]
    slot = sum(jnp.sum(part, axis=1, keepdims=True) for part in begun) - 1
    slots = lax.broadcasted_iota(jnp.int32, (1, 3 * seg), 1)
    member = (slots == slot).astype(jnp.bfloat16)
    earlier = (slots == slot - 1).astype(jnp.bfloat16)
    token_copy.wait()
    token = contract_first(member, token_ref[...])
    grad_copy.wait()
    grad = contract_first(earlier, grad_ref[...])
    outside = jnp.broadcast_to((slot == 0).astype(jnp.bfloat16), (rows, HEAD))
    first_ref[...] = contract_first(outside, grad_ref[...])[:1]
    mid_token[...] = token[seg : 2 * seg]
    mid_grad[...] = grad[seg : 2 * seg]

    def send(lower_ref, upper_ref):
        lower_ref[:, :width] = token[:seg].astype(WIRE)
        lower_ref[:, width:] = grad[:seg].astype(WIRE)
        upper_ref[:, :width] = token[2 * seg :].astype(WIRE)
        upper_ref[:, width:] = grad[2 * seg :].astype(WIRE)

    @pl.when(core == 0)
    def _():
        send(chip_ref, core_ref)

    @pl.when(core == 1)
    def _():
        send(core_ref, chip_ref)


def window_sums(own, beside, facing, tokens, grads):
    rows, width = tokens.shape
    seg = own.shape[1]
    shape = jax.ShapeDtypeStruct
    return pl.pallas_call(
        window_kernel,
        out_shape=(
            shape((seg, 2 * width), WIRE),
            shape((seg, 2 * width), WIRE),
            shape((seg, width), F32),
            shape((seg, width), F32),
            shape((1, width), F32),
        ),
        in_specs=[VMEM] * 3 + [HBM] * 2,
        out_specs=(VMEM,) * 5,
        scratch_shapes=[
            pltpu.VMEM((rows, width), tokens.dtype),
            pltpu.VMEM((rows, width), grads.dtype),
            pltpu.SemaphoreType.DMA((2,)),
        ],
        compiler_params=room(16),
    )(own, beside, facing, tokens, grads)


def norm_kernel(core_ref, chip_ref, mid_token, mid_grad, count_ref, gain_ref, *refs):
    mine_ref, theirs_ref, normin_ref, normed_ref, rms_ref, dout_ref, pair_ref = refs
    width = mid_token.shape[1]
    rows = mine_ref.shape[0]
    pair_ref[:rows, :] = mine_ref[...]
    pair_ref[rows:, :] = theirs_ref[...]
    got = core_ref[...].astype(F32) + chip_ref[...].astype(F32)
    pooled = (mid_token[...] + got[:, :width]) / count_ref[...]
    rms = jnp.sqrt(jnp.mean(pooled * pooled, axis=1, keepdims=True) + 1e-06)
    normed = pooled / rms
    normed_ref[...] = normed
    rms_ref[...] = rms
    normin_ref[...] = (normed * gain_ref[...]).astype(jnp.bfloat16)
    dout_ref[...] = mid_grad[...] + got[:, width:]


def norm(from_core, from_chip, mid_token, mid_grad, count, gain, mine, theirs):
    seg, width = mid_token.shape
    shape = jax.ShapeDtypeStruct
    return pl.pallas_call(
        norm_kernel,
        out_shape=(
            shape((seg, width), jnp.bfloat16),
            shape((seg, width), F32),
            shape((seg, 1), F32),
            shape((seg, width), F32),
            shape((2 * mine.shape[0], mine.shape[1]), mine.dtype),
        ),
        in_specs=[VMEM] * 8,
        out_specs=(VMEM,) * 5,
        compiler_params=room(8),
    )(from_core, from_chip, mid_token, mid_grad, count, gain, mine, theirs)


def dout_kernel(dout_ref, second_ref, full_ref, half_ref):
    seg = dout_ref.shape[0]
    last = lax.broadcasted_iota(jnp.int32, (seg, 1), 0) == seg - 1
    dout = dout_ref[...] + jnp.where(last, second_ref[...], 0.0)
    full_ref[...] = dout
    half_ref[...] = dout.astype(jnp.bfloat16)


def whole_dout(dout, second):
    shape = jax.ShapeDtypeStruct
    return pl.pallas_call(
        dout_kernel,
        out_shape=(shape(dout.shape, F32), shape(dout.shape, jnp.bfloat16)),
        in_specs=[VMEM, VMEM],
        out_specs=(VMEM, VMEM),
        compiler_params=room(4),
    )(dout, second)


def dattended_kernel(own_ref, other_ref, weight, ready_ref, *refs):
    outs, rows = refs[:TURNS], refs[TURNS]
    fill(rows, [own_ref, other_ref])
    two = outs[0].shape[1]
    turn = here()[1]
    for step, ref in enumerate(outs):
        at = pl.multiple_of((turn + step) % TURNS * two, two)
        ref[...] = contract_last(rows[...], weight[pl.ds(at, two), :]).astype(jnp.bfloat16)


def dattended(own, other, halves, ready):
    heads, half, width = halves.shape
    rows = 2 * own.shape[0]
    return pl.pallas_call(
        dattended_kernel,
        out_shape=(jax.ShapeDtypeStruct((rows, CORES * half), jnp.bfloat16),) * TURNS,
        in_specs=[VMEM] * 3 + [ANY],
        out_specs=(VMEM,) * TURNS,
        scratch_shapes=[pltpu.VMEM((rows, width), jnp.bfloat16)],
        compiler_params=room(8),
    )(own, other, halves.reshape(heads * half, width), ready)


def project_kernel(*refs):
    pieces, weights = refs[:8], refs[8:12]
    q_ref, kv_ref, w_ref, rows = refs[12:]
    fill(rows, pieces)
    dp = lax.axis_index("dp")
    x, y = dp // ROWS_Y, dp % ROWS_Y
    depth = weights[0].shape[0] // ROWS_X
    for weight, step in zip(weights, (0, 1, -1, 2)):
        its_y = (y - step + ROWS_Y) % ROWS_Y
        for i in range(ROWS_X):
            its_x = x if i == 0 else 1 - x
            at = pl.multiple_of((its_x * ROWS_Y + its_y) * depth, depth)
            w_ref[pl.ds(at, depth), :] = weight[i * depth : (i + 1) * depth, :]
    out = jnp.dot(rows[...], w_ref[...], preferred_element_type=F32).astype(jnp.bfloat16)
    q_ref[...] = out[:, :HEAD]
    kv_ref[...] = out[:, HEAD:]


def project(pieces, weights):
    seg, width = pieces[0].shape
    rows = seg * len(pieces)
    bf16 = lambda *shape: jax.ShapeDtypeStruct(shape, jnp.bfloat16)
    return pl.pallas_call(
        project_kernel,
        out_shape=(bf16(rows, HEAD), bf16(rows, 2 * HEAD), bf16(width, 3 * HEAD)),
        in_specs=[VMEM] * 12,
        out_specs=(VMEM,) * 3,
        scratch_shapes=[pltpu.VMEM((rows, width), jnp.bfloat16)],
        compiler_params=room(12),
    )(*pieces, *weights)


def place_dattended(core, seg, here_refs, there_refs, out_ref):
    half = out_ref.shape[1] // CORES
    mine = slice(core * half, (core + 1) * half)
    other = slice((1 - core) * half, (2 - core) * half)
    slots = ((0, 1), (2, 3), (6, 7), (5, 4)) if core == 0 else ((0, 1), (5, 4), (6, 7), (2, 3))
    for refs in zip(here_refs, there_refs, slots):
        for i, slot in enumerate(refs[2]):
            rows = slice(slot * seg, (slot + 1) * seg)
            out_ref[rows, mine] = refs[0][i * seg : (i + 1) * seg, mine]
            out_ref[rows, other] = refs[1][(1 - i) * seg : (2 - i) * seg, mine]


def attention_kernel(tile, seg, *refs):
    q_ref, here_refs, there_refs, blocks = refs[0], refs[1:5], refs[5:9], refs[9:13]
    dq_ref, outs, (kv, da_ref, dkt, dvt) = refs[13], refs[14:18], refs[18:]
    half, turn, pair, core = here()
    queries = q_ref.shape[0]
    for which in range(CORES):

        @pl.when(core == which)
        def _(which=which):
            place_dattended(which, seg, here_refs, there_refs, da_ref)

    turn_up = math.log2(math.e) / math.sqrt(HEAD)
    scale = 1.0 / math.sqrt(HEAD)

    def run(used):
        keys = used * queries
        fill(kv, blocks[:used])
        near = 2 * queries
        spot = lax.broadcasted_iota(jnp.int32, (1, near), 1)
        key_pair = jnp.where(spot < queries, pair, 1 - pair)
        key_at = rows_at(spot % queries, half, turn, key_pair, core, seg)
        k = kv[:keys, :HEAD]
        v = kv[:keys, HEAD:]
        for step in range(queries // tile):
            rows = slice(step * tile, (step + 1) * tile)
            query = lax.broadcasted_iota(jnp.int32, (tile, 1), 0) + step * tile
            query_at = rows_at(query, half, turn, pair, core, seg)
            q = q_ref[rows, :]
            da = da_ref[rows, :]
            score = contract_last(q, k)
            masked = jnp.where(key_at <= query_at, score[:, :near], NEG)
            score = masked if used == 2 else jnp.concatenate([masked, score[:, near:]], axis=1)
            peak = jnp.max(score, axis=1, keepdims=True)
            expo = jnp.exp2((score - peak) * turn_up)
            probs = expo * (1.0 / jnp.sum(expo, axis=1, keepdims=True))
            probs_b = probs.astype(jnp.bfloat16)
            attended = jnp.dot(probs_b, v, preferred_element_type=F32).astype(jnp.bfloat16)
            delta = jnp.sum(da.astype(F32) * attended.astype(F32), axis=1, keepdims=True)
            dscore = (probs * (contract_last(da, v) - delta)).astype(jnp.bfloat16)
            dq = jnp.dot(dscore, k, preferred_element_type=F32) * scale
            dq_ref[rows, :] = dq.astype(jnp.bfloat16)
            dk_part = contract_first(q, dscore)
            dv_part = contract_first(da, probs_b)
            if step == 0:
                dkt[:, :keys] = dk_part
                dvt[:, :keys] = dv_part
            else:
                dkt[:, :keys] += dk_part
                dvt[:, :keys] += dv_part
        for i, out in enumerate(outs[:used]):
            lanes = slice(i * queries, (i + 1) * queries)
            out[:, :HEAD] = (dkt[:, lanes] * scale).T.astype(jnp.bfloat16)
            out[:, HEAD:] = dvt[:, lanes].T.astype(jnp.bfloat16)

    @pl.when(half == 0)
    def _():
        run(2)
        for out in outs[2:]:
            out[...] = jnp.zeros_like(out)

    @pl.when(half == 1)
    def _():
        run(4)


def attention(q, da_here, da_there, blocks, seg):
    queries = q.shape[0]
    keys = sum(block.shape[0] for block in blocks)
    parts = tuple(jax.ShapeDtypeStruct(block.shape, jnp.bfloat16) for block in blocks)
    return pl.pallas_call(
        functools.partial(attention_kernel, 512, seg),
        out_shape=(jax.ShapeDtypeStruct((queries, HEAD), jnp.bfloat16),) + parts,
        in_specs=[VMEM] * 13,
        out_specs=(VMEM,) * 5,
        scratch_shapes=[
            pltpu.VMEM((keys, 2 * HEAD), jnp.bfloat16),
            pltpu.VMEM((queries, HEAD), jnp.bfloat16),
            pltpu.VMEM((HEAD, keys), F32),
            pltpu.VMEM((HEAD, keys), F32),
        ],
        compiler_params=room(48),
        cost_estimate=pl.CostEstimate(
            flops=12 * queries * keys * HEAD,
            bytes_accessed=2 * HEAD * (3 * queries + 4 * keys),
            transcendentals=queries * keys,
        ),
    )(q, *da_here, *da_there, *blocks)


def unproject_kernel(seg, dq_ref, *refs):
    parts, w_ref, swap_ref, outs = refs[:4], refs[4], refs[5], refs[6:]
    dkv = sum(ref[...].astype(F32) for ref in parts).astype(jnp.bfloat16)
    left = jnp.concatenate([dq_ref[...], dkv], axis=1)
    out = contract_last(left, w_ref[...])
    for i, slot in enumerate((1, 4, 5, 7)):
        swap_ref[i * seg : (i + 1) * seg, :] = out[slot * seg : (slot + 1) * seg].astype(WIRE)
    for ref, slot in zip(outs, (0, 2, 3, 6)):
        ref[...] = out[slot * seg : (slot + 1) * seg]


def unproject(dq, parts, w_full, seg):
    width = w_full.shape[0]
    return pl.pallas_call(
        functools.partial(unproject_kernel, seg),
        out_shape=(jax.ShapeDtypeStruct((4 * seg, width), WIRE),)
        + (jax.ShapeDtypeStruct((seg, width), F32),) * 4,
        in_specs=[VMEM] * 6,
        out_specs=(VMEM,) * 5,
        compiler_params=room(16),
    )(dq, *parts, w_full)


def join_kernel(swapped, own, near, next_to, far, own_out, near_out, next_out, far_out):
    seg = own.shape[0]
    own_out[...] = own[...] + swapped[:seg, :].astype(F32)
    near_out[...] = near[...] + swapped[seg : 2 * seg, :].astype(F32)
    next_out[...] = (next_to[...] + swapped[2 * seg : 3 * seg, :].astype(F32)).astype(WIRE)
    far_out[...] = (far[...] + swapped[3 * seg :, :].astype(F32)).astype(WIRE)


def joined(swapped, own, near, next_to, far):
    wide = jax.ShapeDtypeStruct(own.shape, F32)
    thin = jax.ShapeDtypeStruct(own.shape, WIRE)
    return pl.pallas_call(
        join_kernel,
        out_shape=(wide, wide, thin, thin),
        in_specs=[VMEM] * 5,
        out_specs=(VMEM,) * 4,
        compiler_params=room(6),
    )(swapped, own, near, next_to, far)


def summed_rows(swap, own, near, next_to, far):
    own, near, next_to, far = joined(other_core(swap), own, near, next_to, far)
    far = turned(far, -1).astype(F32)
    next_to = turned_over(next_to).astype(F32)
    near = turned((near + far).astype(WIRE), -1).astype(F32)
    return own + next_to + near


def per_device(tokens, starts, gain, w_query, w_key, w_value, w_out, cotangent):
    token_rows = tokens[0]
    grad_out = cotangent[0]
    rows, width = token_rows.shape
    seg = starts.shape[1]
    length = rows * CTX
    ctx, core = lax.axis_index("ctx"), here()[3]

    mine, half, own_starts = cut_weights(w_query, w_key, w_value, w_out, starts)
    halves = gathered_halves(half)
    theirs = other_x(mine)
    beside, facing = other_core(own_starts), other_chip(own_starts)
    own_starts = starts
    to_core, to_chip, mid_token, mid_grad, first = window_sums(
        own_starts, beside, facing, token_rows, grad_out
    )
    before = jnp.where(core == 0, facing, beside)[0]
    after = jnp.where(core == 0, beside, facing)[0]
    before = jnp.where(ctx == 0, -1, before)
    after = jnp.where(ctx == CTX - 1, length, after)
    stop = jnp.full((1,), length, jnp.int32)
    window = jnp.concatenate([before, own_starts[0], after, stop])
    opens, ends = window[:-1], window[1:]
    count = (ends - opens)[seg : 2 * seg, None].astype(F32)
    second = two_back(first)
    normin, normed, rms, dout, both = norm(
        other_core(to_core),
        other_chip(to_chip),
        mid_token,
        mid_grad,
        count,
        gain[None],
        mine,
        theirs,
    )
    weights = [both, shifted_y(both, 1), shifted_y(both, -1), shifted_y(both, 2)]
    dout, dout_b = whole_dout(dout, second)
    dout_there = other_core(dout_b)
    pieces = gathered_rows(normin, [dout_there], weights[1:])
    q, own, w_full = project(pieces, weights)
    da = dattended(dout_b, dout_there, halves, w_full)
    far, beside = across(own, 0, False), other_pair(own)
    da_here = [da[0]] + [
        moved(da[i], lambda h, t, p, k, i=i: (h, t + i, p, k)) for i in range(1, TURNS)
    ]
    cross = across(passed_on(own, *da_here[1:]), 0, True)
    da_there = [other_core(piece) for piece in da_here]
    blocks = (own, beside, far, cross)
    dq, own, beside, far, cross = attention(q, da_here, da_there, blocks, seg)
    parts = (own, other_pair(beside), across(far, 1, False), across(cross, 1, True))
    dnormin = summed_rows(*unproject(dq, parts, w_full, seg))

    scaled = dnormin * gain
    dpooled = dout + (scaled - normed * jnp.mean(scaled * normed, axis=-1, keepdims=True)) / rms
    per_seg = (dpooled / count).astype(WIRE)
    beside, facing = other_core(per_seg), other_chip(per_seg)
    before = jnp.where(core == 0, facing, beside)
    after = jnp.where(core == 0, beside, facing)
    per_window = jnp.concatenate([before, per_seg, after], axis=0)
    positions = (ctx * rows + lax.iota(jnp.int32, rows))[:, None]
    member = (opens[None] <= positions) & (positions < ends[None])
    spread = jnp.dot(member.astype(WIRE), per_window, preferred_element_type=F32)
    return (grad_out.astype(F32) + spread).astype(jnp.bfloat16)[None]


def solution(mesh):
    return jax.shard_map(
        per_device,
        mesh=mesh,
        in_specs=(
            P("dp", "ctx", None),
            P("dp", "ctx"),
            P(),
            P("dp", None),
            P("dp", None),
            P("dp", None),
            P("dp", None),
            P("dp", "ctx", None),
        ),
        out_specs=P("dp", "ctx", None),
        check_vma=False,
    )
```
